256 devices in a mesh: lon: 32 (over y_lo, z, core), lat: 8 (over x, y_hi).
Axes of the slice: x: 4, y: 4 (y_hi: 2, y_lo: 2; y = y_hi * 2 + y_lo), z: 8, core: 2. Of those that a mesh axis runs over, the one named last changes fastest.
Arguments:
- heat_content: float32 [16, 1024, 4096], P(None, 'lat', 'lon'), may hold values from -18 to 18
- eastern_current: float32 [16, 1024, 4096], P(None, 'lat', 'lon'), may hold values from -12 to 12
- northern_current: float32 [16, 1024, 4096], P(None, 'lat', 'lon'), may hold values from -12 to 12
- mixing_coefficient: float32 [16, 1024, 4096], P(None, 'lat', 'lon'), may hold values from 0.1 to 1
- friction_coefficient: float32 [1024, 4096], P('lat', 'lon'), may hold values from 0.05 to 0.5
- water_indicator: int32 [1024, 4096], P('lat', 'lon'), may hold values from 0 to 1
- flooded_strata: int32 [1024, 4096], P('lat', 'lon'), may hold values from 12 to 16
Outputs:
- temp_next: float32 [16, 1024, 4096], P(None, 'lat', 'lon')
- u_next: float32 [16, 1024, 4096], P(None, 'lat', 'lon')
- v_next: float32 [16, 1024, 4096], P(None, 'lat', 'lon')
The draws below stay inside these ranges and needn't reach their ends.
All inputs are finite; a program needn't handle non-finite values.
Results may differ from the reference program's by a relative error of at most 0.0003.
Values sent between devices are 32-bit elements; how exact they have to be, the bound alone decides.
A program may use at most 128 MiB of HBM per device.

```python
import math
import jax
import jax.numpy as jnp

STRATA_NUMBER = 16
CLAT = 128
CLON = 128
PARALLEL_NUMBER = 1024
MERIDIAN_NUMBER = 4096


def draw_water_indicator(key, part):
    tile_key, cell_key = jax.random.split(jax.random.fold_in(key, 7))
    tile_rows = PARALLEL_NUMBER // (CLAT // 2)
    tile_cols = MERIDIAN_NUMBER // (CLON // 2)
    tile_land = jax.random.randint(tile_key, (tile_rows, tile_cols), 0, 2)
    tile_full = jnp.repeat(jnp.repeat(tile_land, CLAT // 2, axis=0), CLON // 2, axis=1)
    cell_draw = jax.random.randint(cell_key, (PARALLEL_NUMBER, MERIDIAN_NUMBER), 0, 10)
    return (tile_full * (cell_draw > 0)).astype(jnp.int32)


def with_ends(drawn, key, smallest, high):
    longest = drawn.shape.index(max(drawn.shape))
    spots = []
    for shift in (0, 1):
        where = [jax.random.randint(jax.random.fold_in(key, axis), (), 0, length) for axis, length in enumerate(drawn.shape)]
        where[longest] = (where[longest] + shift) % drawn.shape[longest]
        spots.append(tuple(where))
    return drawn.at[spots[0]].set(smallest).at[spots[1]].set(high)


def level_of(rng, extent, pieces, low, high):
    def one(dim, blocks):
        steps = jax.random.uniform(jax.random.fold_in(jax.random.fold_in(rng, 6), dim), (blocks,), jnp.float32, low / len(pieces), high / len(pieces))
        return jnp.repeat(jnp.exp(steps), extent[dim] // blocks).reshape((-1,) + (1,) * (len(extent) - dim - 1))

    level = one(*pieces[0])
    for cut in pieces[1:]:
        level = level * one(*cut)
    return level


def gaussian(rng, shape, width, most, pieces=(), kind=jnp.bfloat16):
    gain = level_of(rng, shape, pieces, -0.22, 0.18) if pieces else 1.0
    entries = jax.random.normal(rng, shape, jnp.float32) * width * gain
    return jnp.minimum(jnp.maximum(entries, -most), most).astype(kind)


def setup_inputs(seed: int = 0) -> dict:
    splits = jax.random.split(jax.random.key(seed), 8)
    return {
        "heat_content": gaussian(splits[0], (STRATA_NUMBER, PARALLEL_NUMBER, MERIDIAN_NUMBER), 3.0, 18.0, ((1, 8), (2, 32)), jnp.float32),
        "eastern_current": gaussian(splits[1], (STRATA_NUMBER, PARALLEL_NUMBER, MERIDIAN_NUMBER), 2.0, 12.0, ((1, 8), (2, 32)), jnp.float32),
        "northern_current": gaussian(splits[2], (STRATA_NUMBER, PARALLEL_NUMBER, MERIDIAN_NUMBER), 2.0, 12.0, ((1, 8), (2, 32)), jnp.float32),
        "mixing_coefficient": jnp.clip(jnp.exp(math.log(1.0) - 2.3025851 * jax.random.uniform(splits[3], (STRATA_NUMBER, PARALLEL_NUMBER, MERIDIAN_NUMBER), jnp.float32) ** level_of(splits[3], (STRATA_NUMBER, PARALLEL_NUMBER, MERIDIAN_NUMBER), ((1, 8), (2, 32)), -0.2, 0.2)), 0.1, 1.0),
        "friction_coefficient": jnp.clip(jnp.exp(math.log(0.5) - 2.3025851 * jax.random.uniform(splits[4], (PARALLEL_NUMBER, MERIDIAN_NUMBER), jnp.float32) ** level_of(splits[4], (PARALLEL_NUMBER, MERIDIAN_NUMBER), ((0, 8), (1, 32)), -0.2, 0.2)), 0.05, 0.5),
        "water_indicator": draw_water_indicator(jax.random.fold_in(splits[7], 71), 0),
        "flooded_strata": with_ends(jax.random.randint(splits[6], (PARALLEL_NUMBER, MERIDIAN_NUMBER), STRATA_NUMBER - STRATA_NUMBER // 4, STRATA_NUMBER + 1), jax.random.fold_in(splits[6], 1), STRATA_NUMBER - STRATA_NUMBER // 4, STRATA_NUMBER).astype(jnp.int32),
    }


DT = 0.25
GRAV = 0.1


def wet_mask(stratum_plane, stratum_number):
    level_index = jnp.arange(stratum_number, dtype=jnp.float32)[:, None, None]
    return (level_index < stratum_plane[None]).astype(jnp.float32)


def neighbours(field):
    return (field[:, 1:-1, 1:-1], field[:, 1:-1, 2:], field[:, 1:-1, :-2], field[:, 2:, 1:-1], field[:, :-2, 1:-1])


def tracer_step(tracer, u_field, v_field, diffus, wetness):
    t_mid, t_east, t_west, t_north, t_south = neighbours(tracer)
    u_mid, u_east, u_west, u_north, u_south = neighbours(u_field)
    v_mid, v_east, v_west, v_north, v_south = neighbours(v_field)
    k_mid, k_east, k_west, k_north, k_south = neighbours(diffus)
    w_mid, w_east, w_west, w_north, w_south = neighbours(wetness)
    flux_east = w_mid * w_east * (0.25 * (u_mid + u_east) * (t_mid + t_east) - 0.5 * (k_mid + k_east) * (t_east - t_mid))
    flux_west = w_mid * w_west * (0.25 * (u_west + u_mid) * (t_west + t_mid) - 0.5 * (k_west + k_mid) * (t_mid - t_west))
    flux_north = w_mid * w_north * (0.25 * (v_mid + v_north) * (t_mid + t_north) - 0.5 * (k_mid + k_north) * (t_north - t_mid))
    flux_south = w_mid * w_south * (0.25 * (v_south + v_mid) * (t_south + t_mid) - 0.5 * (k_south + k_mid) * (t_mid - t_south))
    flux_up = w_mid[1:] * w_mid[:-1] * 0.5 * (k_mid[1:] + k_mid[:-1]) * (t_mid[1:] - t_mid[:-1])
    zero_level = jnp.zeros_like(t_mid[:1])
    vertical = jnp.concatenate([flux_up, zero_level], 0) - jnp.concatenate([zero_level, flux_up], 0)
    return w_mid * (t_mid + DT * (flux_west - flux_east + flux_south - flux_north + vertical))


def laplace(field, wetness):
    f_mid, f_east, f_west, f_north, f_south = neighbours(field)
    w_mid, w_east, w_west, w_north, w_south = neighbours(wetness)
    return w_mid * (w_east * (f_east - f_mid) + w_west * (f_west - f_mid) + w_north * (f_north - f_mid) + w_south * (f_south - f_mid))


def momentum_step(u_field, v_field, pressure, wetness, friction_coefficient, coriolis):
    p_mid, p_east, p_west, p_north, p_south = neighbours(pressure)
    w_mid = wetness[:, 1:-1, 1:-1]
    u_mid = u_field[:, 1:-1, 1:-1]
    v_mid = v_field[:, 1:-1, 1:-1]
    u_new = w_mid * (u_mid + DT * (coriolis * v_mid - GRAV * 0.5 * (p_east - p_west) + friction_coefficient * laplace(u_field, wetness)))
    v_new = w_mid * (v_mid + DT * (-coriolis * u_mid - GRAV * 0.5 * (p_north - p_south) + friction_coefficient * laplace(v_field, wetness)))
    return u_new, v_new


def border_entire_mesh(field, sign_value):
    lon_wide = jnp.concatenate([field[..., -1:], field, field[..., :1]], -1)
    north_rows = lon_wide[:, -1:, ::-1] * sign_value
    south_rows = jnp.zeros_like(north_rows)
    return jnp.concatenate([south_rows, lon_wide, north_rows], 1)


def reference(heat_content, eastern_current, northern_current, mixing_coefficient, friction_coefficient, water_indicator, flooded_strata):
    stratum_plane = (water_indicator * flooded_strata).astype(jnp.float32)[None]
    depth_wide = border_entire_mesh(stratum_plane, 1.0)
    wetness = wet_mask(depth_wide[0], STRATA_NUMBER)
    scalar_bordered = border_entire_mesh(heat_content, 1.0)
    u_wide = border_entire_mesh(eastern_current, -1.0)
    v_wide = border_entire_mesh(northern_current, -1.0)
    k_wide = border_entire_mesh(mixing_coefficient, 1.0)
    temp_next = tracer_step(scalar_bordered, u_wide, v_wide, k_wide, wetness)
    pressure = jnp.cumsum(temp_next, axis=0)
    p_wide = border_entire_mesh(pressure, 1.0)
    row_index = jnp.arange(PARALLEL_NUMBER, dtype=jnp.float32)
    coriolis = jnp.sin(jnp.pi * ((row_index + 0.5) / PARALLEL_NUMBER - 0.5))[:, None]
    u_next, v_next = momentum_step(u_wide, v_wide, p_wide, wetness, friction_coefficient, coriolis)
    return temp_next, u_next, v_next
```

```python
import functools
import math

import jax
import jax.numpy as jnp
from jax import lax
from jax.experimental import pallas as pl
from jax.experimental.pallas import tpu as pltpu
from jax.sharding import PartitionSpec as P

MESH = pl.DeviceIdType.MESH
NK = 16
N = 128
FLAT = NK * N
PAD = N + 8
SCALE = 1.0 / 16.0
PG = 0.25 * 0.05
WEST, EAST, SOUTH, NORTH = 0, 1, 2, 3
MSG = 4 * NK + 8


def east_of(x):
    return pltpu.roll(x, N - 1, 1)


def west_of(x):
    return pltpu.roll(x, 1, 1)


def face(c, d, a, b, ta, tb, ka, kb):
    return jnp.where(c < d, (a + b) * (ta + tb) - (ka + kb) * (tb - ta), 0.0)


def mirrored(x):
    lane = lax.broadcasted_iota(jnp.int32, x.shape, 1)
    for bit in (1, 2, 4, 8, 16, 32, 64):
        x = jnp.where((lane & bit) == 0, pltpu.roll(x, N - bit, 1), pltpu.roll(x, bit, 1))
    return x


def running_sum(x):
    level = lax.broadcasted_iota(jnp.int32, x.shape, 0)
    for step in (1, 2, 4, 8):
        x = x + jnp.where(level >= step, pltpu.roll(x, step, 0), 0.0)
    return x


def kernel(
    n_lon, n_lat,
    t_hbm, u_hbm, v_hbm, k_hbm, fr_hbm, ind_hbm, str_hbm,
    tn, un, vn,
    t, u, v, kd, p, fa, fb, fr, ind, strata, dep, dep_e, dep_n, cor,
    tiles, fix, send, recv, psend, precv,
    in_sem, send_sem, recv_sem, psend_sem, precv_sem,
):
    lon, lat = lax.axis_index("lon"), lax.axis_index("lat")
    is_top, is_bottom = lat == n_lat - 1, lat == 0
    east = (lat, lax.rem(lon + 1, n_lon))
    west = (lat, lax.rem(lon + n_lon - 1, n_lon))
    north = (jnp.where(is_top, lat, lat + 1), jnp.where(is_top, n_lon - 1 - lon, lon))
    south = (jnp.where(is_bottom, lat, lat - 1), lon)

    def at(place):
        return {"lat": place[0], "lon": place[1]}

    loads = [
        pltpu.make_async_copy(src, dst, in_sem.at[i])
        for i, (src, dst) in enumerate(
            (
                (ind_hbm, ind), (str_hbm, strata), (fr_hbm, fr),
                (t_hbm, t.at[pl.ds(0, FLAT)]), (u_hbm, u.at[pl.ds(0, FLAT)]),
                (k_hbm, kd.at[pl.ds(0, FLAT)]), (v_hbm, v.at[pl.ds(0, FLAT)]),
            )
        )
    ]
    for load in loads:
        load.start()
    barrier = pltpu.get_barrier_semaphore()
    for place in (west, east, north):
        pl.semaphore_signal(barrier, inc=1, device_id=at(place), device_id_type=MESH)

    @pl.when(jnp.logical_not(is_bottom))
    def _():
        pl.semaphore_signal(barrier, inc=1, device_id=at(south), device_id_type=MESH)

    lane8 = lax.broadcasted_iota(jnp.int32, (8, N), 1)
    group = lane8 >> 2
    zero8 = jnp.zeros((8, N), jnp.float32)
    lane = lax.broadcasted_iota(jnp.int32, (NK, N), 1)
    level = lax.broadcasted_iota(jnp.int32, (NK, N), 0).astype(jnp.float32)
    first, last = lane == 0, lane == N - 1

    for k in range(NK + 1):
        p[pl.ds(k * PAD, 8), :] = zero8
        fa[pl.ds(k * PAD, 8), :] = zero8
        fb[pl.ds(k * PAD, 8), :] = zero8

    @pl.when(is_bottom)
    def _():
        recv[SOUTH] = jnp.zeros((MSG, N), jnp.float32)
        precv[SOUTH] = jnp.zeros((NK, N), jnp.float32)

    def set_cor(b, _):
        rows = pl.ds(pl.multiple_of(b * 8, 8), 8)
        j = lax.broadcasted_iota(jnp.int32, (8, N), 0) + (b * 8 + lat * N)
        cor[rows, :] = 0.25 * jnp.sin(
            jnp.pi * ((j.astype(jnp.float32) + 0.5) / (N * n_lat) - 0.5)
        )
        return 0

    lax.fori_loop(0, N // 8, set_cor, 0)

    for load in loads[:3]:
        load.wait()
    dep[pl.ds(N, 8), :] = zero8
    dep[pl.ds(0, N), :] = (ind[...] * strata[...]).astype(jnp.float32)
    fr[...] = fr[...] * 0.25

    def set_depth(b, _):
        r = pl.multiple_of(b * 8, 8)
        rows = pl.ds(r, 8)
        d = dep[rows, :]
        dep_e[rows, :] = jnp.where(lane8 == N - 1, 0.0, jnp.minimum(d, east_of(d)))
        dep_n[rows, :] = jnp.minimum(d, dep[pl.ds(r + 1, 8), :])
        x = pltpu.roll(d, 2, 1)
        y = pltpu.roll(fr[rows, :], 6, 1)
        tiles[2, rows, :] = jnp.where(group == 0, x, jnp.where(group == 1, y, 0.0))
        return 0

    lax.fori_loop(0, N // 8, set_depth, 0)

    def pack(f, tile, a, b, double):
        def step(i, _):
            r = pl.multiple_of(i * 8, 8)
            parts = []
            for q in range(2 * NK):
                ref = a if q < NK else b
                rows = pl.ds(r + (q % NK) * N, 8)
                x = ref[rows, :]
                if double and q < NK:
                    x = x + x
                    ref[rows, :] = x
                y = pltpu.roll(x, (2 + 4 * q) % N, 1)
                parts.append(y if q % 4 == 0 else jnp.where(group == q, y, parts.pop()))
            acc = parts[0]
            for g in range(1, 8):
                acc = jnp.where(group >= 4 * g, parts[g], acc)
            tiles[tile, pl.ds(r, 8), :] = acc
            return 0

        lax.fori_loop(0, N // 8, step, 0)
        tiles[tile] = tiles[tile].T

    tiles[2] = tiles[2].T
    loads[3].wait()
    loads[4].wait()
    pack(0, 0, t, u, False)
    loads[5].wait()
    loads[6].wait()
    pack(1, 1, kd, v, True)

    def column(tile, half, entry):
        return tiles[tile, pl.ds(64 * half + entry, NK, stride=4), :]

    def columns(entry):
        return (
            column(0, 0, entry), column(0, 1, entry), column(1, 1, entry), column(1, 0, entry),
            jnp.broadcast_to(tiles[2, pl.ds(entry, 1), :], (NK, N)),
        )

    def row(ref, j):
        return ref[pl.ds(j, NK, stride=N), :]

    def edge_rows(j):
        return (
            row(t, j), row(u, j), row(v, j), row(kd, j),
            jnp.broadcast_to(dep[pl.ds(j, 1), :], (NK, N)),
        )

    def stage(side, values):
        for f in range(4):
            send[side, pl.ds(f * NK, NK), :] = values[f]
        send[side, pl.ds(4 * NK, 8), :] = values[4][:8]

    stage(EAST, columns(1))
    stage(WEST, columns(2))
    stage(NORTH, edge_rows(N - 1))
    stage(SOUTH, edge_rows(0))

    pl.semaphore_wait(barrier, jnp.where(is_bottom, 3, 4))
    north_slot = jnp.where(is_top, NORTH, SOUTH)

    def exchange(out, into, out_sem, into_sem):
        def copy(side, slot, place):
            return pltpu.make_async_remote_copy(
                src_ref=out.at[side], dst_ref=into.at[slot], send_sem=out_sem.at[side],
                recv_sem=into_sem.at[slot], device_id=at(place), device_id_type=MESH,
            )

        sends = [
            copy(EAST, WEST, east), copy(WEST, EAST, west), copy(NORTH, north_slot, north),
        ]
        down = copy(SOUTH, NORTH, south)

        def start():
            for s in sends:
                s.start()

            @pl.when(jnp.logical_not(is_bottom))
            def _():
                down.start()

        def wait_recv():
            copy(WEST, WEST, west).wait_recv()
            copy(EAST, EAST, east).wait_recv()
            copy(NORTH, NORTH, north).wait_recv()

            @pl.when(jnp.logical_not(is_bottom))
            def _():
                copy(SOUTH, SOUTH, south).wait_recv()

        def wait_send():
            for s in sends:
                s.wait_send()

            @pl.when(jnp.logical_not(is_bottom))
            def _():
                down.wait_send()

        return start, wait_recv, wait_send

    start1, arrive1, sent1 = exchange(send, recv, send_sem, recv_sem)
    start2, arrive2, sent2 = exchange(psend, precv, psend_sem, precv_sem)
    start1()

    def tracer(b, _):
        r = pl.multiple_of(b * 8, 8)
        rows = pl.ds(r, 8)
        d, de, dn = dep[rows, :], dep_e[rows, :], dep_n[rows, :]
        below = zero8
        for k in range(NK):
            c = float(k)
            here, up_rows = pl.ds(r + k * N, 8), pl.ds(r + k * N + 1, 8)
            tc, kc, uc, vc = t[here, :], kd[here, :], u[here, :], v[here, :]
            f_e = face(c, de, uc, east_of(uc), tc, east_of(tc), kc, east_of(kc))
            f_n = face(c, dn, vc, v[up_rows, :], tc, t[up_rows, :], kc, kd[up_rows, :])
            fa[pl.ds(r + k * PAD + 8, 8), :] = f_n
            f_s = fa[pl.ds(r + k * PAD + 7, 8), :]
            if k < NK - 1:
                t_up, k_up = t[pl.ds(r + (k + 1) * N, 8), :], kd[pl.ds(r + (k + 1) * N, 8), :]
                above = jnp.where(c + 1.0 < d, (kc + k_up) * (t_up - tc), 0.0)
            else:
                above = zero8
            total = (west_of(f_e) - f_e) + (f_s - f_n) + (above - below)
            below = above
            tn[here, :] = jnp.where(c < d, tc + SCALE * total, 0.0)
        return 0

    lax.fori_loop(0, N // 8, tracer, 0)

    arrive1()

    @pl.when(is_top)
    def _():
        x = mirrored(recv[NORTH])
        sign = lax.broadcasted_iota(jnp.int32, (MSG, N), 0)
        recv[NORTH] = jnp.where((sign >= NK) & (sign < 3 * NK), -x, x)

    def ghost(slot):
        parts = [recv[slot, pl.ds(f * NK, NK), :] for f in range(4)]
        d = recv[slot, pl.ds(4 * NK, 1), :]
        return (*parts, jnp.broadcast_to(d, (NK, N)))

    g_w, g_e, g_s, g_n = ghost(WEST), ghost(EAST), ghost(SOUTH), ghost(NORTH)

    def x_face(a, b):
        return face(level, jnp.minimum(a[4], b[4]), a[1], b[1], a[0], b[0], a[3], b[3])

    def y_face(a, b):
        return face(level, jnp.minimum(a[4], b[4]), a[2], b[2], a[0], b[0], a[3], b[3])

    def column_step(mid, left, right, north_corner, south_corner):
        up = tuple(jnp.where(last, c, east_of(m)) for m, c in zip(mid, north_corner))
        down = tuple(jnp.where(first, c, west_of(m)) for m, c in zip(mid, south_corner))
        tc, _, _, kc, d = mid
        above = jnp.where(
            level + 1.0 < d,
            (kc + pltpu.roll(kc, NK - 1, 0)) * (pltpu.roll(tc, NK - 1, 0) - tc),
            0.0,
        )
        below = pltpu.roll(above, 1, 0)
        total = (
            (x_face(left, mid) - x_face(mid, right))
            + (y_face(down, mid) - y_face(mid, up))
            + (above - below)
        )
        return jnp.where(level < d, tc + SCALE * total, 0.0)

    c_e, c_w = columns(1), columns(2)
    t_w = column_step(
        c_w, g_w, columns(3), tuple(east_of(x) for x in g_n), g_s
    )
    t_e = column_step(
        c_e, columns(0), g_e, g_n, tuple(west_of(x) for x in g_s)
    )
    r_s, r_n = edge_rows(0), edge_rows(N - 1)
    t_n = row(tn, N - 1) - SCALE * y_face(r_n, g_n)
    t_s = row(tn, 0) + SCALE * y_face(g_s, r_s)
    t_n = jnp.where(first, west_of(t_w), jnp.where(last, t_e, t_n))
    t_s = jnp.where(first, t_w, jnp.where(last, east_of(t_e), t_s))
    p_w, p_e = running_sum(PG * t_w), running_sum(PG * t_e)
    psend[EAST] = p_e
    psend[WEST] = p_w
    psend[NORTH] = running_sum(PG * t_n)
    psend[SOUTH] = running_sum(PG * t_s)
    start2()

    tn[pl.ds(N - 1, NK, stride=N), :] = t_n
    tn[pl.ds(0, NK, stride=N), :] = t_s
    fix[pl.ds(0, NK, stride=2), :] = t_e
    fix[pl.ds(1, NK, stride=2), :] = t_w
    for q in range(4, 16):
        fix[pl.ds(q * 8, 8), :] = zero8
    fix[...] = fix[...].T
    rim8 = (lane8 == 0) | (lane8 == N - 1)

    def pressure(b, _):
        r = pl.multiple_of(b * 8, 8)
        x = fix[pl.ds(r, 8), :]
        total = zero8
        for k in range(NK):
            here = pl.ds(r + k * N, 8)
            tc = jnp.where(rim8, pltpu.roll(x, N - 1 - 2 * k, 1), tn[here, :])
            tn[here, :] = tc
            total = total + PG * tc
            p[pl.ds(r + k * PAD + 8, 8), :] = total
        return 0

    lax.fori_loop(0, N // 8, pressure, 0)

    def momentum(b, _):
        r = pl.multiple_of(b * 8, 8)
        rows = pl.ds(r, 8)
        d, de, dn = dep[rows, :], dep_e[rows, :], dep_n[rows, :]
        f, co = fr[rows, :], cor[rows, :]
        for k in range(NK):
            c = float(k)
            here, up_rows = pl.ds(r + k * N, 8), pl.ds(r + k * N + 1, 8)
            mine, south_rows = pl.ds(r + k * PAD + 8, 8), pl.ds(r + k * PAD + 7, 8)
            uc, vc, pc = u[here, :], v[here, :], p[mine, :]
            wet_e, wet_n, wet = c < de, c < dn, c < d
            u_e = jnp.where(wet_e, east_of(uc) - uc, 0.0)
            v_e = jnp.where(wet_e, east_of(vc) - vc, 0.0)
            u_n = jnp.where(wet_n, u[up_rows, :] - uc, 0.0)
            v_n = jnp.where(wet_n, v[up_rows, :] - vc, 0.0)
            fa[mine, :] = u_n
            fb[mine, :] = v_n
            lap_u = (u_e - west_of(u_e)) + (u_n - fa[south_rows, :])
            lap_v = (v_e - west_of(v_e)) + (v_n - fb[south_rows, :])
            dp_x = east_of(pc) - west_of(pc)
            dp_y = p[pl.ds(r + k * PAD + 9, 8), :] - p[south_rows, :]
            un[here, :] = jnp.where(wet, (uc + co * vc) - dp_x + f * lap_u, 0.0)
            vn[here, :] = jnp.where(wet, (vc - co * uc) - dp_y + f * lap_v, 0.0)
        return 0

    lax.fori_loop(0, N // 8, momentum, 0)

    arrive2()

    @pl.when(is_top)
    def _():
        precv[NORTH] = mirrored(precv[NORTH])

    def friction(mid, other, f, i):
        m = level < jnp.minimum(mid[4], other[4])
        return jnp.where(m, f * (other[i] - mid[i]), 0.0)

    def masked(mid, x):
        return jnp.where(level < mid[4], x, 0.0)

    f_e = jnp.broadcast_to(tiles[2, pl.ds(5, 1), :], (NK, N))
    f_w = jnp.broadcast_to(tiles[2, pl.ds(6, 1), :], (NK, N))
    f_s = jnp.broadcast_to(fr[pl.ds(0, 1), :], (NK, N))
    f_n = jnp.broadcast_to(fr[pl.ds(N - 1, 1), :], (NK, N))
    up, down = pl.ds(N - 1, NK, stride=N), pl.ds(0, NK, stride=N)
    un[up, :] = un[up, :] + friction(r_n, g_n, f_n, 1)
    un[down, :] = un[down, :] + friction(r_s, g_s, f_s, 1)
    vn[up, :] = vn[up, :] + friction(r_n, g_n, f_n, 2) - masked(r_n, precv[NORTH])
    vn[down, :] = vn[down, :] + friction(r_s, g_s, f_s, 2) + masked(r_s, precv[SOUTH])
    fix[pl.ds(0, NK, stride=2), :] = friction(c_e, g_e, f_e, 1) - masked(c_e, precv[EAST] - p_w)
    fix[pl.ds(1, NK, stride=2), :] = friction(c_w, g_w, f_w, 1) + masked(c_w, precv[WEST] - p_e)
    fix[pl.ds(32, NK, stride=2), :] = friction(c_e, g_e, f_e, 2)
    fix[pl.ds(33, NK, stride=2), :] = friction(c_w, g_w, f_w, 2)
    fix[...] = fix[...].T

    def finish(b, _):
        r = pl.multiple_of(b * 8, 8)
        x = fix[pl.ds(r, 8), :]
        for k in range(NK):
            here = pl.ds(r + k * N, 8)
            un[here, :] = un[here, :] + jnp.where(rim8, pltpu.roll(x, N - 1 - 2 * k, 1), 0.0)
            vn[here, :] = vn[here, :] + jnp.where(rim8, pltpu.roll(x, N - 33 - 2 * k, 1), 0.0)
        return 0

    lax.fori_loop(0, N // 8, finish, 0)
    sent1()
    sent2()


def solution(mesh):
    n_lon, n_lat = mesh.shape["lon"], mesh.shape["lat"]
    f32, i32 = jnp.float32, jnp.int32

    def on_device(t, u, v, kd, fr, ind, strata):
        flat = [x.reshape(FLAT, N) for x in (t, u, v, kd)]
        outs = pl.pallas_call(
            functools.partial(kernel, n_lon, n_lat),
            out_shape=[pltpu.VMEM((FLAT, N), f32)] * 3,
            in_specs=[pl.BlockSpec(memory_space=pltpu.HBM)] * 7,
            out_specs=[pl.BlockSpec(memory_space=pltpu.VMEM)] * 3,
            scratch_shapes=[
                *[pltpu.VMEM((FLAT + 8, N), f32)] * 4,
                *[pltpu.VMEM((NK * PAD + 8, N), f32)] * 3,
                pltpu.VMEM((N, N), f32),
                pltpu.VMEM((N, N), i32),
                pltpu.VMEM((N, N), i32),
                pltpu.VMEM((N + 8, N), f32),
                *[pltpu.VMEM((N, N), f32)] * 3,
                pltpu.VMEM((3, N, N), f32),
                pltpu.VMEM((N, N), f32),
                pltpu.VMEM((4, MSG, N), f32),
                pltpu.VMEM((4, MSG, N), f32),
                pltpu.VMEM((4, NK, N), f32),
                pltpu.VMEM((4, NK, N), f32),
                pltpu.SemaphoreType.DMA((7,)),
                *[pltpu.SemaphoreType.DMA((4,))] * 4,
            ],
            compiler_params=pltpu.CompilerParams(
                collective_id=0, has_side_effects=True, vmem_limit_bytes=60 * 1024 * 1024
            ),
            cost_estimate=pl.CostEstimate(
                flops=80 * FLAT * N, bytes_accessed=30 * FLAT * N, transcendentals=0
            ),
        )(*flat, fr, ind, strata)
        return tuple(x.reshape(NK, N, N) for x in outs)

    plane, field = P("lat", "lon"), P(None, "lat", "lon")
    return jax.shard_map(
        on_device,
        mesh=mesh,
        in_specs=(field, field, field, field, plane, plane, plane),
        out_specs=(field, field, field),
        check_vma=False,
    )
```

```python
import functools
import math

import jax
import jax.numpy as jnp
from jax import lax
from jax.experimental import pallas as pl
from jax.experimental.pallas import tpu as pltpu
from jax.sharding import PartitionSpec as P

MESH = pl.DeviceIdType.MESH
NK = 16
N = 128
FLAT = NK * N
PAD = N + 8
SCALE = 1.0 / 16.0
PG = 0.25 * 0.05
WEST, EAST, SOUTH, NORTH = 0, 1, 2, 3
SW, SE, NW, NE = 0, 1, 2, 3
MSG = 5 * NK + 8


def east_of(x):
    return pltpu.roll(x, N - 1, 1)


def west_of(x):
    return pltpu.roll(x, 1, 1)


def face(c, d, a, b, ta, tb, ka, kb):
    return jnp.where(c < d, (a + b) * (ta + tb) - (ka + kb) * (tb - ta), 0.0)


def mirrored(x):
    lane = lax.broadcasted_iota(jnp.int32, x.shape, 1)
    for bit in (1, 2, 4, 8, 16, 32, 64):
        x = jnp.where((lane & bit) == 0, pltpu.roll(x, N - bit, 1), pltpu.roll(x, bit, 1))
    return x


def running_sum(x):
    level = lax.broadcasted_iota(jnp.int32, x.shape, 0)
    for step in (1, 2, 4, 8):
        x = x + jnp.where(level >= step, pltpu.roll(x, step, 0), 0.0)
    return x


def kernel(
    n_lon, n_lat,
    t_hbm, u_hbm, v_hbm, k_hbm, fr_hbm, ind_hbm, str_hbm,
    tn, un, vn,
    t, u, v, kd, p, fa, fb, fr, ind, strata, dep, dep_e, dep_n, cor,
    cols, fix, send, recv, csend, crecv,
    in_sem, send_sem, recv_sem, csend_sem, crecv_sem,
):
    lon, lat = lax.axis_index("lon"), lax.axis_index("lat")
    is_top, is_bottom = lat == n_lat - 1, lat == 0
    not_bottom = jnp.logical_not(is_bottom)
    lon_e, lon_w = lax.rem(lon + 1, n_lon), lax.rem(lon + n_lon - 1, n_lon)
    lat_n, lat_s = jnp.where(is_top, lat, lat + 1), jnp.where(is_bottom, lat, lat - 1)
    east, west = (lat, lon_e), (lat, lon_w)
    north, south = (lat_n, jnp.where(is_top, n_lon - 1 - lon, lon)), (lat_s, lon)
    fold_e, fold_w = lax.rem(2 * n_lon - 2 - lon, n_lon), lax.rem(n_lon - lon, n_lon)
    own_e = is_top & (fold_e == lon)
    own_w = is_top & (fold_w == lon)
    not_own_e, not_own_w = jnp.logical_not(own_e), jnp.logical_not(own_w)
    north_e = (lat_n, jnp.where(is_top, fold_e, lon_e))
    north_w = (lat_n, jnp.where(is_top, fold_w, lon_w))
    south_e, south_w = (lat_s, lon_e), (lat_s, lon_w)

    def at(place):
        return {"lat": place[0], "lon": place[1]}

    loads = [
        pltpu.make_async_copy(src, dst, in_sem.at[i])
        for i, (src, dst) in enumerate(
            (
                (ind_hbm, ind), (str_hbm, strata), (fr_hbm, fr),
                (t_hbm, t.at[pl.ds(0, FLAT)]), (u_hbm, u.at[pl.ds(0, FLAT)]),
                (k_hbm, kd.at[pl.ds(0, FLAT)]), (v_hbm, v.at[pl.ds(0, FLAT)]),
            )
        )
    ]
    for load in loads:
        load.start()
    barrier = pltpu.get_barrier_semaphore()

    def greet(place):
        pl.semaphore_signal(barrier, inc=1, device_id=at(place), device_id_type=MESH)

    for place in (west, east, north):
        greet(place)

    @pl.when(not_own_e)
    def _():
        greet(north_e)

    @pl.when(not_own_w)
    def _():
        greet(north_w)

    @pl.when(not_bottom)
    def _():
        for place in (south, south_e, south_w):
            greet(place)

    lane8 = lax.broadcasted_iota(jnp.int32, (8, N), 1)
    zero8 = jnp.zeros((8, N), jnp.float32)
    lane = lax.broadcasted_iota(jnp.int32, (NK, N), 1)
    level = lax.broadcasted_iota(jnp.int32, (NK, N), 0).astype(jnp.float32)
    first, last = lane == 0, lane == N - 1

    for k in range(NK + 1):
        p[pl.ds(k * PAD, 8), :] = zero8
        fa[pl.ds(k * PAD, 8), :] = zero8
        fb[pl.ds(k * PAD, 8), :] = zero8

    @pl.when(is_bottom)
    def _():
        recv[SOUTH] = jnp.zeros((MSG, N), jnp.float32)
        crecv[SW] = jnp.zeros((NK, N), jnp.float32)
        crecv[SE] = jnp.zeros((NK, N), jnp.float32)

    def set_cor(b, _):
        rows = pl.ds(pl.multiple_of(b * 8, 8), 8)
        j = lax.broadcasted_iota(jnp.int32, (8, N), 0) + (b * 8 + lat * N)
        cor[rows, :] = 0.25 * jnp.sin(
            jnp.pi * ((j.astype(jnp.float32) + 0.5) / (N * n_lat) - 0.5)
        )
        return 0

    lax.fori_loop(0, N // 8, set_cor, 0)

    for load in loads[:3]:
        load.wait()
    dep[pl.ds(N, 8), :] = zero8
    dep[pl.ds(0, N), :] = (ind[...] * strata[...]).astype(jnp.float32)
    fr[...] = fr[...] * 0.25

    def set_depth(b, _):
        r = pl.multiple_of(b * 8, 8)
        rows = pl.ds(r, 8)
        d = dep[rows, :]
        dep_e[rows, :] = jnp.where(lane8 == N - 1, 0.0, jnp.minimum(d, east_of(d)))
        dep_n[rows, :] = jnp.minimum(d, dep[pl.ds(r + 1, 8), :])
        return 0

    lax.fori_loop(0, N // 8, set_depth, 0, unroll=True)

    def set_columns(place, x):
        y = x.T
        cols[pl.ds(place * 16, 8), :] = y[N - 8 :]
        cols[pl.ds(place * 16 + 8, 8), :] = y[:8]

    set_columns(4 * NK, dep[pl.ds(0, N), :])
    set_columns(4 * NK + 1, fr[...])

    def pack(ref, f, double):
        def step(k, _):
            block = pl.ds(pl.multiple_of(k * N, N), N)
            x = ref[block, :]
            if double:
                x = x + x
                ref[block, :] = x
            set_columns(f * NK + k, x)
            return 0

        lax.fori_loop(0, NK, step, 0, unroll=4)


    def wide(x):
        return jnp.broadcast_to(x, (NK, N))

    def column(f, entry):
        return cols[pl.ds(f * NK * 16 + 6 + entry, NK, stride=16), :]

    def plane_column(i, entry):
        return wide(cols[pl.ds((4 * NK + i) * 16 + 6 + entry, 1), :])

    def columns(entry):
        t_c, u_c, k_c, v_c = (column(f, entry) for f in range(4))
        return t_c, u_c, v_c, k_c, plane_column(0, entry)

    def row(ref, j):
        return ref[pl.ds(j, NK, stride=N), :]

    def edge_rows(j):
        return (
            row(t, j), row(u, j), row(v, j), 2.0 * row(kd, j), wide(dep[pl.ds(j, 1), :]),
        )

    def x_face(a, b):
        return face(level, jnp.minimum(a[4], b[4]), a[1], b[1], a[0], b[0], a[3], b[3])

    def y_face(a, b):
        return face(level, jnp.minimum(a[4], b[4]), a[2], b[2], a[0], b[0], a[3], b[3])

    def closed_step(mid, through, along):
        flow = jnp.where(last, 0.0, along(mid, tuple(east_of(x) for x in mid)))
        tc, _, _, kc, d = mid
        above = jnp.where(
            level + 1.0 < d,
            (kc + pltpu.roll(kc, NK - 1, 0)) * (pltpu.roll(tc, NK - 1, 0) - tc),
            0.0,
        )
        total = through + (west_of(flow) - flow) + (above - pltpu.roll(above, 1, 0))
        return jnp.where(level < d, tc + SCALE * total, 0.0)

    def stage(side, values, tracer):
        for f in range(4):
            send[side, pl.ds(f * NK, NK), :] = values[f]
        send[side, pl.ds(4 * NK, NK), :] = tracer
        send[side, pl.ds(5 * NK, 8), :] = values[4][:8]

    def stage_corners(slab, values):
        x = jnp.zeros((NK, N), jnp.float32)
        for f in range(5):
            x = jnp.where(lane == f, pltpu.roll(values[f], f, 1) if f else values[f], x)
            x = jnp.where(lane == 8 + f, pltpu.roll(values[f], 9 + f, 1), x)
        csend[slab] = x

    for load in loads[3:]:
        load.wait()
    r_n, r_s = edge_rows(N - 1), edge_rows(0)
    stage(NORTH, r_n, closed_step(r_n, y_face(edge_rows(N - 2), r_n), x_face))
    stage(SOUTH, r_s, closed_step(r_s, -y_face(r_s, edge_rows(1)), x_face))
    stage_corners(0, r_n)
    stage_corners(1, r_s)

    pl.semaphore_wait(
        barrier,
        jnp.where(is_bottom, 5, 8) - own_e.astype(jnp.int32) - own_w.astype(jnp.int32),
    )

    def rim(side, slot, place):
        return pltpu.make_async_remote_copy(
            src_ref=send.at[side], dst_ref=recv.at[slot], send_sem=send_sem.at[side],
            recv_sem=recv_sem.at[slot], device_id=at(place), device_id_type=MESH,
        )

    def corner(slab, message, slot, place):
        return pltpu.make_async_remote_copy(
            src_ref=csend.at[slab], dst_ref=crecv.at[slot], send_sem=csend_sem.at[message],
            recv_sem=crecv_sem.at[slot], device_id=at(place), device_id_type=MESH,
        )

    to_north = rim(NORTH, jnp.where(is_top, NORTH, SOUTH), north)
    to_south = rim(SOUTH, NORTH, south)
    to_east, to_west = rim(EAST, WEST, east), rim(WEST, EAST, west)
    to_ne = corner(0, 0, jnp.where(is_top, NE, SW), north_e)
    to_nw = corner(0, 1, jnp.where(is_top, NW, SE), north_w)
    to_se, to_sw = corner(1, 2, NW, south_e), corner(1, 3, NE, south_w)

    to_north.start()

    @pl.when(not_own_e)
    def _():
        to_ne.start()

    @pl.when(not_own_w)
    def _():
        to_nw.start()

    @pl.when(not_bottom)
    def _():
        to_south.start()
        to_se.start()
        to_sw.start()

    for f, ref in enumerate((t, u, kd, v)):
        pack(ref, f, ref is kd)
    c_e, c_w = columns(1), columns(2)
    stage(EAST, c_e, closed_step(c_e, x_face(columns(0), c_e), y_face))
    stage(WEST, c_w, closed_step(c_w, -x_face(c_w, columns(3)), y_face))
    to_east.start()
    to_west.start()

    def tracer(b, _):
        r = pl.multiple_of(b * 8, 8)
        rows = pl.ds(r, 8)
        d, de, dn = dep[rows, :], dep_e[rows, :], dep_n[rows, :]
        below = zero8
        press = zero8
        for k in range(NK):
            c = float(k)
            here, up_rows = pl.ds(r + k * N, 8), pl.ds(r + k * N + 1, 8)
            tc, kc, uc, vc = t[here, :], kd[here, :], u[here, :], v[here, :]
            f_e = face(c, de, uc, east_of(uc), tc, east_of(tc), kc, east_of(kc))
            f_n = face(c, dn, vc, v[up_rows, :], tc, t[up_rows, :], kc, kd[up_rows, :])
            fa[pl.ds(r + k * PAD + 8, 8), :] = f_n
            f_s = fa[pl.ds(r + k * PAD + 7, 8), :]
            if k < NK - 1:
                t_up, k_up = t[pl.ds(r + (k + 1) * N, 8), :], kd[pl.ds(r + (k + 1) * N, 8), :]
                above = jnp.where(c + 1.0 < d, (kc + k_up) * (t_up - tc), 0.0)
            else:
                above = zero8
            total = (west_of(f_e) - f_e) + (f_s - f_n) + (above - below)
            below = above
            tc = jnp.where(c < d, tc + SCALE * total, 0.0)
            tn[here, :] = tc
            press = press + PG * tc
            p[pl.ds(r + k * PAD + 8, 8), :] = press
        return 0

    lax.fori_loop(0, N // 8, tracer, 0)

    def momentum(b, _):
        r = pl.multiple_of(b * 8, 8)
        rows = pl.ds(r, 8)
        d, de, dn = dep[rows, :], dep_e[rows, :], dep_n[rows, :]
        f, co = fr[rows, :], cor[rows, :]
        for k in range(NK):
            c = float(k)
            here, up_rows = pl.ds(r + k * N, 8), pl.ds(r + k * N + 1, 8)
            mine, south_rows = pl.ds(r + k * PAD + 8, 8), pl.ds(r + k * PAD + 7, 8)
            uc, vc, pc = u[here, :], v[here, :], p[mine, :]
            wet_e, wet_n, wet = c < de, c < dn, c < d
            u_e = jnp.where(wet_e, east_of(uc) - uc, 0.0)
            v_e = jnp.where(wet_e, east_of(vc) - vc, 0.0)
            u_n = jnp.where(wet_n, u[up_rows, :] - uc, 0.0)
            v_n = jnp.where(wet_n, v[up_rows, :] - vc, 0.0)
            fa[mine, :] = u_n
            fb[mine, :] = v_n
            lap_u = (u_e - west_of(u_e)) + (u_n - fa[south_rows, :])
            lap_v = (v_e - west_of(v_e)) + (v_n - fb[south_rows, :])
            dp_x = east_of(pc) - west_of(pc)
            dp_y = p[pl.ds(r + k * PAD + 9, 8), :] - p[south_rows, :]
            un[here, :] = jnp.where(wet, (uc + co * vc) - dp_x + f * lap_u, 0.0)
            vn[here, :] = jnp.where(wet, (vc - co * uc) - dp_y + f * lap_v, 0.0)
        return 0

    lax.fori_loop(0, N // 8, momentum, 0)

    rim(NORTH, NORTH, north).wait_recv()
    rim(EAST, EAST, east).wait_recv()
    rim(WEST, WEST, west).wait_recv()

    @pl.when(not_own_e)
    def _():
        corner(0, 0, NE, north_e).wait_recv()

    @pl.when(not_own_w)
    def _():
        corner(0, 1, NW, north_w).wait_recv()

    @pl.when(own_e)
    def _():
        crecv[NE] = csend[0]

    @pl.when(own_w)
    def _():
        crecv[NW] = csend[0]

    @pl.when(not_bottom)
    def _():
        rim(SOUTH, SOUTH, south).wait_recv()
        corner(1, 2, SE, south_e).wait_recv()
        corner(1, 3, SW, south_w).wait_recv()

    @pl.when(is_top)
    def _():
        x = mirrored(recv[NORTH])
        r = lax.broadcasted_iota(jnp.int32, (MSG, N), 0)
        recv[NORTH] = jnp.where((r >= NK) & (r < 3 * NK), -x, x)
        x = pltpu.roll(crecv[NW], 8, 1)
        crecv[NW] = jnp.where((lane == 9) | (lane == 10), -x, x)
        x = pltpu.roll(crecv[NE], N - 8, 1)
        crecv[NE] = jnp.where((lane == 1) | (lane == 2), -x, x)

    def ghost(slot):
        parts = [recv[slot, pl.ds(f * NK, NK), :] for f in range(4)]
        return (*parts, wide(recv[slot, pl.ds(5 * NK, 1), :]))

    def beyond(slot, entry, to):
        x = crecv[slot]
        return tuple(pltpu.roll(x, (to - entry - f) % N, 1) for f in range(5))

    g_w, g_e, g_s, g_n = ghost(WEST), ghost(EAST), ghost(SOUTH), ghost(NORTH)
    f_w, f_e = x_face(g_w, c_w), x_face(c_e, g_e)
    f_s, f_n = y_face(g_s, r_s), y_face(r_n, g_n)

    def whole(slot, flow, low, high):
        ends = jnp.where(first, low, jnp.where(last, high, 0.0))
        return running_sum(PG * (recv[slot, pl.ds(4 * NK, NK), :] + SCALE * (flow + ends)))

    p_w = whole(WEST, -f_w, y_face(beyond(SW, 8, 0), g_w), -y_face(g_w, beyond(NW, 8, N - 1)))
    p_e = whole(EAST, f_e, y_face(beyond(SE, 0, 0), g_e), -y_face(g_e, beyond(NE, 0, N - 1)))
    p_s = whole(SOUTH, -f_s, x_face(beyond(SW, 8, 0), g_s), -x_face(g_s, beyond(SE, 0, N - 1)))
    p_n = whole(NORTH, f_n, x_face(beyond(NW, 8, 0), g_n), -x_face(g_n, beyond(NE, 0, N - 1)))
    t_w, t_e, t_s, t_n = SCALE * f_w, -SCALE * f_e, SCALE * f_s, -SCALE * f_n
    d_w, d_e, d_s, d_n = (running_sum(PG * x) for x in (t_w, t_e, t_s, t_n))
    q_w = running_sum(PG * send[WEST, pl.ds(4 * NK, NK), :])
    q_e = running_sum(PG * send[EAST, pl.ds(4 * NK, NK), :])

    def across(x):
        return jnp.where(first, 0.0, west_of(x)) - jnp.where(last, 0.0, east_of(x))

    def friction(mid, other, f, i):
        m = level < jnp.minimum(mid[4], other[4])
        return jnp.where(m, f * (other[i] - mid[i]), 0.0)

    def masked(depth, x):
        return jnp.where(level < depth, x, 0.0)

    fr_e, fr_w = plane_column(1, 1), plane_column(1, 2)
    fr_s, fr_n = wide(fr[pl.ds(0, 1), :]), wide(fr[pl.ds(N - 1, 1), :])
    def add(ref, j, x):
        rows = pl.ds(j, NK, stride=N)
        ref[rows, :] = ref[rows, :] + x

    add(tn, N - 1, t_n)
    add(tn, 0, t_s)
    add(un, N - 1, friction(r_n, g_n, fr_n, 1) + masked(r_n[4], across(d_n)))
    add(un, 0, friction(r_s, g_s, fr_s, 1) + masked(r_s[4], across(d_s)))
    add(vn, N - 1, friction(r_n, g_n, fr_n, 2) - masked(r_n[4], p_n))
    add(vn, 0, friction(r_s, g_s, fr_s, 2) + masked(r_s[4], p_s))
    add(vn, N - 2, -masked(wide(dep[pl.ds(N - 2, 1), :]), d_n))
    add(vn, 1, masked(wide(dep[pl.ds(1, 1), :]), d_s))
    fix[pl.ds(0, NK, stride=4), :] = -masked(plane_column(0, 0), d_e)
    fix[pl.ds(1, NK, stride=4), :] = friction(c_e, g_e, fr_e, 1) - masked(c_e[4], p_e - q_w)
    fix[pl.ds(2, NK, stride=4), :] = friction(c_w, g_w, fr_w, 1) + masked(c_w[4], p_w - q_e)
    fix[pl.ds(3, NK, stride=4), :] = masked(plane_column(0, 3), d_w)
    fix[pl.ds(64, NK, stride=2), :] = friction(c_e, g_e, fr_e, 2) + masked(c_e[4], across(d_e))
    fix[pl.ds(65, NK, stride=2), :] = friction(c_w, g_w, fr_w, 2) + masked(c_w[4], across(d_w))
    fix[pl.ds(96, NK, stride=2), :] = t_e
    fix[pl.ds(97, NK, stride=2), :] = t_w
    fix[...] = fix[...].T
    rim2 = (lane8 == 0) | (lane8 == N - 1)
    rim4 = (lane8 <= 1) | (lane8 >= N - 2)

    def finish(b, _):
        r = pl.multiple_of(b * 8, 8)
        x = fix[pl.ds(r, 8), :]
        for k in range(NK):
            here = pl.ds(r + k * N, 8)
            un[here, :] = un[here, :] + jnp.where(rim4, pltpu.roll(x, N - 2 - 4 * k, 1), 0.0)
            vn[here, :] = vn[here, :] + jnp.where(rim2, pltpu.roll(x, 63 - 2 * k, 1), 0.0)
            tn[here, :] = tn[here, :] + jnp.where(rim2, pltpu.roll(x, 31 - 2 * k, 1), 0.0)
        return 0

    lax.fori_loop(0, N // 8, finish, 0, unroll=2)

    to_north.wait_send()
    to_east.wait_send()
    to_west.wait_send()

    @pl.when(not_own_e)
    def _():
        to_ne.wait_send()

    @pl.when(not_own_w)
    def _():
        to_nw.wait_send()

    @pl.when(not_bottom)
    def _():
        to_south.wait_send()
        to_se.wait_send()
        to_sw.wait_send()


def solution(mesh):
    n_lon, n_lat = mesh.shape["lon"], mesh.shape["lat"]
    f32, i32 = jnp.float32, jnp.int32

    def on_device(t, u, v, kd, fr, ind, strata):
        flat = [x.reshape(FLAT, N) for x in (t, u, v, kd)]
        outs = pl.pallas_call(
            functools.partial(kernel, n_lon, n_lat),
            out_shape=[pltpu.VMEM((FLAT, N), f32)] * 3,
            in_specs=[pl.BlockSpec(memory_space=pltpu.HBM)] * 7,
            out_specs=[pl.BlockSpec(memory_space=pltpu.VMEM)] * 3,
            scratch_shapes=[
                *[pltpu.VMEM((FLAT + 8, N), f32)] * 4,
                *[pltpu.VMEM((NK * PAD + 8, N), f32)] * 3,
                pltpu.VMEM((N, N), f32),
                pltpu.VMEM((N, N), i32),
                pltpu.VMEM((N, N), i32),
                pltpu.VMEM((N + 8, N), f32),
                *[pltpu.VMEM((N, N), f32)] * 3,
                pltpu.VMEM(((4 * NK + 2) * 16, N), f32),
                pltpu.VMEM((N, N), f32),
                pltpu.VMEM((4, MSG, N), f32),
                pltpu.VMEM((4, MSG, N), f32),
                pltpu.VMEM((4, NK, N), f32),
                pltpu.VMEM((4, NK, N), f32),
                pltpu.SemaphoreType.DMA((7,)),
                *[pltpu.SemaphoreType.DMA((4,))] * 4,
            ],
            compiler_params=pltpu.CompilerParams(
                collective_id=0, has_side_effects=True, vmem_limit_bytes=60 * 1024 * 1024
            ),
            cost_estimate=pl.CostEstimate(
                flops=80 * FLAT * N, bytes_accessed=30 * FLAT * N, transcendentals=0
            ),
        )(*flat, fr, ind, strata)
        return tuple(x.reshape(NK, N, N) for x in outs)

    plane, field = P("lat", "lon"), P(None, "lat", "lon")
    return jax.shard_map(
        on_device,
        mesh=mesh,
        in_specs=(field, field, field, field, plane, plane, plane),
        out_specs=(field, field, field),
        check_vma=False,
    )
```

```python
import functools
import math

import jax
import jax.numpy as jnp
from jax import lax
from jax.experimental import pallas as pl
from jax.experimental.pallas import tpu as pltpu
from jax.sharding import PartitionSpec as P

MESH = pl.DeviceIdType.MESH
NK = 16
N = 128
FLAT = NK * N
PAD = N + 8
SCALE = 1.0 / 16.0
PG = 0.25 * 0.05
WEST, EAST, SOUTH, NORTH = 0, 1, 2, 3
SW, SE, NW, NE = 0, 1, 2, 3
MSG = 5 * NK + 8


def east_of(x):
    return pltpu.roll(x, N - 1, 1)


def west_of(x):
    return pltpu.roll(x, 1, 1)


def face(c, d, a, b, ta, tb, ka, kb):
    return jnp.where(c < d, (a + b) * (ta + tb) - (ka + kb) * (tb - ta), 0.0)


def mirrored(x):
    lane = lax.broadcasted_iota(jnp.int32, x.shape, 1)
    for bit in (1, 2, 4, 8, 16, 32, 64):
        x = jnp.where((lane & bit) == 0, pltpu.roll(x, N - bit, 1), pltpu.roll(x, bit, 1))
    return x


def running_sum(x):
    level = lax.broadcasted_iota(jnp.int32, x.shape, 0)
    for step in (1, 2, 4, 8):
        x = x + jnp.where(level >= step, pltpu.roll(x, step, 0), 0.0)
    return x


def kernel(
    n_lon, n_lat,
    t_hbm, u_hbm, v_hbm, k_hbm, fr_hbm, ind_hbm, str_hbm,
    tn, un, vn, fix_out,
    t, u, v, kd, p, fa, fb, fr, ind, strata, dep, dep_e, dep_n, cor, fr_e,
    ue, cols, fix, send, recv, csend, crecv,
    in_sem, send_sem, recv_sem, csend_sem, crecv_sem,
):
    lon, lat = lax.axis_index("lon"), lax.axis_index("lat")
    is_top, is_bottom = lat == n_lat - 1, lat == 0
    not_bottom = jnp.logical_not(is_bottom)
    lon_e, lon_w = lax.rem(lon + 1, n_lon), lax.rem(lon + n_lon - 1, n_lon)
    lat_n, lat_s = jnp.where(is_top, lat, lat + 1), jnp.where(is_bottom, lat, lat - 1)
    east, west = (lat, lon_e), (lat, lon_w)
    north, south = (lat_n, jnp.where(is_top, n_lon - 1 - lon, lon)), (lat_s, lon)
    fold_e, fold_w = lax.rem(2 * n_lon - 2 - lon, n_lon), lax.rem(n_lon - lon, n_lon)
    own_e = is_top & (fold_e == lon)
    own_w = is_top & (fold_w == lon)
    not_own_e, not_own_w = jnp.logical_not(own_e), jnp.logical_not(own_w)
    north_e = (lat_n, jnp.where(is_top, fold_e, lon_e))
    north_w = (lat_n, jnp.where(is_top, fold_w, lon_w))
    south_e, south_w = (lat_s, lon_e), (lat_s, lon_w)

    def at(place):
        return {"lat": place[0], "lon": place[1]}

    loads = [
        pltpu.make_async_copy(src, dst, in_sem.at[i])
        for i, (src, dst) in enumerate(
            (
                (ind_hbm, ind), (str_hbm, strata), (fr_hbm, fr),
                (t_hbm, t.at[pl.ds(0, FLAT)]), (u_hbm, u.at[pl.ds(0, FLAT)]),
                (k_hbm, kd.at[pl.ds(0, FLAT)]), (v_hbm, v.at[pl.ds(0, FLAT)]),
            )
        )
    ]
    for load in loads:
        load.start()
    barrier = pltpu.get_barrier_semaphore()

    def greet(place):
        pl.semaphore_signal(barrier, inc=1, device_id=at(place), device_id_type=MESH)

    for place in (west, east, north):
        greet(place)

    @pl.when(not_own_e)
    def _():
        greet(north_e)

    @pl.when(not_own_w)
    def _():
        greet(north_w)

    @pl.when(not_bottom)
    def _():
        for place in (south, south_e, south_w):
            greet(place)

    lane8 = lax.broadcasted_iota(jnp.int32, (8, N), 1)
    zero8 = jnp.zeros((8, N), jnp.float32)
    lane = lax.broadcasted_iota(jnp.int32, (NK, N), 1)
    level = lax.broadcasted_iota(jnp.int32, (NK, N), 0).astype(jnp.float32)
    first, last = lane == 0, lane == N - 1

    for k in range(NK + 1):
        p[pl.ds(k * PAD, 8), :] = zero8
        fa[pl.ds(k * PAD, 8), :] = zero8
        fb[pl.ds(k * PAD, 8), :] = zero8

    @pl.when(is_bottom)
    def _():
        recv[SOUTH] = jnp.zeros((MSG, N), jnp.float32)
        crecv[SW] = jnp.zeros((NK, N), jnp.float32)
        crecv[SE] = jnp.zeros((NK, N), jnp.float32)

    def set_cor(b, _):
        rows = pl.ds(pl.multiple_of(b * 8, 8), 8)
        j = lax.broadcasted_iota(jnp.int32, (8, N), 0) + (b * 8 + lat * N)
        cor[rows, :] = 0.25 * jnp.sin(
            jnp.pi * ((j.astype(jnp.float32) + 0.5) / (N * n_lat) - 0.5)
        )
        return 0

    lax.fori_loop(0, N // 8, set_cor, 0)

    for load in loads[:3]:
        load.wait()
    dep[pl.ds(N, 8), :] = zero8
    dep[pl.ds(0, N), :] = (ind[...] * strata[...]).astype(jnp.float32)
    fr[...] = fr[...] * 0.25

    def set_depth(b, _):
        r = pl.multiple_of(b * 8, 8)
        rows = pl.ds(r, 8)
        d = dep[rows, :]
        dep_e[rows, :] = jnp.where(lane8 == N - 1, 0.0, jnp.minimum(d, east_of(d)))
        dep_n[rows, :] = jnp.minimum(d, dep[pl.ds(r + 1, 8), :])
        fr_e[rows, :] = east_of(fr[rows, :])
        return 0

    lax.fori_loop(0, N // 8, set_depth, 0, unroll=True)

    def set_columns(place, x):
        y = x.T
        cols[pl.ds(place * 16, 8), :] = y[N - 8 :]
        cols[pl.ds(place * 16 + 8, 8), :] = y[:8]

    set_columns(4 * NK, dep[pl.ds(0, N), :])
    set_columns(4 * NK + 1, fr[...])

    def pack(ref, f, double):
        def step(k, _):
            block = pl.ds(pl.multiple_of(k * N, N), N)
            x = ref[block, :]
            if double:
                x = x + x
                ref[block, :] = x
            set_columns(f * NK + k, x)
            return 0

        lax.fori_loop(0, NK, step, 0, unroll=4)


    def wide(x):
        return jnp.broadcast_to(x, (NK, N))

    def column(f, entry):
        return cols[pl.ds(f * NK * 16 + 6 + entry, NK, stride=16), :]

    def plane_column(i, entry):
        return wide(cols[pl.ds((4 * NK + i) * 16 + 6 + entry, 1), :])

    def columns(entry):
        t_c, u_c, k_c, v_c = (column(f, entry) for f in range(4))
        return t_c, u_c, v_c, k_c, plane_column(0, entry)

    def row(ref, j):
        return ref[pl.ds(j, NK, stride=N), :]

    def edge_rows(j):
        return (
            row(t, j), row(u, j), row(v, j), 2.0 * row(kd, j), wide(dep[pl.ds(j, 1), :]),
        )

    def x_face(a, b):
        return face(level, jnp.minimum(a[4], b[4]), a[1], b[1], a[0], b[0], a[3], b[3])

    def y_face(a, b):
        return face(level, jnp.minimum(a[4], b[4]), a[2], b[2], a[0], b[0], a[3], b[3])

    def closed_step(mid, through, along):
        flow = jnp.where(last, 0.0, along(mid, tuple(east_of(x) for x in mid)))
        tc, _, _, kc, d = mid
        above = jnp.where(
            level + 1.0 < d,
            (kc + pltpu.roll(kc, NK - 1, 0)) * (pltpu.roll(tc, NK - 1, 0) - tc),
            0.0,
        )
        total = through + (west_of(flow) - flow) + (above - pltpu.roll(above, 1, 0))
        return jnp.where(level < d, tc + SCALE * total, 0.0)

    def stage(side, values, tracer):
        for f in range(4):
            send[side, pl.ds(f * NK, NK), :] = values[f]
        send[side, pl.ds(4 * NK, NK), :] = tracer
        send[side, pl.ds(5 * NK, 8), :] = values[4][:8]

    def stage_corners(slab, values):
        x = jnp.zeros((NK, N), jnp.float32)
        for f in range(5):
            x = jnp.where(lane == f, pltpu.roll(values[f], f, 1) if f else values[f], x)
            x = jnp.where(lane == 8 + f, pltpu.roll(values[f], 9 + f, 1), x)
        csend[slab] = x

    for load in loads[3:]:
        load.wait()
    r_n, r_s = edge_rows(N - 1), edge_rows(0)
    stage(NORTH, r_n, closed_step(r_n, y_face(edge_rows(N - 2), r_n), x_face))
    stage(SOUTH, r_s, closed_step(r_s, -y_face(r_s, edge_rows(1)), x_face))
    stage_corners(0, r_n)
    stage_corners(1, r_s)

    pl.semaphore_wait(
        barrier,
        jnp.where(is_bottom, 5, 8) - own_e.astype(jnp.int32) - own_w.astype(jnp.int32),
    )

    def rim(side, slot, place):
        return pltpu.make_async_remote_copy(
            src_ref=send.at[side], dst_ref=recv.at[slot], send_sem=send_sem.at[side],
            recv_sem=recv_sem.at[slot], device_id=at(place), device_id_type=MESH,
        )

    def corner(slab, message, slot, place):
        return pltpu.make_async_remote_copy(
            src_ref=csend.at[slab], dst_ref=crecv.at[slot], send_sem=csend_sem.at[message],
            recv_sem=crecv_sem.at[slot], device_id=at(place), device_id_type=MESH,
        )

    to_north = rim(NORTH, jnp.where(is_top, NORTH, SOUTH), north)
    to_south = rim(SOUTH, NORTH, south)
    to_east, to_west = rim(EAST, WEST, east), rim(WEST, EAST, west)
    to_ne = corner(0, 0, jnp.where(is_top, NE, SW), north_e)
    to_nw = corner(0, 1, jnp.where(is_top, NW, SE), north_w)
    to_se, to_sw = corner(1, 2, NW, south_e), corner(1, 3, NE, south_w)

    to_north.start()

    @pl.when(not_own_e)
    def _():
        to_ne.start()

    @pl.when(not_own_w)
    def _():
        to_nw.start()

    @pl.when(not_bottom)
    def _():
        to_south.start()
        to_se.start()
        to_sw.start()

    for f, ref in enumerate((t, u, kd, v)):
        pack(ref, f, ref is kd)
    c_e, c_w = columns(1), columns(2)
    stage(EAST, c_e, closed_step(c_e, x_face(columns(0), c_e), y_face))
    stage(WEST, c_w, closed_step(c_w, -x_face(c_w, columns(3)), y_face))
    to_east.start()
    to_west.start()

    def tracer(b, _):
        r = pl.multiple_of(b * 8, 8)
        rows = pl.ds(r, 8)
        d, de, dn = dep[rows, :], dep_e[rows, :], dep_n[rows, :]
        below = zero8
        press = zero8
        for k in range(NK):
            c = float(k)
            here, up_rows = pl.ds(r + k * N, 8), pl.ds(r + k * N + 1, 8)
            tc, kc, uc, vc = t[here, :], kd[here, :], u[here, :], v[here, :]
            next_u = east_of(uc)
            ue[here, :] = next_u
            f_e = face(c, de, uc, next_u, tc, east_of(tc), kc, east_of(kc))
            f_n = face(c, dn, vc, v[up_rows, :], tc, t[up_rows, :], kc, kd[up_rows, :])
            fa[pl.ds(r + k * PAD + 8, 8), :] = f_n
            f_s = fa[pl.ds(r + k * PAD + 7, 8), :]
            if k < NK - 1:
                t_up, k_up = t[pl.ds(r + (k + 1) * N, 8), :], kd[pl.ds(r + (k + 1) * N, 8), :]
                above = jnp.where(c + 1.0 < d, (kc + k_up) * (t_up - tc), 0.0)
            else:
                above = zero8
            total = (west_of(f_e) - f_e) + (f_s - f_n) + (above - below)
            below = above
            tc = jnp.where(c < d, tc + SCALE * total, 0.0)
            tn[here, :] = tc
            press = press + PG * tc
            p[pl.ds(r + k * PAD + 8, 8), :] = press
        return 0

    lax.fori_loop(0, N // 8, tracer, 0, unroll=2)

    def momentum(b, _):
        r = pl.multiple_of(b * 8, 8)
        rows = pl.ds(r, 8)
        d, de, dn = dep[rows, :], dep_e[rows, :], dep_n[rows, :]
        f, f_next, co = fr[rows, :], fr_e[rows, :], cor[rows, :]
        for k in range(NK):
            c = float(k)
            here, up_rows = pl.ds(r + k * N, 8), pl.ds(r + k * N + 1, 8)
            mine, south_rows = pl.ds(r + k * PAD + 8, 8), pl.ds(r + k * PAD + 7, 8)
            uc, vc, pc = u[here, :], v[here, :], p[mine, :]
            wet_e, wet_n, wet = c < de, c < dn, c < d
            u_e = jnp.where(wet_e, ue[here, :] - uc, 0.0)
            v_e = jnp.where(wet_e, east_of(vc) - vc, 0.0)
            u_n = jnp.where(wet_n, u[up_rows, :] - uc, 0.0)
            v_n = jnp.where(wet_n, v[up_rows, :] - vc, 0.0)
            fa[mine, :] = u_n
            fb[mine, :] = v_n
            gain = east_of(pc) - pc
            across_x = (f * u_e - gain) - west_of(gain + f_next * u_e)
            lap_u = u_n - fa[south_rows, :]
            lap_v = (v_e - west_of(v_e)) + (v_n - fb[south_rows, :])
            dp_y = p[pl.ds(r + k * PAD + 9, 8), :] - p[south_rows, :]
            un[here, :] = jnp.where(wet, (uc + co * vc) + across_x + f * lap_u, 0.0)
            vn[here, :] = jnp.where(wet, (vc - co * uc) - dp_y + f * lap_v, 0.0)
        return 0

    lax.fori_loop(0, N // 8, momentum, 0)

    rim(NORTH, NORTH, north).wait_recv()
    rim(EAST, EAST, east).wait_recv()
    rim(WEST, WEST, west).wait_recv()

    @pl.when(not_own_e)
    def _():
        corner(0, 0, NE, north_e).wait_recv()

    @pl.when(not_own_w)
    def _():
        corner(0, 1, NW, north_w).wait_recv()

    @pl.when(own_e)
    def _():
        crecv[NE] = csend[0]

    @pl.when(own_w)
    def _():
        crecv[NW] = csend[0]

    @pl.when(not_bottom)
    def _():
        rim(SOUTH, SOUTH, south).wait_recv()
        corner(1, 2, SE, south_e).wait_recv()
        corner(1, 3, SW, south_w).wait_recv()

    @pl.when(is_top)
    def _():
        x = mirrored(recv[NORTH])
        r = lax.broadcasted_iota(jnp.int32, (MSG, N), 0)
        recv[NORTH] = jnp.where((r >= NK) & (r < 3 * NK), -x, x)
        x = pltpu.roll(crecv[NW], 8, 1)
        crecv[NW] = jnp.where((lane == 9) | (lane == 10), -x, x)
        x = pltpu.roll(crecv[NE], N - 8, 1)
        crecv[NE] = jnp.where((lane == 1) | (lane == 2), -x, x)

    def ghost(slot):
        parts = [recv[slot, pl.ds(f * NK, NK), :] for f in range(4)]
        return (*parts, wide(recv[slot, pl.ds(5 * NK, 1), :]))

    def beyond(slot, entry, to):
        x = crecv[slot]
        return tuple(pltpu.roll(x, (to - entry - f) % N, 1) for f in range(5))

    g_w, g_e, g_s, g_n = ghost(WEST), ghost(EAST), ghost(SOUTH), ghost(NORTH)
    f_w, f_e = x_face(g_w, c_w), x_face(c_e, g_e)
    f_s, f_n = y_face(g_s, r_s), y_face(r_n, g_n)

    def whole(slot, flow, low, high):
        ends = jnp.where(first, low, jnp.where(last, high, 0.0))
        return running_sum(PG * (recv[slot, pl.ds(4 * NK, NK), :] + SCALE * (flow + ends)))

    p_w = whole(WEST, -f_w, y_face(beyond(SW, 8, 0), g_w), -y_face(g_w, beyond(NW, 8, N - 1)))
    p_e = whole(EAST, f_e, y_face(beyond(SE, 0, 0), g_e), -y_face(g_e, beyond(NE, 0, N - 1)))
    p_s = whole(SOUTH, -f_s, x_face(beyond(SW, 8, 0), g_s), -x_face(g_s, beyond(SE, 0, N - 1)))
    p_n = whole(NORTH, f_n, x_face(beyond(NW, 8, 0), g_n), -x_face(g_n, beyond(NE, 0, N - 1)))
    t_w, t_e, t_s, t_n = SCALE * f_w, -SCALE * f_e, SCALE * f_s, -SCALE * f_n
    d_w, d_e, d_s, d_n = (running_sum(PG * x) for x in (t_w, t_e, t_s, t_n))
    q_w = running_sum(PG * send[WEST, pl.ds(4 * NK, NK), :])
    q_e = running_sum(PG * send[EAST, pl.ds(4 * NK, NK), :])

    def across(x):
        return jnp.where(first, 0.0, west_of(x)) - jnp.where(last, 0.0, east_of(x))

    def friction(mid, other, f, i):
        m = level < jnp.minimum(mid[4], other[4])
        return jnp.where(m, f * (other[i] - mid[i]), 0.0)

    def masked(depth, x):
        return jnp.where(level < depth, x, 0.0)

    col_e, col_w = plane_column(1, 1), plane_column(1, 2)
    row_s, row_n = wide(fr[pl.ds(0, 1), :]), wide(fr[pl.ds(N - 1, 1), :])
    def add(ref, j, x):
        rows = pl.ds(j, NK, stride=N)
        ref[rows, :] = ref[rows, :] + x

    add(tn, N - 1, t_n)
    add(tn, 0, t_s)
    add(un, N - 1, friction(r_n, g_n, row_n, 1) + masked(r_n[4], across(d_n)))
    add(un, 0, friction(r_s, g_s, row_s, 1) + masked(r_s[4], across(d_s)))
    add(vn, N - 1, friction(r_n, g_n, row_n, 2) - masked(r_n[4], p_n))
    add(vn, 0, friction(r_s, g_s, row_s, 2) + masked(r_s[4], p_s))
    add(vn, N - 2, -masked(wide(dep[pl.ds(N - 2, 1), :]), d_n))
    add(vn, 1, masked(wide(dep[pl.ds(1, 1), :]), d_s))
    fix[pl.ds(0, NK, stride=4), :] = -masked(plane_column(0, 0), d_e)
    fix[pl.ds(1, NK, stride=4), :] = friction(c_e, g_e, col_e, 1) - masked(c_e[4], p_e - q_w)
    fix[pl.ds(2, NK, stride=4), :] = friction(c_w, g_w, col_w, 1) + masked(c_w[4], p_w - q_e)
    fix[pl.ds(3, NK, stride=4), :] = masked(plane_column(0, 3), d_w)
    fix[pl.ds(64, NK, stride=2), :] = friction(c_e, g_e, col_e, 2) + masked(c_e[4], across(d_e))
    fix[pl.ds(65, NK, stride=2), :] = friction(c_w, g_w, col_w, 2) + masked(c_w[4], across(d_w))
    fix[pl.ds(96, NK, stride=2), :] = t_e
    fix[pl.ds(97, NK, stride=2), :] = t_w
    fix_out[...] = fix[...].T

    to_north.wait_send()
    to_east.wait_send()
    to_west.wait_send()

    @pl.when(not_own_e)
    def _():
        to_ne.wait_send()

    @pl.when(not_own_w)
    def _():
        to_nw.wait_send()

    @pl.when(not_bottom)
    def _():
        to_south.wait_send()
        to_se.wait_send()
        to_sw.wait_send()


def finish(tn, un, vn, fix, t_out, u_out, v_out, t, u, v, out_sem):
    lane8 = lax.broadcasted_iota(jnp.int32, (8, N), 1)
    rim2 = (lane8 == 0) | (lane8 == N - 1)
    rim4 = (lane8 <= 1) | (lane8 >= N - 2)

    def copies(k):
        block = pl.ds(pl.multiple_of(k * N, N), N)
        return [
            pltpu.make_async_copy(src.at[block], dst.at[block], out_sem.at[i, k])
            for i, (src, dst) in enumerate(((t, t_out), (u, u_out), (v, v_out)))
        ]

    def level(k, _):
        for r in range(0, N, 8):
            here = pl.ds(pl.multiple_of(k * N + r, 8), 8)
            x = fix[pl.ds(r, 8), :]
            for new, old, rim, shift in (
                (u, un, rim4, N - 2 - 4 * k), (v, vn, rim2, 63 - 2 * k), (t, tn, rim2, 31 - 2 * k),
            ):
                new[here, :] = old[here, :] + jnp.where(rim, pltpu.roll(x, shift, 1), 0.0)
        for copy in copies(k):
            copy.start()
        return 0

    lax.fori_loop(0, NK, level, 0)

    def drain(k, _):
        for copy in copies(k):
            copy.wait()
        return 0

    lax.fori_loop(0, NK, drain, 0)


def solution(mesh):
    n_lon, n_lat = mesh.shape["lon"], mesh.shape["lat"]
    f32, i32 = jnp.float32, jnp.int32

    def on_device(t, u, v, kd, fr, ind, strata):
        flat = [x.reshape(FLAT, N) for x in (t, u, v, kd)]
        outs = pl.pallas_call(
            functools.partial(kernel, n_lon, n_lat),
            out_shape=[*[pltpu.VMEM((FLAT, N), f32)] * 3, pltpu.VMEM((N, N), f32)],
            in_specs=[pl.BlockSpec(memory_space=pltpu.HBM)] * 7,
            out_specs=[pl.BlockSpec(memory_space=pltpu.VMEM)] * 4,
            scratch_shapes=[
                *[pltpu.VMEM((FLAT + 8, N), f32)] * 4,
                *[pltpu.VMEM((NK * PAD + 8, N), f32)] * 3,
                pltpu.VMEM((N, N), f32),
                pltpu.VMEM((N, N), i32),
                pltpu.VMEM((N, N), i32),
                pltpu.VMEM((N + 8, N), f32),
                *[pltpu.VMEM((N, N), f32)] * 4,
                pltpu.VMEM((FLAT, N), f32),
                pltpu.VMEM(((4 * NK + 2) * 16, N), f32),
                pltpu.VMEM((N, N), f32),
                pltpu.VMEM((4, MSG, N), f32),
                pltpu.VMEM((4, MSG, N), f32),
                pltpu.VMEM((4, NK, N), f32),
                pltpu.VMEM((4, NK, N), f32),
                pltpu.SemaphoreType.DMA((7,)),
                *[pltpu.SemaphoreType.DMA((4,))] * 4,
            ],
            compiler_params=pltpu.CompilerParams(
                collective_id=0, has_side_effects=True, vmem_limit_bytes=60 * 1024 * 1024
            ),
            cost_estimate=pl.CostEstimate(
                flops=80 * FLAT * N, bytes_accessed=30 * FLAT * N, transcendentals=0
            ),
        )(*flat, fr, ind, strata)
        outs = pl.pallas_call(
            finish,
            out_shape=[jax.ShapeDtypeStruct((FLAT, N), f32)] * 3,
            in_specs=[pl.BlockSpec(memory_space=pltpu.VMEM)] * 4,
            out_specs=[pl.BlockSpec(memory_space=pltpu.HBM)] * 3,
            scratch_shapes=[
                *[pltpu.VMEM((FLAT, N), f32)] * 3,
                pltpu.SemaphoreType.DMA((3, NK)),
            ],
            compiler_params=pltpu.CompilerParams(vmem_limit_bytes=32 * 1024 * 1024),
        )(*outs)
        return tuple(x.reshape(NK, N, N) for x in outs)

    plane, field = P("lat", "lon"), P(None, "lat", "lon")
    return jax.shard_map(
        on_device,
        mesh=mesh,
        in_specs=(field, field, field, field, plane, plane, plane),
        out_specs=(field, field, field),
        check_vma=False,
    )
```

```python
import functools
import math

import jax
import jax.numpy as jnp
from jax import lax
from jax.experimental import pallas as pl
from jax.experimental.pallas import tpu as pltpu
from jax.sharding import PartitionSpec as P

MESH = pl.DeviceIdType.MESH
NK = 16
N = 128
FLAT = NK * N
PAD = N + 8
SCALE = 1.0 / 16.0
PG = 0.25 * 0.05
WEST, EAST, SOUTH, NORTH = 0, 1, 2, 3
SW, SE, NW, NE = 0, 1, 2, 3
MSG = 5 * NK + 8
CHUNK = 4


def east_of(x):
    return pltpu.roll(x, N - 1, 1)


def west_of(x):
    return pltpu.roll(x, 1, 1)


def face(c, d, a, b, ta, tb, ka, kb):
    return jnp.where(c < d, (a + b) * (ta + tb) - (ka + kb) * (tb - ta), 0.0)


def mirrored(x):
    lane = lax.broadcasted_iota(jnp.int32, x.shape, 1)
    for bit in (1, 2, 4, 8, 16, 32, 64):
        x = jnp.where((lane & bit) == 0, pltpu.roll(x, N - bit, 1), pltpu.roll(x, bit, 1))
    return x


def running_sum(x):
    level = lax.broadcasted_iota(jnp.int32, x.shape, 0)
    for step in (1, 2, 4, 8):
        x = x + jnp.where(level >= step, pltpu.roll(x, step, 0), 0.0)
    return x


def kernel(
    n_lon, n_lat,
    t_hbm, u_hbm, v_hbm, k_hbm, fr_hbm, ind_hbm, str_hbm,
    tn, un, vn, fix_out,
    t, u, v, kd, p, fa, fb, fr, ind, strata, dep, dep_e, dep_n, cor, fr_e,
    ue, cols, fix, send, recv, csend, crecv,
    in_sem, send_sem, recv_sem, csend_sem, crecv_sem,
):
    lon, lat = lax.axis_index("lon"), lax.axis_index("lat")
    is_top, is_bottom = lat == n_lat - 1, lat == 0
    not_bottom = jnp.logical_not(is_bottom)
    lon_e, lon_w = lax.rem(lon + 1, n_lon), lax.rem(lon + n_lon - 1, n_lon)
    lat_n, lat_s = jnp.where(is_top, lat, lat + 1), jnp.where(is_bottom, lat, lat - 1)
    east, west = (lat, lon_e), (lat, lon_w)
    north, south = (lat_n, jnp.where(is_top, n_lon - 1 - lon, lon)), (lat_s, lon)
    fold_e, fold_w = lax.rem(2 * n_lon - 2 - lon, n_lon), lax.rem(n_lon - lon, n_lon)
    own_e = is_top & (fold_e == lon)
    own_w = is_top & (fold_w == lon)
    not_own_e, not_own_w = jnp.logical_not(own_e), jnp.logical_not(own_w)
    north_e = (lat_n, jnp.where(is_top, fold_e, lon_e))
    north_w = (lat_n, jnp.where(is_top, fold_w, lon_w))
    south_e, south_w = (lat_s, lon_e), (lat_s, lon_w)

    def at(place):
        return {"lat": place[0], "lon": place[1]}

    loads = [
        pltpu.make_async_copy(src, dst, in_sem.at[i])
        for i, (src, dst) in enumerate(
            (
                (ind_hbm, ind), (str_hbm, strata), (fr_hbm, fr),
                (t_hbm, t.at[pl.ds(0, FLAT)]), (u_hbm, u.at[pl.ds(0, FLAT)]),
                (k_hbm, kd.at[pl.ds(0, FLAT)]), (v_hbm, v.at[pl.ds(0, FLAT)]),
            )
        )
    ]
    for load in loads:
        load.start()
    barrier = pltpu.get_barrier_semaphore()

    def greet(place):
        pl.semaphore_signal(barrier, inc=1, device_id=at(place), device_id_type=MESH)

    for place in (west, east, north):
        greet(place)

    @pl.when(not_own_e)
    def _():
        greet(north_e)

    @pl.when(not_own_w)
    def _():
        greet(north_w)

    @pl.when(not_bottom)
    def _():
        for place in (south, south_e, south_w):
            greet(place)

    lane8 = lax.broadcasted_iota(jnp.int32, (8, N), 1)
    zero8 = jnp.zeros((8, N), jnp.float32)
    lane = lax.broadcasted_iota(jnp.int32, (NK, N), 1)
    level = lax.broadcasted_iota(jnp.int32, (NK, N), 0).astype(jnp.float32)
    first, last = lane == 0, lane == N - 1

    for k in range(NK + 1):
        p[pl.ds(k * PAD, 8), :] = zero8
        fa[pl.ds(k * PAD, 8), :] = zero8
        fb[pl.ds(k * PAD, 8), :] = zero8

    @pl.when(is_bottom)
    def _():
        recv[SOUTH] = jnp.zeros((MSG, N), jnp.float32)
        crecv[SW] = jnp.zeros((NK, N), jnp.float32)
        crecv[SE] = jnp.zeros((NK, N), jnp.float32)

    def set_cor(b, _):
        rows = pl.ds(pl.multiple_of(b * 8, 8), 8)
        j = lax.broadcasted_iota(jnp.int32, (8, N), 0) + (b * 8 + lat * N)
        cor[rows, :] = 0.25 * jnp.sin(
            jnp.pi * ((j.astype(jnp.float32) + 0.5) / (N * n_lat) - 0.5)
        )
        return 0

    lax.fori_loop(0, N // 8, set_cor, 0)

    for load in loads[:3]:
        load.wait()
    dep[pl.ds(N, 8), :] = zero8
    dep[pl.ds(0, N), :] = (ind[...] * strata[...]).astype(jnp.float32)
    fr[...] = fr[...] * 0.25

    def set_depth(b, _):
        r = pl.multiple_of(b * 8, 8)
        rows = pl.ds(r, 8)
        d = dep[rows, :]
        dep_e[rows, :] = jnp.where(lane8 == N - 1, 0.0, jnp.minimum(d, east_of(d)))
        dep_n[rows, :] = jnp.minimum(d, dep[pl.ds(r + 1, 8), :])
        fr_e[rows, :] = east_of(fr[rows, :])
        return 0

    lax.fori_loop(0, N // 8, set_depth, 0, unroll=True)

    def set_columns(place, x):
        y = x.T
        cols[pl.ds(place * 16, 8), :] = y[N - 8 :]
        cols[pl.ds(place * 16 + 8, 8), :] = y[:8]

    set_columns(4 * NK, dep[pl.ds(0, N), :])
    set_columns(4 * NK + 1, fr[...])

    def pack(ref, f, double):
        def step(k, _):
            block = pl.ds(pl.multiple_of(k * N, N), N)
            x = ref[block, :]
            if double:
                x = x + x
                ref[block, :] = x
            set_columns(f * NK + k, x)
            return 0

        lax.fori_loop(0, NK, step, 0, unroll=8)


    def wide(x):
        return jnp.broadcast_to(x, (NK, N))

    def column(f, entry):
        return cols[pl.ds(f * NK * 16 + 6 + entry, NK, stride=16), :]

    def plane_column(i, entry):
        return wide(cols[pl.ds((4 * NK + i) * 16 + 6 + entry, 1), :])

    def columns(entry):
        t_c, u_c, k_c, v_c = (column(f, entry) for f in range(4))
        return t_c, u_c, v_c, k_c, plane_column(0, entry)

    def row(ref, j):
        return ref[pl.ds(j, NK, stride=N), :]

    def edge_rows(j):
        return (
            row(t, j), row(u, j), row(v, j), 2.0 * row(kd, j), wide(dep[pl.ds(j, 1), :]),
        )

    def x_face(a, b):
        return face(level, jnp.minimum(a[4], b[4]), a[1], b[1], a[0], b[0], a[3], b[3])

    def y_face(a, b):
        return face(level, jnp.minimum(a[4], b[4]), a[2], b[2], a[0], b[0], a[3], b[3])

    def closed_step(mid, through, along):
        flow = jnp.where(last, 0.0, along(mid, tuple(east_of(x) for x in mid)))
        tc, _, _, kc, d = mid
        above = jnp.where(
            level + 1.0 < d,
            (kc + pltpu.roll(kc, NK - 1, 0)) * (pltpu.roll(tc, NK - 1, 0) - tc),
            0.0,
        )
        total = through + (west_of(flow) - flow) + (above - pltpu.roll(above, 1, 0))
        return jnp.where(level < d, tc + SCALE * total, 0.0)

    def stage(side, values, tracer):
        for f in range(4):
            send[side, pl.ds(f * NK, NK), :] = values[f]
        send[side, pl.ds(4 * NK, NK), :] = tracer
        send[side, pl.ds(5 * NK, 8), :] = values[4][:8]

    def stage_corners(slab, values):
        x = jnp.zeros((NK, N), jnp.float32)
        for f in range(5):
            x = jnp.where(lane == f, pltpu.roll(values[f], f, 1) if f else values[f], x)
            x = jnp.where(lane == 8 + f, pltpu.roll(values[f], 9 + f, 1), x)
        csend[slab] = x

    for load in loads[3:]:
        load.wait()
    r_n, r_s = edge_rows(N - 1), edge_rows(0)
    stage(NORTH, r_n, closed_step(r_n, y_face(edge_rows(N - 2), r_n), x_face))
    stage(SOUTH, r_s, closed_step(r_s, -y_face(r_s, edge_rows(1)), x_face))
    stage_corners(0, r_n)
    stage_corners(1, r_s)

    for f, ref in enumerate((t, u, kd, v)):
        pack(ref, f, ref is kd)
    c_e, c_w = columns(1), columns(2)
    stage(EAST, c_e, closed_step(c_e, x_face(columns(0), c_e), y_face))
    stage(WEST, c_w, closed_step(c_w, -x_face(c_w, columns(3)), y_face))

    pl.semaphore_wait(
        barrier,
        jnp.where(is_bottom, 5, 8) - own_e.astype(jnp.int32) - own_w.astype(jnp.int32),
    )

    def rim(side, slot, place):
        return pltpu.make_async_remote_copy(
            src_ref=send.at[side], dst_ref=recv.at[slot], send_sem=send_sem.at[side],
            recv_sem=recv_sem.at[slot], device_id=at(place), device_id_type=MESH,
        )

    def corner(slab, message, slot, place):
        return pltpu.make_async_remote_copy(
            src_ref=csend.at[slab], dst_ref=crecv.at[slot], send_sem=csend_sem.at[message],
            recv_sem=crecv_sem.at[slot], device_id=at(place), device_id_type=MESH,
        )

    to_north = rim(NORTH, jnp.where(is_top, NORTH, SOUTH), north)
    to_south = rim(SOUTH, NORTH, south)
    to_east, to_west = rim(EAST, WEST, east), rim(WEST, EAST, west)
    to_ne = corner(0, 0, jnp.where(is_top, NE, SW), north_e)
    to_nw = corner(0, 1, jnp.where(is_top, NW, SE), north_w)
    to_se, to_sw = corner(1, 2, NW, south_e), corner(1, 3, NE, south_w)

    to_north.start()

    @pl.when(not_own_e)
    def _():
        to_ne.start()

    @pl.when(not_own_w)
    def _():
        to_nw.start()

    @pl.when(not_bottom)
    def _():
        to_south.start()
        to_se.start()
        to_sw.start()

    to_east.start()
    to_west.start()

    def tracer(b, _):
        r = pl.multiple_of(b * 8, 8)
        rows = pl.ds(r, 8)
        d, de, dn = dep[rows, :], dep_e[rows, :], dep_n[rows, :]
        below = zero8
        press = zero8
        for k in range(NK):
            c = float(k)
            here, up_rows = pl.ds(r + k * N, 8), pl.ds(r + k * N + 1, 8)
            tc, kc, uc, vc = t[here, :], kd[here, :], u[here, :], v[here, :]
            next_u = east_of(uc)
            ue[here, :] = next_u
            f_e = face(c, de, uc, next_u, tc, east_of(tc), kc, east_of(kc))
            f_n = face(c, dn, vc, v[up_rows, :], tc, t[up_rows, :], kc, kd[up_rows, :])
            fa[pl.ds(r + k * PAD + 8, 8), :] = f_n
            f_s = fa[pl.ds(r + k * PAD + 7, 8), :]
            if k < NK - 1:
                t_up, k_up = t[pl.ds(r + (k + 1) * N, 8), :], kd[pl.ds(r + (k + 1) * N, 8), :]
                above = jnp.where(c + 1.0 < d, (kc + k_up) * (t_up - tc), 0.0)
            else:
                above = zero8
            total = (west_of(f_e) - f_e) + (f_s - f_n) + (above - below)
            below = above
            tc = jnp.where(c < d, tc + SCALE * total, 0.0)
            tn[here, :] = tc
            press = press + PG * tc
            p[pl.ds(r + k * PAD + 8, 8), :] = press
        return 0

    lax.fori_loop(0, N // 8, tracer, 0, unroll=2)

    def momentum(b, _):
        r = pl.multiple_of(b * 8, 8)
        rows = pl.ds(r, 8)
        d, de, dn = dep[rows, :], dep_e[rows, :], dep_n[rows, :]
        f, f_next, co = fr[rows, :], fr_e[rows, :], cor[rows, :]
        for k in range(NK):
            c = float(k)
            here, up_rows = pl.ds(r + k * N, 8), pl.ds(r + k * N + 1, 8)
            mine, south_rows = pl.ds(r + k * PAD + 8, 8), pl.ds(r + k * PAD + 7, 8)
            uc, vc, pc = u[here, :], v[here, :], p[mine, :]
            wet_e, wet_n, wet = c < de, c < dn, c < d
            u_e = jnp.where(wet_e, ue[here, :] - uc, 0.0)
            v_e = jnp.where(wet_e, east_of(vc) - vc, 0.0)
            u_n = jnp.where(wet_n, u[up_rows, :] - uc, 0.0)
            v_n = jnp.where(wet_n, v[up_rows, :] - vc, 0.0)
            fa[mine, :] = u_n
            fb[mine, :] = v_n
            gain = east_of(pc) - pc
            across_x = (f * u_e - gain) - west_of(gain + f_next * u_e)
            lap_u = u_n - fa[south_rows, :]
            lap_v = (v_e - west_of(v_e)) + (v_n - fb[south_rows, :])
            dp_y = p[pl.ds(r + k * PAD + 9, 8), :] - p[south_rows, :]
            un[here, :] = jnp.where(wet, (uc + co * vc) + across_x + f * lap_u, 0.0)
            vn[here, :] = jnp.where(wet, (vc - co * uc) - dp_y + f * lap_v, 0.0)
        return 0

    lax.fori_loop(0, N // 8, momentum, 0)

    rim(NORTH, NORTH, north).wait_recv()
    rim(EAST, EAST, east).wait_recv()
    rim(WEST, WEST, west).wait_recv()

    @pl.when(not_own_e)
    def _():
        corner(0, 0, NE, north_e).wait_recv()

    @pl.when(not_own_w)
    def _():
        corner(0, 1, NW, north_w).wait_recv()

    @pl.when(own_e)
    def _():
        crecv[NE] = csend[0]

    @pl.when(own_w)
    def _():
        crecv[NW] = csend[0]

    @pl.when(not_bottom)
    def _():
        rim(SOUTH, SOUTH, south).wait_recv()
        corner(1, 2, SE, south_e).wait_recv()
        corner(1, 3, SW, south_w).wait_recv()

    @pl.when(is_top)
    def _():
        x = mirrored(recv[NORTH])
        r = lax.broadcasted_iota(jnp.int32, (MSG, N), 0)
        recv[NORTH] = jnp.where((r >= NK) & (r < 3 * NK), -x, x)
        x = pltpu.roll(crecv[NW], 8, 1)
        crecv[NW] = jnp.where((lane == 9) | (lane == 10), -x, x)
        x = pltpu.roll(crecv[NE], N - 8, 1)
        crecv[NE] = jnp.where((lane == 1) | (lane == 2), -x, x)

    def ghost(slot):
        parts = [recv[slot, pl.ds(f * NK, NK), :] for f in range(4)]
        return (*parts, wide(recv[slot, pl.ds(5 * NK, 1), :]))

    def beyond(slot, entry, to):
        x = crecv[slot]
        return tuple(pltpu.roll(x, (to - entry - f) % N, 1) for f in range(5))

    g_w, g_e, g_s, g_n = ghost(WEST), ghost(EAST), ghost(SOUTH), ghost(NORTH)
    f_w, f_e = x_face(g_w, c_w), x_face(c_e, g_e)
    f_s, f_n = y_face(g_s, r_s), y_face(r_n, g_n)

    def whole(slot, flow, low, high):
        ends = jnp.where(first, low, jnp.where(last, high, 0.0))
        return running_sum(PG * (recv[slot, pl.ds(4 * NK, NK), :] + SCALE * (flow + ends)))

    p_w = whole(WEST, -f_w, y_face(beyond(SW, 8, 0), g_w), -y_face(g_w, beyond(NW, 8, N - 1)))
    p_e = whole(EAST, f_e, y_face(beyond(SE, 0, 0), g_e), -y_face(g_e, beyond(NE, 0, N - 1)))
    p_s = whole(SOUTH, -f_s, x_face(beyond(SW, 8, 0), g_s), -x_face(g_s, beyond(SE, 0, N - 1)))
    p_n = whole(NORTH, f_n, x_face(beyond(NW, 8, 0), g_n), -x_face(g_n, beyond(NE, 0, N - 1)))
    t_w, t_e, t_s, t_n = SCALE * f_w, -SCALE * f_e, SCALE * f_s, -SCALE * f_n
    d_w, d_e, d_s, d_n = (running_sum(PG * x) for x in (t_w, t_e, t_s, t_n))
    q_w = running_sum(PG * send[WEST, pl.ds(4 * NK, NK), :])
    q_e = running_sum(PG * send[EAST, pl.ds(4 * NK, NK), :])

    def across(x):
        return jnp.where(first, 0.0, west_of(x)) - jnp.where(last, 0.0, east_of(x))

    def friction(mid, other, f, i):
        m = level < jnp.minimum(mid[4], other[4])
        return jnp.where(m, f * (other[i] - mid[i]), 0.0)

    def masked(depth, x):
        return jnp.where(level < depth, x, 0.0)

    col_e, col_w = plane_column(1, 1), plane_column(1, 2)
    row_s, row_n = wide(fr[pl.ds(0, 1), :]), wide(fr[pl.ds(N - 1, 1), :])
    def add(ref, j, x):
        rows = pl.ds(j, NK, stride=N)
        ref[rows, :] = ref[rows, :] + x

    add(tn, N - 1, t_n)
    add(tn, 0, t_s)
    add(un, N - 1, friction(r_n, g_n, row_n, 1) + masked(r_n[4], across(d_n)))
    add(un, 0, friction(r_s, g_s, row_s, 1) + masked(r_s[4], across(d_s)))
    add(vn, N - 1, friction(r_n, g_n, row_n, 2) - masked(r_n[4], p_n))
    add(vn, 0, friction(r_s, g_s, row_s, 2) + masked(r_s[4], p_s))
    add(vn, N - 2, -masked(wide(dep[pl.ds(N - 2, 1), :]), d_n))
    add(vn, 1, masked(wide(dep[pl.ds(1, 1), :]), d_s))
    fix[pl.ds(0, NK, stride=4), :] = -masked(plane_column(0, 0), d_e)
    fix[pl.ds(1, NK, stride=4), :] = friction(c_e, g_e, col_e, 1) - masked(c_e[4], p_e - q_w)
    fix[pl.ds(2, NK, stride=4), :] = friction(c_w, g_w, col_w, 1) + masked(c_w[4], p_w - q_e)
    fix[pl.ds(3, NK, stride=4), :] = masked(plane_column(0, 3), d_w)
    fix[pl.ds(64, NK, stride=2), :] = friction(c_e, g_e, col_e, 2) + masked(c_e[4], across(d_e))
    fix[pl.ds(65, NK, stride=2), :] = friction(c_w, g_w, col_w, 2) + masked(c_w[4], across(d_w))
    fix[pl.ds(96, NK, stride=2), :] = t_e
    fix[pl.ds(97, NK, stride=2), :] = t_w
    fix_out[...] = fix[...].T

    to_north.wait_send()
    to_east.wait_send()
    to_west.wait_send()

    @pl.when(not_own_e)
    def _():
        to_ne.wait_send()

    @pl.when(not_own_w)
    def _():
        to_nw.wait_send()

    @pl.when(not_bottom)
    def _():
        to_south.wait_send()
        to_se.wait_send()
        to_sw.wait_send()


def finish(tn, un, vn, fix, t_out, u_out, v_out, t, u, v, out_sem):
    lane8 = lax.broadcasted_iota(jnp.int32, (8, N), 1)
    rim2 = (lane8 == 0) | (lane8 == N - 1)
    rim4 = (lane8 <= 1) | (lane8 >= N - 2)

    outs = ((t, t_out), (u, u_out), (v, v_out))

    def step(g, _):
        for k in range(CHUNK):
            start = pl.multiple_of((g * CHUNK + k) * N, N)
            for r in range(0, N, 8):
                here = pl.ds(start + r, 8)
                x = fix[pl.ds(r, 8), :]
                for new, old, rim, shift in (
                    (u, un, rim4, N - 2 - 4 * k), (v, vn, rim2, 63 - 2 * k), (t, tn, rim2, 31 - 2 * k),
                ):
                    shift = lax.rem(shift + N - g * CHUNK * (4 if rim is rim4 else 2), N)
                    new[here, :] = old[here, :] + jnp.where(rim, pltpu.roll(x, shift, 1), 0.0)
        block = pl.ds(pl.multiple_of(g * CHUNK * N, N), CHUNK * N)
        for i, (src, dst) in enumerate(outs):
            pltpu.make_async_copy(src.at[block], dst.at[block], out_sem.at[i]).start()
        return 0

    lax.fori_loop(0, NK // CHUNK, step, 0)
    for i, (src, dst) in enumerate(outs):
        pltpu.make_async_copy(src, dst, out_sem.at[i]).wait()


def solution(mesh):
    n_lon, n_lat = mesh.shape["lon"], mesh.shape["lat"]
    f32, i32 = jnp.float32, jnp.int32

    def on_device(t, u, v, kd, fr, ind, strata):
        flat = [x.reshape(FLAT, N) for x in (t, u, v, kd)]
        outs = pl.pallas_call(
            functools.partial(kernel, n_lon, n_lat),
            out_shape=[*[pltpu.VMEM((FLAT, N), f32)] * 3, pltpu.VMEM((N, N), f32)],
            in_specs=[pl.BlockSpec(memory_space=pltpu.HBM)] * 7,
            out_specs=[pl.BlockSpec(memory_space=pltpu.VMEM)] * 4,
            scratch_shapes=[
                *[pltpu.VMEM((FLAT + 8, N), f32)] * 4,
                *[pltpu.VMEM((NK * PAD + 8, N), f32)] * 3,
                pltpu.VMEM((N, N), f32),
                pltpu.VMEM((N, N), i32),
                pltpu.VMEM((N, N), i32),
                pltpu.VMEM((N + 8, N), f32),
                *[pltpu.VMEM((N, N), f32)] * 4,
                pltpu.VMEM((FLAT, N), f32),
                pltpu.VMEM(((4 * NK + 2) * 16, N), f32),
                pltpu.VMEM((N, N), f32),
                pltpu.VMEM((4, MSG, N), f32),
                pltpu.VMEM((4, MSG, N), f32),
                pltpu.VMEM((4, NK, N), f32),
                pltpu.VMEM((4, NK, N), f32),
                pltpu.SemaphoreType.DMA((7,)),
                *[pltpu.SemaphoreType.DMA((4,))] * 4,
            ],
            compiler_params=pltpu.CompilerParams(
                collective_id=0, has_side_effects=True, vmem_limit_bytes=60 * 1024 * 1024
            ),
            cost_estimate=pl.CostEstimate(
                flops=80 * FLAT * N, bytes_accessed=30 * FLAT * N, transcendentals=0
            ),
        )(*flat, fr, ind, strata)
        outs = pl.pallas_call(
            finish,
            out_shape=[jax.ShapeDtypeStruct((FLAT, N), f32)] * 3,
            in_specs=[pl.BlockSpec(memory_space=pltpu.VMEM)] * 4,
            out_specs=[pl.BlockSpec(memory_space=pltpu.HBM)] * 3,
            scratch_shapes=[
                *[pltpu.VMEM((FLAT, N), f32)] * 3,
                pltpu.SemaphoreType.DMA((3,)),
            ],
            compiler_params=pltpu.CompilerParams(vmem_limit_bytes=32 * 1024 * 1024),
        )(*outs)
        return tuple(x.reshape(NK, N, N) for x in outs)

    plane, field = P("lat", "lon"), P(None, "lat", "lon")
    return jax.shard_map(
        on_device,
        mesh=mesh,
        in_specs=(field, field, field, field, plane, plane, plane),
        out_specs=(field, field, field),
        check_vma=False,
    )
```

```python
import functools
import math

import jax
import jax.numpy as jnp
from jax import lax
from jax.experimental import pallas as pl
from jax.experimental.pallas import tpu as pltpu
from jax.sharding import PartitionSpec as P

MESH = pl.DeviceIdType.MESH
NK = 16
N = 128
FLAT = NK * N
PAD = N + 8
SCALE = 1.0 / 16.0
PG = 0.25 * 0.05
WEST, EAST, SOUTH, NORTH = 0, 1, 2, 3
SW, SE, NW, NE = 0, 1, 2, 3
MSG = 5 * NK + 8
CHUNK = 4


def east_of(x):
    return pltpu.roll(x, N - 1, 1)


def west_of(x):
    return pltpu.roll(x, 1, 1)


def face(c, d, a, b, ta, tb, ka, kb):
    return jnp.where(c < d, (a + b) * (ta + tb) - (ka + kb) * (tb - ta), 0.0)


def mirrored(x):
    lane = lax.broadcasted_iota(jnp.int32, x.shape, 1)
    for bit in (1, 2, 4, 8, 16, 32, 64):
        x = jnp.where((lane & bit) == 0, pltpu.roll(x, N - bit, 1), pltpu.roll(x, bit, 1))
    return x


def running_sum(x):
    level = lax.broadcasted_iota(jnp.int32, x.shape, 0)
    for step in (1, 2, 4, 8):
        x = x + jnp.where(level >= step, pltpu.roll(x, step, 0), 0.0)
    return x


def kernel(
    n_lon, n_lat,
    t_hbm, u_hbm, v_hbm, k_hbm, fr_hbm, ind_hbm, str_hbm,
    tn, un, vn, fix_out,
    t, u, v, kd, p, fa, fb, fr, ind, strata, dep, dep_e, dep_n, cor, fr_e,
    ue, cols, fix, send, recv, csend, crecv,
    in_sem, send_sem, recv_sem, csend_sem, crecv_sem,
):
    lon, lat = lax.axis_index("lon"), lax.axis_index("lat")
    is_top, is_bottom = lat == n_lat - 1, lat == 0
    not_bottom = jnp.logical_not(is_bottom)
    lon_e, lon_w = lax.rem(lon + 1, n_lon), lax.rem(lon + n_lon - 1, n_lon)
    lat_n, lat_s = jnp.where(is_top, lat, lat + 1), jnp.where(is_bottom, lat, lat - 1)
    east, west = (lat, lon_e), (lat, lon_w)
    north, south = (lat_n, jnp.where(is_top, n_lon - 1 - lon, lon)), (lat_s, lon)
    fold_e, fold_w = lax.rem(2 * n_lon - 2 - lon, n_lon), lax.rem(n_lon - lon, n_lon)
    own_e = is_top & (fold_e == lon)
    own_w = is_top & (fold_w == lon)
    not_own_e, not_own_w = jnp.logical_not(own_e), jnp.logical_not(own_w)
    north_e = (lat_n, jnp.where(is_top, fold_e, lon_e))
    north_w = (lat_n, jnp.where(is_top, fold_w, lon_w))
    south_e, south_w = (lat_s, lon_e), (lat_s, lon_w)

    def at(place):
        return {"lat": place[0], "lon": place[1]}

    loads = [
        pltpu.make_async_copy(src, dst, in_sem.at[i])
        for i, (src, dst) in enumerate(
            (
                (ind_hbm, ind), (str_hbm, strata), (fr_hbm, fr),
                (t_hbm, t.at[pl.ds(0, FLAT)]), (u_hbm, u.at[pl.ds(0, FLAT)]),
                (k_hbm, kd.at[pl.ds(0, FLAT)]), (v_hbm, v.at[pl.ds(0, FLAT)]),
            )
        )
    ]
    for load in loads:
        load.start()
    barrier = pltpu.get_barrier_semaphore()

    def greet(place):
        pl.semaphore_signal(barrier, inc=1, device_id=at(place), device_id_type=MESH)

    for place in (west, east, north):
        greet(place)

    @pl.when(not_own_e)
    def _():
        greet(north_e)

    @pl.when(not_own_w)
    def _():
        greet(north_w)

    @pl.when(not_bottom)
    def _():
        for place in (south, south_e, south_w):
            greet(place)

    lane8 = lax.broadcasted_iota(jnp.int32, (8, N), 1)
    zero8 = jnp.zeros((8, N), jnp.float32)
    lane = lax.broadcasted_iota(jnp.int32, (NK, N), 1)
    level = lax.broadcasted_iota(jnp.int32, (NK, N), 0).astype(jnp.float32)
    first, last = lane == 0, lane == N - 1

    for k in range(NK + 1):
        p[pl.ds(k * PAD, 8), :] = zero8
        fa[pl.ds(k * PAD, 8), :] = zero8
        fb[pl.ds(k * PAD, 8), :] = zero8

    @pl.when(is_bottom)
    def _():
        recv[SOUTH] = jnp.zeros((MSG, N), jnp.float32)
        crecv[SW] = jnp.zeros((NK, N), jnp.float32)
        crecv[SE] = jnp.zeros((NK, N), jnp.float32)

    def set_cor(b, _):
        rows = pl.ds(pl.multiple_of(b * 8, 8), 8)
        j = lax.broadcasted_iota(jnp.int32, (8, N), 0) + (b * 8 + lat * N)
        cor[rows, :] = 0.25 * jnp.sin(
            jnp.pi * ((j.astype(jnp.float32) + 0.5) / (N * n_lat) - 0.5)
        )
        return 0

    lax.fori_loop(0, N // 8, set_cor, 0)

    for load in loads[:3]:
        load.wait()
    dep[pl.ds(N, 8), :] = zero8
    dep[pl.ds(0, N), :] = (ind[...] * strata[...]).astype(jnp.float32)
    fr[...] = fr[...] * 0.25

    def set_depth(b, _):
        r = pl.multiple_of(b * 8, 8)
        rows = pl.ds(r, 8)
        d = dep[rows, :]
        dep_e[rows, :] = jnp.where(lane8 == N - 1, 0.0, jnp.minimum(d, east_of(d)))
        dep_n[rows, :] = jnp.minimum(d, dep[pl.ds(r + 1, 8), :])
        fr_e[rows, :] = east_of(fr[rows, :])
        return 0

    lax.fori_loop(0, N // 8, set_depth, 0, unroll=True)

    def set_columns(place, x):
        y = x.T
        cols[pl.ds(place * 16, 8), :] = y[N - 8 :]
        cols[pl.ds(place * 16 + 8, 8), :] = y[:8]

    set_columns(4 * NK, dep[pl.ds(0, N), :])
    set_columns(4 * NK + 1, fr[...])

    def pack(ref, f, double):
        def step(k, _):
            block = pl.ds(pl.multiple_of(k * N, N), N)
            x = ref[block, :]
            if double:
                x = x + x
                ref[block, :] = x
            set_columns(f * NK + k, x)
            return 0

        lax.fori_loop(0, NK, step, 0, unroll=8)


    def wide(x):
        return jnp.broadcast_to(x, (NK, N))

    def column(f, entry):
        return cols[pl.ds(f * NK * 16 + 6 + entry, NK, stride=16), :]

    def plane_column(i, entry):
        return wide(cols[pl.ds((4 * NK + i) * 16 + 6 + entry, 1), :])

    def columns(entry):
        t_c, u_c, k_c, v_c = (column(f, entry) for f in range(4))
        return t_c, u_c, v_c, k_c, plane_column(0, entry)

    def row(ref, j):
        return ref[pl.ds(j, NK, stride=N), :]

    def edge_rows(j):
        return (
            row(t, j), row(u, j), row(v, j), row(kd, j), wide(dep[pl.ds(j, 1), :]),
        )

    def x_face(a, b):
        return face(level, jnp.minimum(a[4], b[4]), a[1], b[1], a[0], b[0], a[3], b[3])

    def y_face(a, b):
        return face(level, jnp.minimum(a[4], b[4]), a[2], b[2], a[0], b[0], a[3], b[3])

    def closed_step(mid, through, along):
        flow = jnp.where(last, 0.0, along(mid, tuple(east_of(x) for x in mid)))
        tc, _, _, kc, d = mid
        above = jnp.where(
            level + 1.0 < d,
            (kc + pltpu.roll(kc, NK - 1, 0)) * (pltpu.roll(tc, NK - 1, 0) - tc),
            0.0,
        )
        total = through + (west_of(flow) - flow) + (above - pltpu.roll(above, 1, 0))
        return jnp.where(level < d, tc + SCALE * total, 0.0)

    def stage(side, values, tracer):
        for f in range(4):
            send[side, pl.ds(f * NK, NK), :] = values[f]
        send[side, pl.ds(4 * NK, NK), :] = tracer
        send[side, pl.ds(5 * NK, 8), :] = values[4][:8]

    def stage_corners(slab, values):
        x = jnp.zeros((NK, N), jnp.float32)
        for f in range(5):
            x = jnp.where(lane == f, pltpu.roll(values[f], f, 1) if f else values[f], x)
            x = jnp.where(lane == 8 + f, pltpu.roll(values[f], 9 + f, 1), x)
        csend[slab] = x

    for f, ref in enumerate((t, u, kd)):
        loads[3 + f].wait()
        pack(ref, f, ref is kd)
    loads[6].wait()
    r_n, r_s = edge_rows(N - 1), edge_rows(0)
    stage(NORTH, r_n, closed_step(r_n, y_face(edge_rows(N - 2), r_n), x_face))
    stage(SOUTH, r_s, closed_step(r_s, -y_face(r_s, edge_rows(1)), x_face))
    stage_corners(0, r_n)
    stage_corners(1, r_s)

    def tracer(b, _):
        r = pl.multiple_of(b * 8, 8)
        rows = pl.ds(r, 8)
        d, de, dn = dep[rows, :], dep_e[rows, :], dep_n[rows, :]
        below = zero8
        press = zero8
        for k in range(NK):
            c = float(k)
            here, up_rows = pl.ds(r + k * N, 8), pl.ds(r + k * N + 1, 8)
            tc, kc, uc, vc = t[here, :], kd[here, :], u[here, :], v[here, :]
            next_u = east_of(uc)
            ue[here, :] = next_u
            f_e = face(c, de, uc, next_u, tc, east_of(tc), kc, east_of(kc))
            f_n = face(c, dn, vc, v[up_rows, :], tc, t[up_rows, :], kc, kd[up_rows, :])
            fa[pl.ds(r + k * PAD + 8, 8), :] = f_n
            f_s = fa[pl.ds(r + k * PAD + 7, 8), :]
            if k < NK - 1:
                t_up, k_up = t[pl.ds(r + (k + 1) * N, 8), :], kd[pl.ds(r + (k + 1) * N, 8), :]
                above = jnp.where(c + 1.0 < d, (kc + k_up) * (t_up - tc), 0.0)
            else:
                above = zero8
            total = (west_of(f_e) - f_e) + (f_s - f_n) + (above - below)
            below = above
            tc = jnp.where(c < d, tc + SCALE * total, 0.0)
            tn[here, :] = tc
            press = press + PG * tc
            p[pl.ds(r + k * PAD + 8, 8), :] = press
        return 0

    ahead = lax.rem(lon, n_lon // 2) < 3 * n_lon // 16

    @pl.when(ahead)
    def _():
        lax.fori_loop(0, N // 8, tracer, 0, unroll=2)

    pl.semaphore_wait(
        barrier,
        jnp.where(is_bottom, 5, 8) - own_e.astype(jnp.int32) - own_w.astype(jnp.int32),
    )

    def rim(side, slot, place):
        return pltpu.make_async_remote_copy(
            src_ref=send.at[side], dst_ref=recv.at[slot], send_sem=send_sem.at[side],
            recv_sem=recv_sem.at[slot], device_id=at(place), device_id_type=MESH,
        )

    def corner(slab, message, slot, place):
        return pltpu.make_async_remote_copy(
            src_ref=csend.at[slab], dst_ref=crecv.at[slot], send_sem=csend_sem.at[message],
            recv_sem=crecv_sem.at[slot], device_id=at(place), device_id_type=MESH,
        )

    to_north = rim(NORTH, jnp.where(is_top, NORTH, SOUTH), north)
    to_south = rim(SOUTH, NORTH, south)
    to_east, to_west = rim(EAST, WEST, east), rim(WEST, EAST, west)
    to_ne = corner(0, 0, jnp.where(is_top, NE, SW), north_e)
    to_nw = corner(0, 1, jnp.where(is_top, NW, SE), north_w)
    to_se, to_sw = corner(1, 2, NW, south_e), corner(1, 3, NE, south_w)

    to_north.start()

    @pl.when(not_own_e)
    def _():
        to_ne.start()

    @pl.when(not_own_w)
    def _():
        to_nw.start()

    @pl.when(not_bottom)
    def _():
        to_south.start()
        to_se.start()
        to_sw.start()

    pack(v, 3, False)
    c_e, c_w = columns(1), columns(2)
    stage(EAST, c_e, closed_step(c_e, x_face(columns(0), c_e), y_face))
    stage(WEST, c_w, closed_step(c_w, -x_face(c_w, columns(3)), y_face))
    to_east.start()
    to_west.start()

    @pl.when(jnp.logical_not(ahead))
    def _():
        lax.fori_loop(0, N // 8, tracer, 0, unroll=2)

    def momentum(b, _):
        r = pl.multiple_of(b * 8, 8)
        rows = pl.ds(r, 8)
        d, de, dn = dep[rows, :], dep_e[rows, :], dep_n[rows, :]
        f, f_next, co = fr[rows, :], fr_e[rows, :], cor[rows, :]
        for k in range(NK):
            c = float(k)
            here, up_rows = pl.ds(r + k * N, 8), pl.ds(r + k * N + 1, 8)
            mine, south_rows = pl.ds(r + k * PAD + 8, 8), pl.ds(r + k * PAD + 7, 8)
            uc, vc, pc = u[here, :], v[here, :], p[mine, :]
            wet_e, wet_n, wet = c < de, c < dn, c < d
            u_e = jnp.where(wet_e, ue[here, :] - uc, 0.0)
            v_e = jnp.where(wet_e, east_of(vc) - vc, 0.0)
            u_n = jnp.where(wet_n, u[up_rows, :] - uc, 0.0)
            v_n = jnp.where(wet_n, v[up_rows, :] - vc, 0.0)
            fa[mine, :] = u_n
            fb[mine, :] = v_n
            gain = east_of(pc) - pc
            across_x = (f * u_e - gain) - west_of(gain + f_next * u_e)
            lap_u = u_n - fa[south_rows, :]
            lap_v = (v_e - west_of(v_e)) + (v_n - fb[south_rows, :])
            dp_y = p[pl.ds(r + k * PAD + 9, 8), :] - p[south_rows, :]
            un[here, :] = jnp.where(wet, (uc + co * vc) + across_x + f * lap_u, 0.0)
            vn[here, :] = jnp.where(wet, (vc - co * uc) - dp_y + f * lap_v, 0.0)
        return 0

    lax.fori_loop(0, N // 8, momentum, 0)

    rim(NORTH, NORTH, north).wait_recv()
    rim(EAST, EAST, east).wait_recv()
    rim(WEST, WEST, west).wait_recv()

    @pl.when(not_own_e)
    def _():
        corner(0, 0, NE, north_e).wait_recv()

    @pl.when(not_own_w)
    def _():
        corner(0, 1, NW, north_w).wait_recv()

    @pl.when(own_e)
    def _():
        crecv[NE] = csend[0]

    @pl.when(own_w)
    def _():
        crecv[NW] = csend[0]

    @pl.when(not_bottom)
    def _():
        rim(SOUTH, SOUTH, south).wait_recv()
        corner(1, 2, SE, south_e).wait_recv()
        corner(1, 3, SW, south_w).wait_recv()

    @pl.when(is_top)
    def _():
        x = mirrored(recv[NORTH])
        r = lax.broadcasted_iota(jnp.int32, (MSG, N), 0)
        recv[NORTH] = jnp.where((r >= NK) & (r < 3 * NK), -x, x)
        x = pltpu.roll(crecv[NW], 8, 1)
        crecv[NW] = jnp.where((lane == 9) | (lane == 10), -x, x)
        x = pltpu.roll(crecv[NE], N - 8, 1)
        crecv[NE] = jnp.where((lane == 1) | (lane == 2), -x, x)

    def ghost(slot):
        parts = [recv[slot, pl.ds(f * NK, NK), :] for f in range(4)]
        return (*parts, wide(recv[slot, pl.ds(5 * NK, 1), :]))

    def beyond(slot, entry, to):
        x = crecv[slot]
        return tuple(pltpu.roll(x, (to - entry - f) % N, 1) for f in range(5))

    g_w, g_e, g_s, g_n = ghost(WEST), ghost(EAST), ghost(SOUTH), ghost(NORTH)
    f_w, f_e = x_face(g_w, c_w), x_face(c_e, g_e)
    f_s, f_n = y_face(g_s, r_s), y_face(r_n, g_n)

    def whole(slot, flow, low, high):
        ends = jnp.where(first, low, jnp.where(last, high, 0.0))
        return running_sum(PG * (recv[slot, pl.ds(4 * NK, NK), :] + SCALE * (flow + ends)))

    p_w = whole(WEST, -f_w, y_face(beyond(SW, 8, 0), g_w), -y_face(g_w, beyond(NW, 8, N - 1)))
    p_e = whole(EAST, f_e, y_face(beyond(SE, 0, 0), g_e), -y_face(g_e, beyond(NE, 0, N - 1)))
    p_s = whole(SOUTH, -f_s, x_face(beyond(SW, 8, 0), g_s), -x_face(g_s, beyond(SE, 0, N - 1)))
    p_n = whole(NORTH, f_n, x_face(beyond(NW, 8, 0), g_n), -x_face(g_n, beyond(NE, 0, N - 1)))
    t_w, t_e, t_s, t_n = SCALE * f_w, -SCALE * f_e, SCALE * f_s, -SCALE * f_n
    d_w, d_e, d_s, d_n = (running_sum(PG * x) for x in (t_w, t_e, t_s, t_n))
    q_w = running_sum(PG * send[WEST, pl.ds(4 * NK, NK), :])
    q_e = running_sum(PG * send[EAST, pl.ds(4 * NK, NK), :])

    def across(x):
        return jnp.where(first, 0.0, west_of(x)) - jnp.where(last, 0.0, east_of(x))

    def friction(mid, other, f, i):
        m = level < jnp.minimum(mid[4], other[4])
        return jnp.where(m, f * (other[i] - mid[i]), 0.0)

    def masked(depth, x):
        return jnp.where(level < depth, x, 0.0)

    col_e, col_w = plane_column(1, 1), plane_column(1, 2)
    row_s, row_n = wide(fr[pl.ds(0, 1), :]), wide(fr[pl.ds(N - 1, 1), :])
    def add(ref, j, x):
        rows = pl.ds(j, NK, stride=N)
        ref[rows, :] = ref[rows, :] + x

    add(tn, N - 1, t_n)
    add(tn, 0, t_s)
    add(un, N - 1, friction(r_n, g_n, row_n, 1) + masked(r_n[4], across(d_n)))
    add(un, 0, friction(r_s, g_s, row_s, 1) + masked(r_s[4], across(d_s)))
    add(vn, N - 1, friction(r_n, g_n, row_n, 2) - masked(r_n[4], p_n))
    add(vn, 0, friction(r_s, g_s, row_s, 2) + masked(r_s[4], p_s))
    add(vn, N - 2, -masked(wide(dep[pl.ds(N - 2, 1), :]), d_n))
    add(vn, 1, masked(wide(dep[pl.ds(1, 1), :]), d_s))
    fix[pl.ds(0, NK, stride=4), :] = -masked(plane_column(0, 0), d_e)
    fix[pl.ds(1, NK, stride=4), :] = friction(c_e, g_e, col_e, 1) - masked(c_e[4], p_e - q_w)
    fix[pl.ds(2, NK, stride=4), :] = friction(c_w, g_w, col_w, 1) + masked(c_w[4], p_w - q_e)
    fix[pl.ds(3, NK, stride=4), :] = masked(plane_column(0, 3), d_w)
    fix[pl.ds(64, NK, stride=2), :] = friction(c_e, g_e, col_e, 2) + masked(c_e[4], across(d_e))
    fix[pl.ds(65, NK, stride=2), :] = friction(c_w, g_w, col_w, 2) + masked(c_w[4], across(d_w))
    fix[pl.ds(96, NK, stride=2), :] = t_e
    fix[pl.ds(97, NK, stride=2), :] = t_w
    fix_out[...] = fix[...].T

    to_north.wait_send()
    to_east.wait_send()
    to_west.wait_send()

    @pl.when(not_own_e)
    def _():
        to_ne.wait_send()

    @pl.when(not_own_w)
    def _():
        to_nw.wait_send()

    @pl.when(not_bottom)
    def _():
        to_south.wait_send()
        to_se.wait_send()
        to_sw.wait_send()


def finish(tn, un, vn, fix, t_out, u_out, v_out, t, u, v, out_sem):
    lane8 = lax.broadcasted_iota(jnp.int32, (8, N), 1)
    rim2 = (lane8 == 0) | (lane8 == N - 1)
    rim4 = (lane8 <= 1) | (lane8 >= N - 2)

    outs = ((t, t_out), (u, u_out), (v, v_out))

    def step(g, _):
        for k in range(CHUNK):
            start = pl.multiple_of((g * CHUNK + k) * N, N)
            for r in range(0, N, 8):
                here = pl.ds(start + r, 8)
                x = fix[pl.ds(r, 8), :]
                for new, old, rim, shift in (
                    (u, un, rim4, N - 2 - 4 * k), (v, vn, rim2, 63 - 2 * k), (t, tn, rim2, 31 - 2 * k),
                ):
                    shift = lax.rem(shift + N - g * CHUNK * (4 if rim is rim4 else 2), N)
                    new[here, :] = old[here, :] + jnp.where(rim, pltpu.roll(x, shift, 1), 0.0)
        block = pl.ds(pl.multiple_of(g * CHUNK * N, N), CHUNK * N)
        for i, (src, dst) in enumerate(outs):
            pltpu.make_async_copy(src.at[block], dst.at[block], out_sem.at[i]).start()
        return 0

    lax.fori_loop(0, NK // CHUNK, step, 0)
    for i, (src, dst) in enumerate(outs):
        pltpu.make_async_copy(src, dst, out_sem.at[i]).wait()


def solution(mesh):
    n_lon, n_lat = mesh.shape["lon"], mesh.shape["lat"]
    f32, i32 = jnp.float32, jnp.int32

    def on_device(t, u, v, kd, fr, ind, strata):
        flat = [x.reshape(FLAT, N) for x in (t, u, v, kd)]
        outs = pl.pallas_call(
            functools.partial(kernel, n_lon, n_lat),
            out_shape=[*[pltpu.VMEM((FLAT, N), f32)] * 3, pltpu.VMEM((N, N), f32)],
            in_specs=[pl.BlockSpec(memory_space=pltpu.HBM)] * 7,
            out_specs=[pl.BlockSpec(memory_space=pltpu.VMEM)] * 4,
            scratch_shapes=[
                *[pltpu.VMEM((FLAT + 8, N), f32)] * 4,
                *[pltpu.VMEM((NK * PAD + 8, N), f32)] * 3,
                pltpu.VMEM((N, N), f32),
                pltpu.VMEM((N, N), i32),
                pltpu.VMEM((N, N), i32),
                pltpu.VMEM((N + 8, N), f32),
                *[pltpu.VMEM((N, N), f32)] * 4,
                pltpu.VMEM((FLAT, N), f32),
                pltpu.VMEM(((4 * NK + 2) * 16, N), f32),
                pltpu.VMEM((N, N), f32),
                pltpu.VMEM((4, MSG, N), f32),
                pltpu.VMEM((4, MSG, N), f32),
                pltpu.VMEM((4, NK, N), f32),
                pltpu.VMEM((4, NK, N), f32),
                pltpu.SemaphoreType.DMA((7,)),
                *[pltpu.SemaphoreType.DMA((4,))] * 4,
            ],
            compiler_params=pltpu.CompilerParams(
                collective_id=0, has_side_effects=True, vmem_limit_bytes=60 * 1024 * 1024
            ),
            cost_estimate=pl.CostEstimate(
                flops=80 * FLAT * N, bytes_accessed=30 * FLAT * N, transcendentals=0
            ),
        )(*flat, fr, ind, strata)
        outs = pl.pallas_call(
            finish,
            out_shape=[jax.ShapeDtypeStruct((FLAT, N), f32)] * 3,
            in_specs=[pl.BlockSpec(memory_space=pltpu.VMEM)] * 4,
            out_specs=[pl.BlockSpec(memory_space=pltpu.HBM)] * 3,
            scratch_shapes=[
                *[pltpu.VMEM((FLAT, N), f32)] * 3,
                pltpu.SemaphoreType.DMA((3,)),
            ],
            compiler_params=pltpu.CompilerParams(vmem_limit_bytes=32 * 1024 * 1024),
        )(*outs)
        return tuple(x.reshape(NK, N, N) for x in outs)

    plane, field = P("lat", "lon"), P(None, "lat", "lon")
    return jax.shard_map(
        on_device,
        mesh=mesh,
        in_specs=(field, field, field, field, plane, plane, plane),
        out_specs=(field, field, field),
        check_vma=False,
    )
```

```python
import functools
import math

import jax
import jax.numpy as jnp
from jax import lax
from jax.experimental import pallas as pl
from jax.experimental.pallas import tpu as pltpu
from jax.sharding import PartitionSpec as P

MESH = pl.DeviceIdType.MESH
NK = 16
N = 128
FLAT = NK * N
PAD = N + 8
SCALE = 1.0 / 16.0
PG = 0.25 * 0.05
WEST, EAST, SOUTH, NORTH = 0, 1, 2, 3
SW, SE, NW, NE = 0, 1, 2, 3
MSG = 5 * NK
CHUNK = 4


def east_of(x):
    return pltpu.roll(x, N - 1, 1)


def west_of(x):
    return pltpu.roll(x, 1, 1)


def face(c, d, a, b, ta, tb, ka, kb):
    return jnp.where(c < d, (a + b) * (ta + tb) - (ka + kb) * (tb - ta), 0.0)


def mirrored(x):
    lane = lax.broadcasted_iota(jnp.int32, x.shape, 1)
    return jnp.take_along_axis(x, N - 1 - lane, axis=1)


def running_sum(x):
    level = lax.broadcasted_iota(jnp.int32, x.shape, 0)
    for step in (1, 2, 4, 8):
        x = x + jnp.where(level >= step, pltpu.roll(x, step, 0), 0.0)
    return x


def kernel(
    n_lon, n_lat,
    t_hbm, u_hbm, v_hbm, k_hbm, t_rows, u_rows, v_rows, k_rows, fr_hbm, ind_hbm, str_hbm,
    tn, un, vn, fix_out,
    t, u, v, kd, p, fa, fb, fr, ind, strata, dep, dep_e, dep_n, cor, fr_e,
    ue, slabs, cols, fix, send, recv, csend, crecv,
    in_sem, send_sem, recv_sem, csend_sem, crecv_sem,
):
    lon, lat = lax.axis_index("lon"), lax.axis_index("lat")
    is_top, is_bottom = lat == n_lat - 1, lat == 0
    not_bottom = jnp.logical_not(is_bottom)
    lon_e, lon_w = lax.rem(lon + 1, n_lon), lax.rem(lon + n_lon - 1, n_lon)
    lat_n, lat_s = jnp.where(is_top, lat, lat + 1), jnp.where(is_bottom, lat, lat - 1)
    east, west = (lat, lon_e), (lat, lon_w)
    north, south = (lat_n, jnp.where(is_top, n_lon - 1 - lon, lon)), (lat_s, lon)
    fold_e, fold_w = lax.rem(2 * n_lon - 2 - lon, n_lon), lax.rem(n_lon - lon, n_lon)
    own_e = is_top & (fold_e == lon)
    own_w = is_top & (fold_w == lon)
    not_own_e, not_own_w = jnp.logical_not(own_e), jnp.logical_not(own_w)
    north_e = (lat_n, jnp.where(is_top, fold_e, lon_e))
    north_w = (lat_n, jnp.where(is_top, fold_w, lon_w))
    south_e, south_w = (lat_s, lon_e), (lat_s, lon_w)

    def at(place):
        return {"lat": place[0], "lon": place[1]}

    loads = [
        pltpu.make_async_copy(src, dst, in_sem.at[i])
        for i, (src, dst) in enumerate(
            (
                (ind_hbm, ind), (str_hbm, strata), (fr_hbm, fr),
                *(
                    (ref.at[:, pl.ds(side * (N - 8), 8), :], slabs.at[2 * f + side])
                    for f, ref in enumerate((t_rows, u_rows, v_rows, k_rows))
                    for side in (0, 1)
                ),
                (t_hbm, t.at[pl.ds(0, FLAT)]), (u_hbm, u.at[pl.ds(0, FLAT)]),
                (k_hbm, kd.at[pl.ds(0, FLAT)]), (v_hbm, v.at[pl.ds(0, FLAT)]),
            )
        )
    ]
    for load in loads:
        load.start()
    barrier = pltpu.get_barrier_semaphore()

    def greet(place):
        pl.semaphore_signal(barrier, inc=1, device_id=at(place), device_id_type=MESH)

    for place in (west, east, north):
        greet(place)

    @pl.when(not_own_e)
    def _():
        greet(north_e)

    @pl.when(not_own_w)
    def _():
        greet(north_w)

    @pl.when(not_bottom)
    def _():
        for place in (south, south_e, south_w):
            greet(place)

    lane8 = lax.broadcasted_iota(jnp.int32, (8, N), 1)
    zero8 = jnp.zeros((8, N), jnp.float32)
    lane = lax.broadcasted_iota(jnp.int32, (NK, N), 1)
    level = lax.broadcasted_iota(jnp.int32, (NK, N), 0).astype(jnp.float32)
    first, last = lane == 0, lane == N - 1

    for k in range(NK + 1):
        p[pl.ds(k * PAD, 8), :] = zero8
        fa[pl.ds(k * PAD, 8), :] = zero8
        fb[pl.ds(k * PAD, 8), :] = zero8

    @pl.when(is_bottom)
    def _():
        recv[SOUTH] = jnp.zeros((MSG, N), jnp.float32)
        crecv[SW] = zero8
        crecv[SE] = zero8

    def set_cor(b, _):
        rows = pl.ds(pl.multiple_of(b * 8, 8), 8)
        j = lax.broadcasted_iota(jnp.int32, (8, N), 0) + (b * 8 + lat * N)
        cor[rows, :] = 0.25 * jnp.sin(
            jnp.pi * ((j.astype(jnp.float32) + 0.5) / (N * n_lat) - 0.5)
        )
        return 0

    lax.fori_loop(0, N // 8, set_cor, 0)

    for load in loads[:3]:
        load.wait()
    dep[pl.ds(N, 8), :] = zero8
    dep[pl.ds(0, N), :] = (ind[...] * strata[...]).astype(jnp.float32)
    fr[...] = fr[...] * 0.25

    def set_depth(b, _):
        r = pl.multiple_of(b * 8, 8)
        rows = pl.ds(r, 8)
        d = dep[rows, :]
        dep_e[rows, :] = jnp.where(lane8 == N - 1, 0.0, jnp.minimum(d, east_of(d)))
        dep_n[rows, :] = jnp.minimum(d, dep[pl.ds(r + 1, 8), :])
        fr_e[rows, :] = east_of(fr[rows, :])
        return 0

    lax.fori_loop(0, N // 8, set_depth, 0, unroll=True)

    def set_columns(place, x):
        y = x.T
        cols[pl.ds(place * 16, 8), :] = y[N - 8 :]
        cols[pl.ds(place * 16 + 8, 8), :] = y[:8]

    set_columns(4 * NK, dep[pl.ds(0, N), :])
    set_columns(4 * NK + 1, fr[...])

    def pack(ref, f, double):
        def step(k, _):
            block = pl.ds(pl.multiple_of(k * N, N), N)
            x = ref[block, :]
            if double:
                x = x + x
                ref[block, :] = x
            set_columns(f * NK + k, x)
            return 0

        lax.fori_loop(0, NK, step, 0, unroll=8)


    def wide(x):
        return jnp.broadcast_to(x, (NK, N))

    def column(f, entry):
        return cols[pl.ds(f * NK * 16 + 6 + entry, NK, stride=16), :]

    def plane_column(i, entry):
        return wide(cols[pl.ds((4 * NK + i) * 16 + 6 + entry, 1), :])

    def columns(entry):
        t_c, u_c, k_c, v_c = (column(f, entry) for f in range(4))
        return t_c, u_c, v_c, k_c, plane_column(0, entry)

    slab_rows = slabs.reshape(8 * NK * 8, N)

    def edge_rows(j):
        side = 0 if j < 8 else 1
        t_r, u_r, v_r, k_r = (
            slab_rows[pl.ds((2 * f + side) * NK * 8 + j % 8, NK, stride=8), :] for f in range(4)
        )
        return t_r, u_r, v_r, k_r + k_r, wide(dep[pl.ds(j, 1), :])

    def x_face(a, b):
        return face(level, jnp.minimum(a[4], b[4]), a[1], b[1], a[0], b[0], a[3], b[3])

    def y_face(a, b):
        return face(level, jnp.minimum(a[4], b[4]), a[2], b[2], a[0], b[0], a[3], b[3])

    def closed_step(mid, through, along):
        flow = jnp.where(last, 0.0, along(mid, tuple(east_of(x) for x in mid)))
        tc, _, _, kc, d = mid
        above = jnp.where(
            level + 1.0 < d,
            (kc + pltpu.roll(kc, NK - 1, 0)) * (pltpu.roll(tc, NK - 1, 0) - tc),
            0.0,
        )
        total = through + (west_of(flow) - flow) + (above - pltpu.roll(above, 1, 0))
        return jnp.where(level < d, tc + SCALE * total, 0.0)

    def marked(values):
        return (*values[:3], jnp.where(level < values[4], values[3], 0.0))

    def stage(side, values, tracer):
        for f, x in enumerate((*marked(values), tracer)):
            send[side, pl.ds(f * NK, NK), :] = x

    def stage_corners(slab, values):
        x = zero8
        for f, y in enumerate(marked(values)):
            for half in (0, 1):
                z, to = y[8 * half : 8 * half + 8], f + 16 * half
                x = jnp.where(lane8 == to, pltpu.roll(z, to, 1) if to else z, x)
                x = jnp.where(lane8 == 8 + to, pltpu.roll(z, 9 + to, 1), x)
        csend[slab] = x

    for load in loads[3:11]:
        load.wait()
    r_n, r_s = edge_rows(N - 1), edge_rows(0)
    stage(NORTH, r_n, closed_step(r_n, y_face(edge_rows(N - 2), r_n), x_face))
    stage(SOUTH, r_s, closed_step(r_s, -y_face(r_s, edge_rows(1)), x_face))
    stage_corners(0, r_n)
    stage_corners(1, r_s)

    def tracer(b, _):
        r = pl.multiple_of(b * 8, 8)
        rows = pl.ds(r, 8)
        d, de, dn = dep[rows, :], dep_e[rows, :], dep_n[rows, :]
        below = zero8
        press = zero8
        for k in range(NK):
            c = float(k)
            here, up_rows = pl.ds(r + k * N, 8), pl.ds(r + k * N + 1, 8)
            tc, kc, uc, vc = t[here, :], kd[here, :], u[here, :], v[here, :]
            next_u = east_of(uc)
            ue[here, :] = next_u
            f_e = face(c, de, uc, next_u, tc, east_of(tc), kc, east_of(kc))
            f_n = face(c, dn, vc, v[up_rows, :], tc, t[up_rows, :], kc, kd[up_rows, :])
            fa[pl.ds(r + k * PAD + 8, 8), :] = f_n
            f_s = fa[pl.ds(r + k * PAD + 7, 8), :]
            if k < NK - 1:
                t_up, k_up = t[pl.ds(r + (k + 1) * N, 8), :], kd[pl.ds(r + (k + 1) * N, 8), :]
                above = jnp.where(c + 1.0 < d, (kc + k_up) * (t_up - tc), 0.0)
            else:
                above = zero8
            total = (west_of(f_e) - f_e) + (f_s - f_n) + (above - below)
            below = above
            tc = jnp.where(c < d, tc + SCALE * total, 0.0)
            tn[here, :] = tc
            press = press + PG * tc
            p[pl.ds(r + k * PAD + 8, 8), :] = press
        return 0

    ahead = lax.rem(lon, n_lon // 2) < 3 * n_lon // 16

    def pack_fields():
        for f, ref in enumerate((t, u, kd, v)):
            loads[11 + f].wait()
            pack(ref, f, ref is kd)

    @pl.when(ahead)
    def _():
        pack_fields()
        lax.fori_loop(0, N // 8, tracer, 0, unroll=2)

    pl.semaphore_wait(
        barrier,
        jnp.where(is_bottom, 5, 8) - own_e.astype(jnp.int32) - own_w.astype(jnp.int32),
    )

    def rim(side, slot, place):
        return pltpu.make_async_remote_copy(
            src_ref=send.at[side], dst_ref=recv.at[slot], send_sem=send_sem.at[side],
            recv_sem=recv_sem.at[slot], device_id=at(place), device_id_type=MESH,
        )

    def corner(slab, message, slot, place):
        return pltpu.make_async_remote_copy(
            src_ref=csend.at[slab], dst_ref=crecv.at[slot], send_sem=csend_sem.at[message],
            recv_sem=crecv_sem.at[slot], device_id=at(place), device_id_type=MESH,
        )

    to_north = rim(NORTH, jnp.where(is_top, NORTH, SOUTH), north)
    to_south = rim(SOUTH, NORTH, south)
    to_east, to_west = rim(EAST, WEST, east), rim(WEST, EAST, west)
    to_ne = corner(0, 0, jnp.where(is_top, NE, SW), north_e)
    to_nw = corner(0, 1, jnp.where(is_top, NW, SE), north_w)
    to_se, to_sw = corner(1, 2, NW, south_e), corner(1, 3, NE, south_w)

    to_north.start()

    @pl.when(not_own_e)
    def _():
        to_ne.start()

    @pl.when(not_own_w)
    def _():
        to_nw.start()

    @pl.when(not_bottom)
    def _():
        to_south.start()
        to_se.start()
        to_sw.start()

    @pl.when(jnp.logical_not(ahead))
    def _():
        pack_fields()

    c_e, c_w = columns(1), columns(2)
    stage(EAST, c_e, closed_step(c_e, x_face(columns(0), c_e), y_face))
    stage(WEST, c_w, closed_step(c_w, -x_face(c_w, columns(3)), y_face))
    to_east.start()
    to_west.start()

    @pl.when(jnp.logical_not(ahead))
    def _():
        lax.fori_loop(0, N // 8, tracer, 0, unroll=2)

    def momentum(b, _):
        r = pl.multiple_of(b * 8, 8)
        rows = pl.ds(r, 8)
        d, de, dn = dep[rows, :], dep_e[rows, :], dep_n[rows, :]
        f, f_next, co = fr[rows, :], fr_e[rows, :], cor[rows, :]
        for k in range(NK):
            c = float(k)
            here, up_rows = pl.ds(r + k * N, 8), pl.ds(r + k * N + 1, 8)
            mine, south_rows = pl.ds(r + k * PAD + 8, 8), pl.ds(r + k * PAD + 7, 8)
            uc, vc, pc = u[here, :], v[here, :], p[mine, :]
            wet_e, wet_n, wet = c < de, c < dn, c < d
            u_e = jnp.where(wet_e, ue[here, :] - uc, 0.0)
            v_e = jnp.where(wet_e, east_of(vc) - vc, 0.0)
            u_n = jnp.where(wet_n, u[up_rows, :] - uc, 0.0)
            v_n = jnp.where(wet_n, v[up_rows, :] - vc, 0.0)
            fa[mine, :] = u_n
            fb[mine, :] = v_n
            gain = east_of(pc) - pc
            across_x = (f * u_e - gain) - west_of(gain + f_next * u_e)
            lap_u = u_n - fa[south_rows, :]
            lap_v = (v_e - west_of(v_e)) + (v_n - fb[south_rows, :])
            dp_y = p[pl.ds(r + k * PAD + 9, 8), :] - p[south_rows, :]
            un[here, :] = jnp.where(wet, (uc + co * vc) + across_x + f * lap_u, 0.0)
            vn[here, :] = jnp.where(wet, (vc - co * uc) - dp_y + f * lap_v, 0.0)
        return 0

    lax.fori_loop(0, N // 8, momentum, 0)

    rim(NORTH, NORTH, north).wait_recv()
    rim(EAST, EAST, east).wait_recv()
    rim(WEST, WEST, west).wait_recv()

    @pl.when(not_own_e)
    def _():
        corner(0, 0, NE, north_e).wait_recv()

    @pl.when(not_own_w)
    def _():
        corner(0, 1, NW, north_w).wait_recv()

    @pl.when(own_e)
    def _():
        crecv[NE] = csend[0]

    @pl.when(own_w)
    def _():
        crecv[NW] = csend[0]

    @pl.when(not_bottom)
    def _():
        rim(SOUTH, SOUTH, south).wait_recv()
        corner(1, 2, SE, south_e).wait_recv()
        corner(1, 3, SW, south_w).wait_recv()

    @pl.when(is_top)
    def _():
        x = mirrored(recv[NORTH])
        r = lax.broadcasted_iota(jnp.int32, (MSG, N), 0)
        recv[NORTH] = jnp.where((r >= NK) & (r < 3 * NK), -x, x)
        turned = ((lane8 & 7) == 1) | ((lane8 & 7) == 2)
        x = crecv[NW]
        x = pltpu.roll(jnp.where(turned, -x, x), 8, 1)
        crecv[NW] = x
        x = crecv[NE]
        crecv[NE] = pltpu.roll(jnp.where(turned, -x, x), N - 8, 1)

    def with_depth(t_g, u_g, v_g, k_g):
        return t_g, u_g, v_g, k_g, jnp.where(k_g > 0.0, float(NK), 0.0)

    def ghost(slot):
        return with_depth(*(recv[slot, pl.ds(f * NK, NK), :] for f in range(4)))

    def beyond(slot, entry, to):
        x = crecv[slot]

        def value(f):
            shift = to - entry - f + N
            return jnp.concatenate(
                [pltpu.roll(x, shift % N, 1), pltpu.roll(x, (shift - 16) % N, 1)], 0
            )

        return with_depth(*(value(f) for f in range(4)))

    g_w, g_e, g_s, g_n = ghost(WEST), ghost(EAST), ghost(SOUTH), ghost(NORTH)
    f_w, f_e = x_face(g_w, c_w), x_face(c_e, g_e)
    f_s, f_n = y_face(g_s, r_s), y_face(r_n, g_n)

    def whole(slot, flow, low, high):
        ends = jnp.where(first, low, jnp.where(last, high, 0.0))
        return running_sum(PG * (recv[slot, pl.ds(4 * NK, NK), :] + SCALE * (flow + ends)))

    p_w = whole(WEST, -f_w, y_face(beyond(SW, 8, 0), g_w), -y_face(g_w, beyond(NW, 8, N - 1)))
    p_e = whole(EAST, f_e, y_face(beyond(SE, 0, 0), g_e), -y_face(g_e, beyond(NE, 0, N - 1)))
    p_s = whole(SOUTH, -f_s, x_face(beyond(SW, 8, 0), g_s), -x_face(g_s, beyond(SE, 0, N - 1)))
    p_n = whole(NORTH, f_n, x_face(beyond(NW, 8, 0), g_n), -x_face(g_n, beyond(NE, 0, N - 1)))
    t_w, t_e, t_s, t_n = SCALE * f_w, -SCALE * f_e, SCALE * f_s, -SCALE * f_n
    d_w, d_e, d_s, d_n = (running_sum(PG * x) for x in (t_w, t_e, t_s, t_n))
    q_w = running_sum(PG * send[WEST, pl.ds(4 * NK, NK), :])
    q_e = running_sum(PG * send[EAST, pl.ds(4 * NK, NK), :])

    def across(x):
        return jnp.where(first, 0.0, west_of(x)) - jnp.where(last, 0.0, east_of(x))

    def friction(mid, other, f, i):
        m = level < jnp.minimum(mid[4], other[4])
        return jnp.where(m, f * (other[i] - mid[i]), 0.0)

    def masked(depth, x):
        return jnp.where(level < depth, x, 0.0)

    col_e, col_w = plane_column(1, 1), plane_column(1, 2)
    row_s, row_n = wide(fr[pl.ds(0, 1), :]), wide(fr[pl.ds(N - 1, 1), :])
    def add(ref, j, x):
        rows = pl.ds(j, NK, stride=N)
        ref[rows, :] = ref[rows, :] + x

    add(tn, N - 1, t_n)
    add(tn, 0, t_s)
    add(un, N - 1, friction(r_n, g_n, row_n, 1) + masked(r_n[4], across(d_n)))
    add(un, 0, friction(r_s, g_s, row_s, 1) + masked(r_s[4], across(d_s)))
    add(vn, N - 1, friction(r_n, g_n, row_n, 2) - masked(r_n[4], p_n))
    add(vn, 0, friction(r_s, g_s, row_s, 2) + masked(r_s[4], p_s))
    add(vn, N - 2, -masked(wide(dep[pl.ds(N - 2, 1), :]), d_n))
    add(vn, 1, masked(wide(dep[pl.ds(1, 1), :]), d_s))
    fix[pl.ds(0, NK, stride=4), :] = -masked(plane_column(0, 0), d_e)
    fix[pl.ds(1, NK, stride=4), :] = friction(c_e, g_e, col_e, 1) - masked(c_e[4], p_e - q_w)
    fix[pl.ds(2, NK, stride=4), :] = friction(c_w, g_w, col_w, 1) + masked(c_w[4], p_w - q_e)
    fix[pl.ds(3, NK, stride=4), :] = masked(plane_column(0, 3), d_w)
    fix[pl.ds(64, NK, stride=2), :] = friction(c_e, g_e, col_e, 2) + masked(c_e[4], across(d_e))
    fix[pl.ds(65, NK, stride=2), :] = friction(c_w, g_w, col_w, 2) + masked(c_w[4], across(d_w))
    fix[pl.ds(96, NK, stride=2), :] = t_e
    fix[pl.ds(97, NK, stride=2), :] = t_w
    fix_out[...] = fix[...].T

    to_north.wait_send()
    to_east.wait_send()
    to_west.wait_send()

    @pl.when(not_own_e)
    def _():
        to_ne.wait_send()

    @pl.when(not_own_w)
    def _():
        to_nw.wait_send()

    @pl.when(not_bottom)
    def _():
        to_south.wait_send()
        to_se.wait_send()
        to_sw.wait_send()


def finish(tn, un, vn, fix, t_out, u_out, v_out, t, u, v, out_sem):
    lane8 = lax.broadcasted_iota(jnp.int32, (8, N), 1)
    rim2 = (lane8 == 0) | (lane8 == N - 1)
    rim4 = (lane8 <= 1) | (lane8 >= N - 2)

    outs = ((t, t_out), (u, u_out), (v, v_out))

    def step(g, _):
        for k in range(CHUNK):
            start = pl.multiple_of((g * CHUNK + k) * N, N)
            for r in range(0, N, 8):
                here = pl.ds(start + r, 8)
                x = fix[pl.ds(r, 8), :]
                for new, old, rim, shift in (
                    (u, un, rim4, N - 2 - 4 * k), (v, vn, rim2, 63 - 2 * k), (t, tn, rim2, 31 - 2 * k),
                ):
                    shift = lax.rem(shift + N - g * CHUNK * (4 if rim is rim4 else 2), N)
                    new[here, :] = old[here, :] + jnp.where(rim, pltpu.roll(x, shift, 1), 0.0)
        block = pl.ds(pl.multiple_of(g * CHUNK * N, N), CHUNK * N)
        for i, (src, dst) in enumerate(outs):
            pltpu.make_async_copy(src.at[block], dst.at[block], out_sem.at[i]).start()
        return 0

    lax.fori_loop(0, NK // CHUNK, step, 0)
    for i, (src, dst) in enumerate(outs):
        pltpu.make_async_copy(src, dst, out_sem.at[i]).wait()


def solution(mesh):
    n_lon, n_lat = mesh.shape["lon"], mesh.shape["lat"]
    f32, i32 = jnp.float32, jnp.int32

    def on_device(t, u, v, kd, fr, ind, strata):
        flat = [x.reshape(FLAT, N) for x in (t, u, v, kd)]
        outs = pl.pallas_call(
            functools.partial(kernel, n_lon, n_lat),
            out_shape=[*[pltpu.VMEM((FLAT, N), f32)] * 3, pltpu.VMEM((N, N), f32)],
            in_specs=[pl.BlockSpec(memory_space=pltpu.HBM)] * 11,
            out_specs=[pl.BlockSpec(memory_space=pltpu.VMEM)] * 4,
            scratch_shapes=[
                *[pltpu.VMEM((FLAT + 8, N), f32)] * 4,
                *[pltpu.VMEM((NK * PAD + 8, N), f32)] * 3,
                pltpu.VMEM((N, N), f32),
                pltpu.VMEM((N, N), i32),
                pltpu.VMEM((N, N), i32),
                pltpu.VMEM((N + 8, N), f32),
                *[pltpu.VMEM((N, N), f32)] * 4,
                pltpu.VMEM((FLAT, N), f32),
                pltpu.VMEM((8, NK, 8, N), f32),
                pltpu.VMEM(((4 * NK + 2) * 16, N), f32),
                pltpu.VMEM((N, N), f32),
                pltpu.VMEM((4, MSG, N), f32),
                pltpu.VMEM((4, MSG, N), f32),
                pltpu.VMEM((2, 8, N), f32),
                pltpu.VMEM((4, 8, N), f32),
                pltpu.SemaphoreType.DMA((15,)),
                *[pltpu.SemaphoreType.DMA((4,))] * 4,
            ],
            compiler_params=pltpu.CompilerParams(
                collective_id=0, has_side_effects=True, vmem_limit_bytes=60 * 1024 * 1024
            ),
            cost_estimate=pl.CostEstimate(
                flops=80 * FLAT * N, bytes_accessed=30 * FLAT * N, transcendentals=0
            ),
        )(*flat, t, u, v, kd, fr, ind, strata)
        outs = pl.pallas_call(
            finish,
            out_shape=[jax.ShapeDtypeStruct((FLAT, N), f32)] * 3,
            in_specs=[pl.BlockSpec(memory_space=pltpu.VMEM)] * 4,
            out_specs=[pl.BlockSpec(memory_space=pltpu.HBM)] * 3,
            scratch_shapes=[
                *[pltpu.VMEM((FLAT, N), f32)] * 3,
                pltpu.SemaphoreType.DMA((3,)),
            ],
            compiler_params=pltpu.CompilerParams(vmem_limit_bytes=32 * 1024 * 1024),
        )(*outs)
        return tuple(x.reshape(NK, N, N) for x in outs)

    plane, field = P("lat", "lon"), P(None, "lat", "lon")
    return jax.shard_map(
        on_device,
        mesh=mesh,
        in_specs=(field, field, field, field, plane, plane, plane),
        out_specs=(field, field, field),
        check_vma=False,
    )
```

```python
import functools
import math

import jax
import jax.numpy as jnp
from jax import lax
from jax.experimental import pallas as pl
from jax.experimental.pallas import tpu as pltpu
from jax.sharding import PartitionSpec as P

MESH = pl.DeviceIdType.MESH
NK = 16
N = 128
FLAT = NK * N
PAD = N + 8
SCALE = 1.0 / 16.0
PG = 0.25 * 0.05
WEST, EAST, SOUTH, NORTH = 0, 1, 2, 3
SW, SE, NW, NE = 0, 1, 2, 3
MSG = 5 * NK
CHUNK = 4


def east_of(x):
    return pltpu.roll(x, N - 1, 1)


def west_of(x):
    return pltpu.roll(x, 1, 1)


def face(c, d, a, b, ta, tb, ka, kb):
    return jnp.where(c < d, (a + b) * (ta + tb) - (ka + kb) * (tb - ta), 0.0)


def mirrored(x):
    lane = lax.broadcasted_iota(jnp.int32, x.shape, 1)
    return jnp.take_along_axis(x, N - 1 - lane, axis=1)


def running_sum(x):
    level = lax.broadcasted_iota(jnp.int32, x.shape, 0)
    for step in (1, 2, 4, 8):
        x = x + jnp.where(level >= step, pltpu.roll(x, step, 0), 0.0)
    return x


def kernel(
    n_lon, n_lat,
    t_hbm, u_hbm, v_hbm, k_hbm, t_rows, u_rows, v_rows, k_rows, fr_hbm, ind_hbm, str_hbm,
    tn, un, vn, fix_out,
    t, u, v, kd, p, fa, fb, fr, ind, strata, dep, dep_e, dep_n, cor, fr_e,
    ue, slabs, cols, fix, send, recv, csend, crecv,
    in_sem, send_sem, recv_sem, csend_sem, crecv_sem, ready,
):
    lon, lat = lax.axis_index("lon"), lax.axis_index("lat")
    is_top, is_bottom = lat == n_lat - 1, lat == 0
    not_bottom = jnp.logical_not(is_bottom)
    lon_e, lon_w = lax.rem(lon + 1, n_lon), lax.rem(lon + n_lon - 1, n_lon)
    lat_n, lat_s = jnp.where(is_top, lat, lat + 1), jnp.where(is_bottom, lat, lat - 1)
    east, west = (lat, lon_e), (lat, lon_w)
    north, south = (lat_n, jnp.where(is_top, n_lon - 1 - lon, lon)), (lat_s, lon)
    fold_e, fold_w = lax.rem(2 * n_lon - 2 - lon, n_lon), lax.rem(n_lon - lon, n_lon)
    own_e = is_top & (fold_e == lon)
    own_w = is_top & (fold_w == lon)
    not_own_e, not_own_w = jnp.logical_not(own_e), jnp.logical_not(own_w)
    north_e = (lat_n, jnp.where(is_top, fold_e, lon_e))
    north_w = (lat_n, jnp.where(is_top, fold_w, lon_w))
    south_e, south_w = (lat_s, lon_e), (lat_s, lon_w)

    def at(place):
        return {"lat": place[0], "lon": place[1]}

    loads = [
        pltpu.make_async_copy(src, dst, in_sem.at[i])
        for i, (src, dst) in enumerate(
            (
                (ind_hbm, ind), (str_hbm, strata), (fr_hbm, fr),
                *(
                    (ref.at[:, pl.ds(side * (N - 8), 8), :], slabs.at[2 * f + side])
                    for f, ref in enumerate((t_rows, u_rows, v_rows, k_rows))
                    for side in (0, 1)
                ),
                (t_hbm, t.at[pl.ds(0, FLAT)]), (u_hbm, u.at[pl.ds(0, FLAT)]),
                (k_hbm, kd.at[pl.ds(0, FLAT)]), (v_hbm, v.at[pl.ds(0, FLAT)]),
            )
        )
    ]
    for load in loads:
        load.start()
    barrier = pltpu.get_barrier_semaphore()

    def is_early(place):
        return lax.rem(place[1], n_lon // 2) < n_lon // 4

    early = is_early((lat, lon))
    always = lat >= 0
    peers = (
        (east, always, 1),
        (west, always, 0),
        (north, always, jnp.where(is_top, 2, 3)),
        (south, not_bottom, 2),
        (north_e, not_own_e, jnp.where(is_top, 4, 7)),
        (north_w, not_own_w, jnp.where(is_top, 5, 6)),
        (south_e, not_bottom, 5),
        (south_w, not_bottom, 4),
    )
    to_late = [ok & early & jnp.logical_not(is_early(place)) for place, ok, _ in peers]
    to_early = [ok & jnp.logical_not(early) & is_early(place) for place, ok, _ in peers]
    expected = jnp.int32(0)
    for (place, ok, _), ahead, behind in zip(peers, to_early, to_late):

        @pl.when(ok & jnp.logical_not(ahead))
        def _(place=place):
            pl.semaphore_signal(barrier, inc=1, device_id=at(place), device_id_type=MESH)

        expected = expected + (ok & jnp.logical_not(behind)).astype(jnp.int32)

    lane8 = lax.broadcasted_iota(jnp.int32, (8, N), 1)
    zero8 = jnp.zeros((8, N), jnp.float32)
    lane = lax.broadcasted_iota(jnp.int32, (NK, N), 1)
    level = lax.broadcasted_iota(jnp.int32, (NK, N), 0).astype(jnp.float32)
    first, last = lane == 0, lane == N - 1

    for k in range(NK + 1):
        p[pl.ds(k * PAD, 8), :] = zero8
        fa[pl.ds(k * PAD, 8), :] = zero8
        fb[pl.ds(k * PAD, 8), :] = zero8

    @pl.when(is_bottom)
    def _():
        recv[SOUTH] = jnp.zeros((MSG, N), jnp.float32)
        crecv[SW] = zero8
        crecv[SE] = zero8

    def set_cor(b, _):
        rows = pl.ds(pl.multiple_of(b * 8, 8), 8)
        j = lax.broadcasted_iota(jnp.int32, (8, N), 0) + (b * 8 + lat * N)
        cor[rows, :] = 0.25 * jnp.sin(
            jnp.pi * ((j.astype(jnp.float32) + 0.5) / (N * n_lat) - 0.5)
        )
        return 0

    lax.fori_loop(0, N // 8, set_cor, 0)

    for load in loads[:3]:
        load.wait()
    dep[pl.ds(N, 8), :] = zero8
    dep[pl.ds(0, N), :] = (ind[...] * strata[...]).astype(jnp.float32)
    fr[...] = fr[...] * 0.25

    def set_depth(b, _):
        r = pl.multiple_of(b * 8, 8)
        rows = pl.ds(r, 8)
        d = dep[rows, :]
        dep_e[rows, :] = jnp.where(lane8 == N - 1, 0.0, jnp.minimum(d, east_of(d)))
        dep_n[rows, :] = jnp.minimum(d, dep[pl.ds(r + 1, 8), :])
        fr_e[rows, :] = east_of(fr[rows, :])
        return 0

    lax.fori_loop(0, N // 8, set_depth, 0, unroll=True)

    def set_columns(place, x):
        y = x.T
        cols[pl.ds(place * 16, 8), :] = y[N - 8 :]
        cols[pl.ds(place * 16 + 8, 8), :] = y[:8]

    set_columns(4 * NK, dep[pl.ds(0, N), :])
    set_columns(4 * NK + 1, fr[...])

    def pack(ref, f, double):
        def step(k, _):
            block = pl.ds(pl.multiple_of(k * N, N), N)
            x = ref[block, :]
            if double:
                x = x + x
                ref[block, :] = x
            set_columns(f * NK + k, x)
            return 0

        lax.fori_loop(0, NK, step, 0, unroll=8)


    def wide(x):
        return jnp.broadcast_to(x, (NK, N))

    def column(f, entry):
        return cols[pl.ds(f * NK * 16 + 6 + entry, NK, stride=16), :]

    def plane_column(i, entry):
        return wide(cols[pl.ds((4 * NK + i) * 16 + 6 + entry, 1), :])

    def columns(entry):
        t_c, u_c, k_c, v_c = (column(f, entry) for f in range(4))
        return t_c, u_c, v_c, k_c, plane_column(0, entry)

    slab_rows = slabs.reshape(8 * NK * 8, N)

    def edge_rows(j):
        side = 0 if j < 8 else 1
        t_r, u_r, v_r, k_r = (
            slab_rows[pl.ds((2 * f + side) * NK * 8 + j % 8, NK, stride=8), :] for f in range(4)
        )
        return t_r, u_r, v_r, k_r + k_r, wide(dep[pl.ds(j, 1), :])

    def x_face(a, b):
        return face(level, jnp.minimum(a[4], b[4]), a[1], b[1], a[0], b[0], a[3], b[3])

    def y_face(a, b):
        return face(level, jnp.minimum(a[4], b[4]), a[2], b[2], a[0], b[0], a[3], b[3])

    def closed_step(mid, through, along):
        flow = jnp.where(last, 0.0, along(mid, tuple(east_of(x) for x in mid)))
        tc, _, _, kc, d = mid
        above = jnp.where(
            level + 1.0 < d,
            (kc + pltpu.roll(kc, NK - 1, 0)) * (pltpu.roll(tc, NK - 1, 0) - tc),
            0.0,
        )
        total = through + (west_of(flow) - flow) + (above - pltpu.roll(above, 1, 0))
        return jnp.where(level < d, tc + SCALE * total, 0.0)

    def marked(values):
        return (*values[:3], jnp.where(level < values[4], values[3], 0.0))

    def stage(side, values, tracer):
        for f, x in enumerate((*marked(values), tracer)):
            send[side, pl.ds(f * NK, NK), :] = x

    def stage_corners(slab, values):
        x = zero8
        for f, y in enumerate(marked(values)):
            for half in (0, 1):
                z, to = y[8 * half : 8 * half + 8], f + 16 * half
                x = jnp.where(lane8 == to, pltpu.roll(z, to, 1) if to else z, x)
                x = jnp.where(lane8 == 8 + to, pltpu.roll(z, 9 + to, 1), x)
        csend[slab] = x

    for load in loads[3:11]:
        load.wait()
    r_n, r_s = edge_rows(N - 1), edge_rows(0)
    stage(NORTH, r_n, closed_step(r_n, y_face(edge_rows(N - 2), r_n), x_face))
    stage(SOUTH, r_s, closed_step(r_s, -y_face(r_s, edge_rows(1)), x_face))
    stage_corners(0, r_n)
    stage_corners(1, r_s)

    def tracer(b, _):
        r = pl.multiple_of(b * 8, 8)
        rows = pl.ds(r, 8)
        d, de, dn = dep[rows, :], dep_e[rows, :], dep_n[rows, :]
        below = zero8
        press = zero8
        for k in range(NK):
            c = float(k)
            here, up_rows = pl.ds(r + k * N, 8), pl.ds(r + k * N + 1, 8)
            tc, kc, uc, vc = t[here, :], kd[here, :], u[here, :], v[here, :]
            next_u = east_of(uc)
            ue[here, :] = next_u
            f_e = face(c, de, uc, next_u, tc, east_of(tc), kc, east_of(kc))
            f_n = face(c, dn, vc, v[up_rows, :], tc, t[up_rows, :], kc, kd[up_rows, :])
            fa[pl.ds(r + k * PAD + 8, 8), :] = f_n
            f_s = fa[pl.ds(r + k * PAD + 7, 8), :]
            if k < NK - 1:
                t_up, k_up = t[pl.ds(r + (k + 1) * N, 8), :], kd[pl.ds(r + (k + 1) * N, 8), :]
                above = jnp.where(c + 1.0 < d, (kc + k_up) * (t_up - tc), 0.0)
            else:
                above = zero8
            total = (west_of(f_e) - f_e) + (f_s - f_n) + (above - below)
            below = above
            tc = jnp.where(c < d, tc + SCALE * total, 0.0)
            tn[here, :] = tc
            press = press + PG * tc
            p[pl.ds(r + k * PAD + 8, 8), :] = press
        return 0

    def pack_fields():
        for f, ref in enumerate((t, u, kd, v)):
            loads[11 + f].wait()
            pack(ref, f, ref is kd)

    pl.semaphore_wait(barrier, expected)
    for (place, _, number), ahead in zip(peers, to_early):

        @pl.when(ahead)
        def _(place=place, number=number):
            pl.semaphore_signal(
                ready.at[number], inc=1, device_id=at(place), device_id_type=MESH
            )

    def rim(side, slot, place):
        return pltpu.make_async_remote_copy(
            src_ref=send.at[side], dst_ref=recv.at[slot], send_sem=send_sem.at[side],
            recv_sem=recv_sem.at[slot], device_id=at(place), device_id_type=MESH,
        )

    def corner(slab, message, slot, place):
        return pltpu.make_async_remote_copy(
            src_ref=csend.at[slab], dst_ref=crecv.at[slot], send_sem=csend_sem.at[message],
            recv_sem=crecv_sem.at[slot], device_id=at(place), device_id_type=MESH,
        )

    to_north = rim(NORTH, jnp.where(is_top, NORTH, SOUTH), north)
    to_south = rim(SOUTH, NORTH, south)
    to_east, to_west = rim(EAST, WEST, east), rim(WEST, EAST, west)
    to_ne = corner(0, 0, jnp.where(is_top, NE, SW), north_e)
    to_nw = corner(0, 1, jnp.where(is_top, NW, SE), north_w)
    to_se, to_sw = corner(1, 2, NW, south_e), corner(1, 3, NE, south_w)

    messages = (to_east, to_west, to_north, to_south, to_ne, to_nw, to_se, to_sw)

    def start(numbers):
        for i in numbers:
            pl.when(peers[i][1] & jnp.logical_not(to_late[i]))(messages[i].start)

    start((2, 3, 4, 5, 6, 7))
    pack_fields()
    c_e, c_w = columns(1), columns(2)
    stage(EAST, c_e, closed_step(c_e, x_face(columns(0), c_e), y_face))
    stage(WEST, c_w, closed_step(c_w, -x_face(c_w, columns(3)), y_face))
    start((0, 1))
    lax.fori_loop(0, N // 8, tracer, 0, unroll=2)

    def momentum(b, _):
        r = pl.multiple_of(b * 8, 8)
        rows = pl.ds(r, 8)
        d, de, dn = dep[rows, :], dep_e[rows, :], dep_n[rows, :]
        f, f_next, co = fr[rows, :], fr_e[rows, :], cor[rows, :]
        for k in range(NK):
            c = float(k)
            here, up_rows = pl.ds(r + k * N, 8), pl.ds(r + k * N + 1, 8)
            mine, south_rows = pl.ds(r + k * PAD + 8, 8), pl.ds(r + k * PAD + 7, 8)
            uc, vc, pc = u[here, :], v[here, :], p[mine, :]
            wet_e, wet_n, wet = c < de, c < dn, c < d
            u_e = jnp.where(wet_e, ue[here, :] - uc, 0.0)
            v_e = jnp.where(wet_e, east_of(vc) - vc, 0.0)
            u_n = jnp.where(wet_n, u[up_rows, :] - uc, 0.0)
            v_n = jnp.where(wet_n, v[up_rows, :] - vc, 0.0)
            fa[mine, :] = u_n
            fb[mine, :] = v_n
            gain = east_of(pc) - pc
            across_x = (f * u_e - gain) - west_of(gain + f_next * u_e)
            lap_u = u_n - fa[south_rows, :]
            lap_v = (v_e - west_of(v_e)) + (v_n - fb[south_rows, :])
            dp_y = p[pl.ds(r + k * PAD + 9, 8), :] - p[south_rows, :]
            un[here, :] = jnp.where(wet, (uc + co * vc) + across_x + f * lap_u, 0.0)
            vn[here, :] = jnp.where(wet, (vc - co * uc) - dp_y + f * lap_v, 0.0)
        return 0

    lax.fori_loop(0, N // 8, momentum, 0)

    for i, message in enumerate(messages):

        @pl.when(to_late[i])
        def _(i=i, message=message):
            pl.semaphore_wait(ready.at[i], 1)
            message.start()

    rim(NORTH, NORTH, north).wait_recv()
    rim(EAST, EAST, east).wait_recv()
    rim(WEST, WEST, west).wait_recv()

    @pl.when(not_own_e)
    def _():
        corner(0, 0, NE, north_e).wait_recv()

    @pl.when(not_own_w)
    def _():
        corner(0, 1, NW, north_w).wait_recv()

    @pl.when(own_e)
    def _():
        crecv[NE] = csend[0]

    @pl.when(own_w)
    def _():
        crecv[NW] = csend[0]

    @pl.when(not_bottom)
    def _():
        rim(SOUTH, SOUTH, south).wait_recv()
        corner(1, 2, SE, south_e).wait_recv()
        corner(1, 3, SW, south_w).wait_recv()

    @pl.when(is_top)
    def _():
        x = mirrored(recv[NORTH])
        r = lax.broadcasted_iota(jnp.int32, (MSG, N), 0)
        recv[NORTH] = jnp.where((r >= NK) & (r < 3 * NK), -x, x)
        turned = ((lane8 & 7) == 1) | ((lane8 & 7) == 2)
        x = crecv[NW]
        x = pltpu.roll(jnp.where(turned, -x, x), 8, 1)
        crecv[NW] = x
        x = crecv[NE]
        crecv[NE] = pltpu.roll(jnp.where(turned, -x, x), N - 8, 1)

    def with_depth(t_g, u_g, v_g, k_g):
        return t_g, u_g, v_g, k_g, jnp.where(k_g > 0.0, float(NK), 0.0)

    def ghost(slot):
        return with_depth(*(recv[slot, pl.ds(f * NK, NK), :] for f in range(4)))

    def beyond(slot, entry, to):
        x = crecv[slot]

        def value(f):
            shift = to - entry - f + N
            return jnp.concatenate(
                [pltpu.roll(x, shift % N, 1), pltpu.roll(x, (shift - 16) % N, 1)], 0
            )

        return with_depth(*(value(f) for f in range(4)))

    g_w, g_e, g_s, g_n = ghost(WEST), ghost(EAST), ghost(SOUTH), ghost(NORTH)
    f_w, f_e = x_face(g_w, c_w), x_face(c_e, g_e)
    f_s, f_n = y_face(g_s, r_s), y_face(r_n, g_n)

    def whole(slot, flow, low, high):
        ends = jnp.where(first, low, jnp.where(last, high, 0.0))
        return running_sum(PG * (recv[slot, pl.ds(4 * NK, NK), :] + SCALE * (flow + ends)))

    p_w = whole(WEST, -f_w, y_face(beyond(SW, 8, 0), g_w), -y_face(g_w, beyond(NW, 8, N - 1)))
    p_e = whole(EAST, f_e, y_face(beyond(SE, 0, 0), g_e), -y_face(g_e, beyond(NE, 0, N - 1)))
    p_s = whole(SOUTH, -f_s, x_face(beyond(SW, 8, 0), g_s), -x_face(g_s, beyond(SE, 0, N - 1)))
    p_n = whole(NORTH, f_n, x_face(beyond(NW, 8, 0), g_n), -x_face(g_n, beyond(NE, 0, N - 1)))
    t_w, t_e, t_s, t_n = SCALE * f_w, -SCALE * f_e, SCALE * f_s, -SCALE * f_n
    d_w, d_e, d_s, d_n = (running_sum(PG * x) for x in (t_w, t_e, t_s, t_n))
    q_w = running_sum(PG * send[WEST, pl.ds(4 * NK, NK), :])
    q_e = running_sum(PG * send[EAST, pl.ds(4 * NK, NK), :])

    def across(x):
        return jnp.where(first, 0.0, west_of(x)) - jnp.where(last, 0.0, east_of(x))

    def friction(mid, other, f, i):
        m = level < jnp.minimum(mid[4], other[4])
        return jnp.where(m, f * (other[i] - mid[i]), 0.0)

    def masked(depth, x):
        return jnp.where(level < depth, x, 0.0)

    col_e, col_w = plane_column(1, 1), plane_column(1, 2)
    row_s, row_n = wide(fr[pl.ds(0, 1), :]), wide(fr[pl.ds(N - 1, 1), :])
    def add(ref, j, x):
        rows = pl.ds(j, NK, stride=N)
        ref[rows, :] = ref[rows, :] + x

    add(tn, N - 1, t_n)
    add(tn, 0, t_s)
    add(un, N - 1, friction(r_n, g_n, row_n, 1) + masked(r_n[4], across(d_n)))
    add(un, 0, friction(r_s, g_s, row_s, 1) + masked(r_s[4], across(d_s)))
    add(vn, N - 1, friction(r_n, g_n, row_n, 2) - masked(r_n[4], p_n))
    add(vn, 0, friction(r_s, g_s, row_s, 2) + masked(r_s[4], p_s))
    add(vn, N - 2, -masked(wide(dep[pl.ds(N - 2, 1), :]), d_n))
    add(vn, 1, masked(wide(dep[pl.ds(1, 1), :]), d_s))
    fix[pl.ds(0, NK, stride=4), :] = -masked(plane_column(0, 0), d_e)
    fix[pl.ds(1, NK, stride=4), :] = friction(c_e, g_e, col_e, 1) - masked(c_e[4], p_e - q_w)
    fix[pl.ds(2, NK, stride=4), :] = friction(c_w, g_w, col_w, 1) + masked(c_w[4], p_w - q_e)
    fix[pl.ds(3, NK, stride=4), :] = masked(plane_column(0, 3), d_w)
    fix[pl.ds(64, NK, stride=2), :] = friction(c_e, g_e, col_e, 2) + masked(c_e[4], across(d_e))
    fix[pl.ds(65, NK, stride=2), :] = friction(c_w, g_w, col_w, 2) + masked(c_w[4], across(d_w))
    fix[pl.ds(96, NK, stride=2), :] = t_e
    fix[pl.ds(97, NK, stride=2), :] = t_w
    fix_out[...] = fix[...].T

    for (_, ok, _), message in zip(peers, messages):
        pl.when(ok)(message.wait_send)


def finish(tn, un, vn, fix, t_out, u_out, v_out, t, u, v, out_sem):
    lane8 = lax.broadcasted_iota(jnp.int32, (8, N), 1)
    rim2 = (lane8 == 0) | (lane8 == N - 1)
    rim4 = (lane8 <= 1) | (lane8 >= N - 2)

    outs = ((t, t_out), (u, u_out), (v, v_out))

    def step(g, _):
        for k in range(CHUNK):
            start = pl.multiple_of((g * CHUNK + k) * N, N)
            for r in range(0, N, 8):
                here = pl.ds(start + r, 8)
                x = fix[pl.ds(r, 8), :]
                for new, old, rim, shift in (
                    (u, un, rim4, N - 2 - 4 * k), (v, vn, rim2, 63 - 2 * k), (t, tn, rim2, 31 - 2 * k),
                ):
                    shift = lax.rem(shift + N - g * CHUNK * (4 if rim is rim4 else 2), N)
                    new[here, :] = old[here, :] + jnp.where(rim, pltpu.roll(x, shift, 1), 0.0)
        block = pl.ds(pl.multiple_of(g * CHUNK * N, N), CHUNK * N)
        for i, (src, dst) in enumerate(outs):
            pltpu.make_async_copy(src.at[block], dst.at[block], out_sem.at[i]).start()
        return 0

    lax.fori_loop(0, NK // CHUNK, step, 0)
    for i, (src, dst) in enumerate(outs):
        pltpu.make_async_copy(src, dst, out_sem.at[i]).wait()


def solution(mesh):
    n_lon, n_lat = mesh.shape["lon"], mesh.shape["lat"]
    f32, i32 = jnp.float32, jnp.int32

    def on_device(t, u, v, kd, fr, ind, strata):
        flat = [x.reshape(FLAT, N) for x in (t, u, v, kd)]
        outs = pl.pallas_call(
            functools.partial(kernel, n_lon, n_lat),
            out_shape=[*[pltpu.VMEM((FLAT, N), f32)] * 3, pltpu.VMEM((N, N), f32)],
            in_specs=[pl.BlockSpec(memory_space=pltpu.HBM)] * 11,
            out_specs=[pl.BlockSpec(memory_space=pltpu.VMEM)] * 4,
            scratch_shapes=[
                *[pltpu.VMEM((FLAT + 8, N), f32)] * 4,
                *[pltpu.VMEM((NK * PAD + 8, N), f32)] * 3,
                pltpu.VMEM((N, N), f32),
                pltpu.VMEM((N, N), i32),
                pltpu.VMEM((N, N), i32),
                pltpu.VMEM((N + 8, N), f32),
                *[pltpu.VMEM((N, N), f32)] * 4,
                pltpu.VMEM((FLAT, N), f32),
                pltpu.VMEM((8, NK, 8, N), f32),
                pltpu.VMEM(((4 * NK + 2) * 16, N), f32),
                pltpu.VMEM((N, N), f32),
                pltpu.VMEM((4, MSG, N), f32),
                pltpu.VMEM((4, MSG, N), f32),
                pltpu.VMEM((2, 8, N), f32),
                pltpu.VMEM((4, 8, N), f32),
                pltpu.SemaphoreType.DMA((15,)),
                *[pltpu.SemaphoreType.DMA((4,))] * 4,
                pltpu.SemaphoreType.REGULAR((8,)),
            ],
            compiler_params=pltpu.CompilerParams(
                collective_id=0, has_side_effects=True, vmem_limit_bytes=60 * 1024 * 1024
            ),
            cost_estimate=pl.CostEstimate(
                flops=80 * FLAT * N, bytes_accessed=30 * FLAT * N, transcendentals=0
            ),
        )(*flat, t, u, v, kd, fr, ind, strata)
        outs = pl.pallas_call(
            finish,
            out_shape=[jax.ShapeDtypeStruct((FLAT, N), f32)] * 3,
            in_specs=[pl.BlockSpec(memory_space=pltpu.VMEM)] * 4,
            out_specs=[pl.BlockSpec(memory_space=pltpu.HBM)] * 3,
            scratch_shapes=[
                *[pltpu.VMEM((FLAT, N), f32)] * 3,
                pltpu.SemaphoreType.DMA((3,)),
            ],
            compiler_params=pltpu.CompilerParams(vmem_limit_bytes=32 * 1024 * 1024),
        )(*outs)
        return tuple(x.reshape(NK, N, N) for x in outs)

    plane, field = P("lat", "lon"), P(None, "lat", "lon")
    return jax.shard_map(
        on_device,
        mesh=mesh,
        in_specs=(field, field, field, field, plane, plane, plane),
        out_specs=(field, field, field),
        check_vma=False,
    )
```

```python
import functools
import math

import jax
import jax.numpy as jnp
from jax import lax
from jax.experimental import pallas as pl
from jax.experimental.pallas import tpu as pltpu
from jax.sharding import PartitionSpec as P

MESH = pl.DeviceIdType.MESH
NK = 16
N = 128
FLAT = NK * N
PAD = N + 8
SCALE = 1.0 / 16.0
PG = 0.25 * 0.05
WEST, EAST, SOUTH, NORTH = 0, 1, 2, 3
SW, SE, NW, NE = 0, 1, 2, 3
MSG = 5 * NK
CHUNK = 4


def east_of(x):
    return pltpu.roll(x, N - 1, 1)


def west_of(x):
    return pltpu.roll(x, 1, 1)


def face(c, d, a, b, ta, tb, ka, kb):
    return jnp.where(c < d, (a + b) * (ta + tb) - (ka + kb) * (tb - ta), 0.0)


def mirrored(x):
    lane = lax.broadcasted_iota(jnp.int32, x.shape, 1)
    return jnp.take_along_axis(x, N - 1 - lane, axis=1)


def running_sum(x):
    level = lax.broadcasted_iota(jnp.int32, x.shape, 0)
    for step in (1, 2, 4, 8):
        x = x + jnp.where(level >= step, pltpu.roll(x, step, 0), 0.0)
    return x


def kernel(
    n_lon, n_lat,
    t_hbm, u_hbm, v_hbm, k_hbm, t_rows, u_rows, v_rows, k_rows, fr_hbm, ind_hbm, str_hbm,
    tn, un, vn, fix_out,
    t, u, v, kd, p, fa, fb, fr, ind, strata, dep, dep_e, dep_n, cor, fr_e,
    ue, slabs, cols, fix, send, recv, csend, crecv,
    in_sem, send_sem, recv_sem, csend_sem, crecv_sem, ready,
):
    lon, lat = lax.axis_index("lon"), lax.axis_index("lat")
    is_top, is_bottom = lat == n_lat - 1, lat == 0
    not_bottom = jnp.logical_not(is_bottom)
    lon_e, lon_w = lax.rem(lon + 1, n_lon), lax.rem(lon + n_lon - 1, n_lon)
    lat_n, lat_s = jnp.where(is_top, lat, lat + 1), jnp.where(is_bottom, lat, lat - 1)
    east, west = (lat, lon_e), (lat, lon_w)
    north, south = (lat_n, jnp.where(is_top, n_lon - 1 - lon, lon)), (lat_s, lon)
    fold_e, fold_w = lax.rem(2 * n_lon - 2 - lon, n_lon), lax.rem(n_lon - lon, n_lon)
    own_e = is_top & (fold_e == lon)
    own_w = is_top & (fold_w == lon)
    not_own_e, not_own_w = jnp.logical_not(own_e), jnp.logical_not(own_w)
    north_e = (lat_n, jnp.where(is_top, fold_e, lon_e))
    north_w = (lat_n, jnp.where(is_top, fold_w, lon_w))
    south_e, south_w = (lat_s, lon_e), (lat_s, lon_w)

    def at(place):
        return {"lat": place[0], "lon": place[1]}

    loads = [
        pltpu.make_async_copy(src, dst, in_sem.at[i])
        for i, (src, dst) in enumerate(
            (
                (ind_hbm, ind), (str_hbm, strata), (fr_hbm, fr),
                *(
                    (ref.at[:, pl.ds(side * (N - 8), 8), :], slabs.at[2 * f + side])
                    for f, ref in enumerate((t_rows, u_rows, v_rows, k_rows))
                    for side in (0, 1)
                ),
                (t_hbm, t.at[pl.ds(0, FLAT)]), (u_hbm, u.at[pl.ds(0, FLAT)]),
                (k_hbm, kd.at[pl.ds(0, FLAT)]), (v_hbm, v.at[pl.ds(0, FLAT)]),
            )
        )
    ]
    for load in loads:
        load.start()
    barrier = pltpu.get_barrier_semaphore()

    def is_early(place):
        return lax.rem(place[1], n_lon // 2) < n_lon // 4

    early = is_early((lat, lon))
    always = lat >= 0
    peers = (
        (east, always, 1),
        (west, always, 0),
        (north, always, jnp.where(is_top, 2, 3)),
        (south, not_bottom, 2),
        (north_e, not_own_e, jnp.where(is_top, 4, 7)),
        (north_w, not_own_w, jnp.where(is_top, 5, 6)),
        (south_e, not_bottom, 5),
        (south_w, not_bottom, 4),
    )
    to_late = [ok & early & jnp.logical_not(is_early(place)) for place, ok, _ in peers]
    to_early = [ok & jnp.logical_not(early) & is_early(place) for place, ok, _ in peers]
    expected = jnp.int32(0)
    for (place, ok, _), ahead, behind in zip(peers, to_early, to_late):

        @pl.when(ok & jnp.logical_not(ahead))
        def _(place=place):
            pl.semaphore_signal(barrier, inc=1, device_id=at(place), device_id_type=MESH)

        expected = expected + (ok & jnp.logical_not(behind)).astype(jnp.int32)

    lane8 = lax.broadcasted_iota(jnp.int32, (8, N), 1)
    zero8 = jnp.zeros((8, N), jnp.float32)
    lane = lax.broadcasted_iota(jnp.int32, (NK, N), 1)
    level = lax.broadcasted_iota(jnp.int32, (NK, N), 0).astype(jnp.float32)
    first, last = lane == 0, lane == N - 1

    for k in range(NK + 1):
        p[pl.ds(k * PAD, 8), :] = zero8
        fa[pl.ds(k * PAD, 8), :] = zero8
        fb[pl.ds(k * PAD, 8), :] = zero8

    @pl.when(is_bottom)
    def _():
        recv[SOUTH] = jnp.zeros((MSG, N), jnp.float32)
        crecv[SW] = zero8
        crecv[SE] = zero8

    def set_cor(b, _):
        rows = pl.ds(pl.multiple_of(b * 8, 8), 8)
        j = lax.broadcasted_iota(jnp.int32, (8, N), 0) + (b * 8 + lat * N)
        cor[rows, :] = 0.25 * jnp.sin(
            jnp.pi * ((j.astype(jnp.float32) + 0.5) / (N * n_lat) - 0.5)
        )
        return 0

    lax.fori_loop(0, N // 8, set_cor, 0)

    for load in loads[:3]:
        load.wait()
    dep[pl.ds(N, 8), :] = zero8
    dep[pl.ds(0, N), :] = (ind[...] * strata[...]).astype(jnp.float32)
    fr[...] = fr[...] * 0.25

    def set_depth(b, _):
        r = pl.multiple_of(b * 8, 8)
        rows = pl.ds(r, 8)
        d = dep[rows, :]
        dep_e[rows, :] = jnp.where(lane8 == N - 1, 0.0, jnp.minimum(d, east_of(d)))
        dep_n[rows, :] = jnp.minimum(d, dep[pl.ds(r + 1, 8), :])
        fr_e[rows, :] = east_of(fr[rows, :])
        return 0

    lax.fori_loop(0, N // 8, set_depth, 0, unroll=True)

    def set_columns(place, x):
        y = x.T
        cols[pl.ds(place * 16, 8), :] = y[N - 8 :]
        cols[pl.ds(place * 16 + 8, 8), :] = y[:8]

    set_columns(4 * NK, dep[pl.ds(0, N), :])
    set_columns(4 * NK + 1, fr[...])

    def pack(ref, f, double):
        def step(k, _):
            block = pl.ds(pl.multiple_of(k * N, N), N)
            x = ref[block, :]
            if double:
                x = x + x
                ref[block, :] = x
            set_columns(f * NK + k, x)
            return 0

        lax.fori_loop(0, NK, step, 0, unroll=8)


    def wide(x):
        return jnp.broadcast_to(x, (NK, N))

    def column(f, entry):
        return cols[pl.ds(f * NK * 16 + 6 + entry, NK, stride=16), :]

    def plane_column(i, entry):
        return wide(cols[pl.ds((4 * NK + i) * 16 + 6 + entry, 1), :])

    def columns(entry):
        t_c, u_c, k_c, v_c = (column(f, entry) for f in range(4))
        return t_c, u_c, v_c, k_c, plane_column(0, entry)

    slab_rows = slabs.reshape(8 * NK * 8, N)

    def edge_rows(j):
        side = 0 if j < 8 else 1
        t_r, u_r, v_r, k_r = (
            slab_rows[pl.ds((2 * f + side) * NK * 8 + j % 8, NK, stride=8), :] for f in range(4)
        )
        return t_r, u_r, v_r, k_r + k_r, wide(dep[pl.ds(j, 1), :])

    def x_face(a, b):
        return face(level, jnp.minimum(a[4], b[4]), a[1], b[1], a[0], b[0], a[3], b[3])

    def y_face(a, b):
        return face(level, jnp.minimum(a[4], b[4]), a[2], b[2], a[0], b[0], a[3], b[3])

    def closed_step(mid, through, along):
        flow = jnp.where(last, 0.0, along(mid, tuple(east_of(x) for x in mid)))
        tc, _, _, kc, d = mid
        above = jnp.where(
            level + 1.0 < d,
            (kc + pltpu.roll(kc, NK - 1, 0)) * (pltpu.roll(tc, NK - 1, 0) - tc),
            0.0,
        )
        total = through + (west_of(flow) - flow) + (above - pltpu.roll(above, 1, 0))
        return jnp.where(level < d, tc + SCALE * total, 0.0)

    def marked(values):
        return (*values[:3], jnp.where(level < values[4], values[3], 0.0))

    def stage(side, values, tracer):
        for f, x in enumerate((*marked(values), tracer)):
            send[side, pl.ds(f * NK, NK), :] = x

    def stage_corners(slab, values):
        x = zero8
        for f, y in enumerate(marked(values)):
            for half in (0, 1):
                z, to = y[8 * half : 8 * half + 8], f + 16 * half
                x = jnp.where(lane8 == to, pltpu.roll(z, to, 1) if to else z, x)
                x = jnp.where(lane8 == 8 + to, pltpu.roll(z, 9 + to, 1), x)
        csend[slab] = x

    for load in loads[3:11]:
        load.wait()
    r_n, r_s = edge_rows(N - 1), edge_rows(0)
    stage(NORTH, r_n, closed_step(r_n, y_face(edge_rows(N - 2), r_n), x_face))
    stage(SOUTH, r_s, closed_step(r_s, -y_face(r_s, edge_rows(1)), x_face))
    stage_corners(0, r_n)
    stage_corners(1, r_s)

    def tracer(b, _):
        r = pl.multiple_of(b * 8, 8)
        rows = pl.ds(r, 8)
        d, de, dn = dep[rows, :], dep_e[rows, :], dep_n[rows, :]
        below = zero8
        press = zero8
        for k in range(NK):
            c = float(k)
            here, up_rows = pl.ds(r + k * N, 8), pl.ds(r + k * N + 1, 8)
            tc, kc, uc, vc = t[here, :], kd[here, :], u[here, :], v[here, :]
            next_u = east_of(uc)
            ue[here, :] = next_u
            f_e = face(c, de, uc, next_u, tc, east_of(tc), kc, east_of(kc))
            f_n = face(c, dn, vc, v[up_rows, :], tc, t[up_rows, :], kc, kd[up_rows, :])
            fa[pl.ds(r + k * PAD + 8, 8), :] = f_n
            f_s = fa[pl.ds(r + k * PAD + 7, 8), :]
            if k < NK - 1:
                t_up, k_up = t[pl.ds(r + (k + 1) * N, 8), :], kd[pl.ds(r + (k + 1) * N, 8), :]
                above = jnp.where(c + 1.0 < d, (kc + k_up) * (t_up - tc), 0.0)
            else:
                above = zero8
            total = (west_of(f_e) - f_e) + (f_s - f_n) + (above - below)
            below = above
            tc = jnp.where(c < d, tc + SCALE * total, 0.0)
            tn[here, :] = tc
            press = press + PG * tc
            p[pl.ds(r + k * PAD + 8, 8), :] = press
        return 0

    def pack_fields():
        for f, ref in enumerate((t, u, kd, v)):
            loads[11 + f].wait()
            pack(ref, f, ref is kd)

    pl.semaphore_wait(barrier, expected)
    for (place, _, number), ahead in zip(peers, to_early):

        @pl.when(ahead)
        def _(place=place, number=number):
            pl.semaphore_signal(
                ready.at[number], inc=1, device_id=at(place), device_id_type=MESH
            )

    def rim(side, slot, place):
        return pltpu.make_async_remote_copy(
            src_ref=send.at[side], dst_ref=recv.at[slot], send_sem=send_sem.at[side],
            recv_sem=recv_sem.at[slot], device_id=at(place), device_id_type=MESH,
        )

    def corner(slab, message, slot, place):
        return pltpu.make_async_remote_copy(
            src_ref=csend.at[slab], dst_ref=crecv.at[slot], send_sem=csend_sem.at[message],
            recv_sem=crecv_sem.at[slot], device_id=at(place), device_id_type=MESH,
        )

    to_north = rim(NORTH, jnp.where(is_top, NORTH, SOUTH), north)
    to_south = rim(SOUTH, NORTH, south)
    to_east, to_west = rim(EAST, WEST, east), rim(WEST, EAST, west)
    to_ne = corner(0, 0, jnp.where(is_top, NE, SW), north_e)
    to_nw = corner(0, 1, jnp.where(is_top, NW, SE), north_w)
    to_se, to_sw = corner(1, 2, NW, south_e), corner(1, 3, NE, south_w)

    messages = (to_east, to_west, to_north, to_south, to_ne, to_nw, to_se, to_sw)

    def start(numbers):
        for i in numbers:
            pl.when(peers[i][1] & jnp.logical_not(to_late[i]))(messages[i].start)

    start((2, 3, 4, 5, 6, 7))
    pack_fields()
    c_e, c_w = columns(1), columns(2)
    stage(EAST, c_e, closed_step(c_e, x_face(columns(0), c_e), y_face))
    stage(WEST, c_w, closed_step(c_w, -x_face(c_w, columns(3)), y_face))
    start((0, 1))
    lax.fori_loop(0, N // 8, tracer, 0, unroll=2)

    for i, message in enumerate(messages):

        @pl.when(to_late[i])
        def _(i=i, message=message):
            pl.semaphore_wait(ready.at[i], 1)
            message.start()

    def momentum(b, _):
        r = pl.multiple_of(b * 8, 8)
        rows = pl.ds(r, 8)
        d, de, dn = dep[rows, :], dep_e[rows, :], dep_n[rows, :]
        f, f_next, co = fr[rows, :], fr_e[rows, :], cor[rows, :]
        for k in range(NK):
            c = float(k)
            here, up_rows = pl.ds(r + k * N, 8), pl.ds(r + k * N + 1, 8)
            mine, south_rows = pl.ds(r + k * PAD + 8, 8), pl.ds(r + k * PAD + 7, 8)
            uc, vc, pc = u[here, :], v[here, :], p[mine, :]
            wet_e, wet_n, wet = c < de, c < dn, c < d
            u_e = jnp.where(wet_e, ue[here, :] - uc, 0.0)
            v_e = jnp.where(wet_e, east_of(vc) - vc, 0.0)
            u_n = jnp.where(wet_n, u[up_rows, :] - uc, 0.0)
            v_n = jnp.where(wet_n, v[up_rows, :] - vc, 0.0)
            fa[mine, :] = u_n
            fb[mine, :] = v_n
            gain = east_of(pc) - pc
            across_x = (f * u_e - gain) - west_of(gain + f_next * u_e)
            lap_u = u_n - fa[south_rows, :]
            lap_v = (v_e - west_of(v_e)) + (v_n - fb[south_rows, :])
            dp_y = p[pl.ds(r + k * PAD + 9, 8), :] - p[south_rows, :]
            un[here, :] = jnp.where(wet, (uc + co * vc) + across_x + f * lap_u, 0.0)
            vn[here, :] = jnp.where(wet, (vc - co * uc) - dp_y + f * lap_v, 0.0)
        return 0

    lax.fori_loop(0, N // 8, momentum, 0)

    rim(NORTH, NORTH, north).wait_recv()
    rim(EAST, EAST, east).wait_recv()
    rim(WEST, WEST, west).wait_recv()

    @pl.when(not_own_e)
    def _():
        corner(0, 0, NE, north_e).wait_recv()

    @pl.when(not_own_w)
    def _():
        corner(0, 1, NW, north_w).wait_recv()

    @pl.when(own_e)
    def _():
        crecv[NE] = csend[0]

    @pl.when(own_w)
    def _():
        crecv[NW] = csend[0]

    @pl.when(not_bottom)
    def _():
        rim(SOUTH, SOUTH, south).wait_recv()
        corner(1, 2, SE, south_e).wait_recv()
        corner(1, 3, SW, south_w).wait_recv()

    @pl.when(is_top)
    def _():
        x = mirrored(recv[NORTH])
        r = lax.broadcasted_iota(jnp.int32, (MSG, N), 0)
        recv[NORTH] = jnp.where((r >= NK) & (r < 3 * NK), -x, x)
        turned = ((lane8 & 7) == 1) | ((lane8 & 7) == 2)
        x = crecv[NW]
        x = pltpu.roll(jnp.where(turned, -x, x), 8, 1)
        crecv[NW] = x
        x = crecv[NE]
        crecv[NE] = pltpu.roll(jnp.where(turned, -x, x), N - 8, 1)

    def with_depth(t_g, u_g, v_g, k_g):
        return t_g, u_g, v_g, k_g, jnp.where(k_g > 0.0, float(NK), 0.0)

    def ghost(slot):
        return with_depth(*(recv[slot, pl.ds(f * NK, NK), :] for f in range(4)))

    def beyond(slot, entry, to):
        x = crecv[slot]

        def value(f):
            shift = to - entry - f + N
            return jnp.concatenate(
                [pltpu.roll(x, shift % N, 1), pltpu.roll(x, (shift - 16) % N, 1)], 0
            )

        return with_depth(*(value(f) for f in range(4)))

    g_w, g_e, g_s, g_n = ghost(WEST), ghost(EAST), ghost(SOUTH), ghost(NORTH)
    f_w, f_e = x_face(g_w, c_w), x_face(c_e, g_e)
    f_s, f_n = y_face(g_s, r_s), y_face(r_n, g_n)

    def whole(slot, flow, low, high):
        ends = jnp.where(first, low, jnp.where(last, high, 0.0))
        return running_sum(PG * (recv[slot, pl.ds(4 * NK, NK), :] + SCALE * (flow + ends)))

    p_w = whole(WEST, -f_w, y_face(beyond(SW, 8, 0), g_w), -y_face(g_w, beyond(NW, 8, N - 1)))
    p_e = whole(EAST, f_e, y_face(beyond(SE, 0, 0), g_e), -y_face(g_e, beyond(NE, 0, N - 1)))
    p_s = whole(SOUTH, -f_s, x_face(beyond(SW, 8, 0), g_s), -x_face(g_s, beyond(SE, 0, N - 1)))
    p_n = whole(NORTH, f_n, x_face(beyond(NW, 8, 0), g_n), -x_face(g_n, beyond(NE, 0, N - 1)))
    t_w, t_e, t_s, t_n = SCALE * f_w, -SCALE * f_e, SCALE * f_s, -SCALE * f_n
    d_w, d_e, d_s, d_n = (running_sum(PG * x) for x in (t_w, t_e, t_s, t_n))
    q_w = running_sum(PG * send[WEST, pl.ds(4 * NK, NK), :])
    q_e = running_sum(PG * send[EAST, pl.ds(4 * NK, NK), :])

    def across(x):
        return jnp.where(first, 0.0, west_of(x)) - jnp.where(last, 0.0, east_of(x))

    def friction(mid, other, f, i):
        m = level < jnp.minimum(mid[4], other[4])
        return jnp.where(m, f * (other[i] - mid[i]), 0.0)

    def masked(depth, x):
        return jnp.where(level < depth, x, 0.0)

    col_e, col_w = plane_column(1, 1), plane_column(1, 2)
    row_s, row_n = wide(fr[pl.ds(0, 1), :]), wide(fr[pl.ds(N - 1, 1), :])
    def add(ref, j, x):
        rows = pl.ds(j, NK, stride=N)
        ref[rows, :] = ref[rows, :] + x

    add(tn, N - 1, t_n)
    add(tn, 0, t_s)
    add(un, N - 1, friction(r_n, g_n, row_n, 1) + masked(r_n[4], across(d_n)))
    add(un, 0, friction(r_s, g_s, row_s, 1) + masked(r_s[4], across(d_s)))
    add(vn, N - 1, friction(r_n, g_n, row_n, 2) - masked(r_n[4], p_n))
    add(vn, 0, friction(r_s, g_s, row_s, 2) + masked(r_s[4], p_s))
    add(vn, N - 2, -masked(wide(dep[pl.ds(N - 2, 1), :]), d_n))
    add(vn, 1, masked(wide(dep[pl.ds(1, 1), :]), d_s))
    fix[pl.ds(0, NK, stride=4), :] = -masked(plane_column(0, 0), d_e)
    fix[pl.ds(1, NK, stride=4), :] = friction(c_e, g_e, col_e, 1) - masked(c_e[4], p_e - q_w)
    fix[pl.ds(2, NK, stride=4), :] = friction(c_w, g_w, col_w, 1) + masked(c_w[4], p_w - q_e)
    fix[pl.ds(3, NK, stride=4), :] = masked(plane_column(0, 3), d_w)
    fix[pl.ds(64, NK, stride=2), :] = friction(c_e, g_e, col_e, 2) + masked(c_e[4], across(d_e))
    fix[pl.ds(65, NK, stride=2), :] = friction(c_w, g_w, col_w, 2) + masked(c_w[4], across(d_w))
    fix[pl.ds(96, NK, stride=2), :] = t_e
    fix[pl.ds(97, NK, stride=2), :] = t_w
    fix_out[...] = fix[...].T

    for (_, ok, _), message in zip(peers, messages):
        pl.when(ok)(message.wait_send)


def finish(tn, un, vn, fix, t_out, u_out, v_out, t, u, v, out_sem):
    lane8 = lax.broadcasted_iota(jnp.int32, (8, N), 1)
    rim2 = (lane8 == 0) | (lane8 == N - 1)
    rim4 = (lane8 <= 1) | (lane8 >= N - 2)

    outs = ((t, t_out), (u, u_out), (v, v_out))

    def step(g, _):
        for k in range(CHUNK):
            start = pl.multiple_of((g * CHUNK + k) * N, N)
            for r in range(0, N, 8):
                here = pl.ds(start + r, 8)
                x = fix[pl.ds(r, 8), :]
                for new, old, rim, shift in (
                    (u, un, rim4, N - 2 - 4 * k), (v, vn, rim2, 63 - 2 * k), (t, tn, rim2, 31 - 2 * k),
                ):
                    shift = lax.rem(shift + N - g * CHUNK * (4 if rim is rim4 else 2), N)
                    new[here, :] = old[here, :] + jnp.where(rim, pltpu.roll(x, shift, 1), 0.0)
        block = pl.ds(pl.multiple_of(g * CHUNK * N, N), CHUNK * N)
        for i, (src, dst) in enumerate(outs):
            pltpu.make_async_copy(src.at[block], dst.at[block], out_sem.at[i]).start()
        return 0

    lax.fori_loop(0, NK // CHUNK, step, 0)
    for i, (src, dst) in enumerate(outs):
        pltpu.make_async_copy(src, dst, out_sem.at[i]).wait()


def solution(mesh):
    n_lon, n_lat = mesh.shape["lon"], mesh.shape["lat"]
    f32, i32 = jnp.float32, jnp.int32

    def on_device(t, u, v, kd, fr, ind, strata):
        flat = [x.reshape(FLAT, N) for x in (t, u, v, kd)]
        outs = pl.pallas_call(
            functools.partial(kernel, n_lon, n_lat),
            out_shape=[*[pltpu.VMEM((FLAT, N), f32)] * 3, pltpu.VMEM((N, N), f32)],
            in_specs=[pl.BlockSpec(memory_space=pltpu.HBM)] * 11,
            out_specs=[pl.BlockSpec(memory_space=pltpu.VMEM)] * 4,
            scratch_shapes=[
                *[pltpu.VMEM((FLAT + 8, N), f32)] * 4,
                *[pltpu.VMEM((NK * PAD + 8, N), f32)] * 3,
                pltpu.VMEM((N, N), f32),
                pltpu.VMEM((N, N), i32),
                pltpu.VMEM((N, N), i32),
                pltpu.VMEM((N + 8, N), f32),
                *[pltpu.VMEM((N, N), f32)] * 4,
                pltpu.VMEM((FLAT, N), f32),
                pltpu.VMEM((8, NK, 8, N), f32),
                pltpu.VMEM(((4 * NK + 2) * 16, N), f32),
                pltpu.VMEM((N, N), f32),
                pltpu.VMEM((4, MSG, N), f32),
                pltpu.VMEM((4, MSG, N), f32),
                pltpu.VMEM((2, 8, N), f32),
                pltpu.VMEM((4, 8, N), f32),
                pltpu.SemaphoreType.DMA((15,)),
                *[pltpu.SemaphoreType.DMA((4,))] * 4,
                pltpu.SemaphoreType.REGULAR((8,)),
            ],
            compiler_params=pltpu.CompilerParams(
                collective_id=0, has_side_effects=True, vmem_limit_bytes=60 * 1024 * 1024
            ),
            cost_estimate=pl.CostEstimate(
                flops=80 * FLAT * N, bytes_accessed=30 * FLAT * N, transcendentals=0
            ),
        )(*flat, t, u, v, kd, fr, ind, strata)
        outs = pl.pallas_call(
            finish,
            out_shape=[jax.ShapeDtypeStruct((FLAT, N), f32)] * 3,
            in_specs=[pl.BlockSpec(memory_space=pltpu.VMEM)] * 4,
            out_specs=[pl.BlockSpec(memory_space=pltpu.HBM)] * 3,
            scratch_shapes=[
                *[pltpu.VMEM((FLAT, N), f32)] * 3,
                pltpu.SemaphoreType.DMA((3,)),
            ],
            compiler_params=pltpu.CompilerParams(vmem_limit_bytes=32 * 1024 * 1024),
        )(*outs)
        return tuple(x.reshape(NK, N, N) for x in outs)

    plane, field = P("lat", "lon"), P(None, "lat", "lon")
    return jax.shard_map(
        on_device,
        mesh=mesh,
        in_specs=(field, field, field, field, plane, plane, plane),
        out_specs=(field, field, field),
        check_vma=False,
    )
```

```python
import functools
import math

import jax
import jax.numpy as jnp
from jax import lax
from jax.experimental import pallas as pl
from jax.experimental.pallas import tpu as pltpu
from jax.sharding import PartitionSpec as P

MESH = pl.DeviceIdType.MESH
NK = 16
N = 128
FLAT = NK * N
PAD = N + 8
SCALE = 1.0 / 16.0
PG = 0.25 * 0.05
WEST, EAST, SOUTH, NORTH = 0, 1, 2, 3
SW, SE, NW, NE = 0, 1, 2, 3
MSG = 5 * NK
CHUNK = 4


def east_of(x):
    return pltpu.roll(x, N - 1, 1)


def west_of(x):
    return pltpu.roll(x, 1, 1)


def face(c, d, a, b, ta, tb, ka, kb):
    return jnp.where(c < d, (a + b) * (ta + tb) - (ka + kb) * (tb - ta), 0.0)


def mirrored(x):
    lane = lax.broadcasted_iota(jnp.int32, x.shape, 1)
    return jnp.take_along_axis(x, N - 1 - lane, axis=1)


def running_sum(x):
    level = lax.broadcasted_iota(jnp.int32, x.shape, 0)
    for step in (1, 2, 4, 8):
        x = x + jnp.where(level >= step, pltpu.roll(x, step, 0), 0.0)
    return x


def kernel(
    n_lon, n_lat,
    t_hbm, u_hbm, v_hbm, k_hbm, t_rows, u_rows, v_rows, k_rows, fr_hbm, ind_hbm, str_hbm,
    tn, un, vn, fix_out,
    t, u, v, kd, p, fa, fb, fr, ind, strata, dep, dep_e, dep_n, cor, fr_e,
    ue, slabs, cols, fix, send, recv, csend, crecv,
    in_sem, send_sem, recv_sem, csend_sem, crecv_sem, ready,
):
    lon, lat = lax.axis_index("lon"), lax.axis_index("lat")
    is_top, is_bottom = lat == n_lat - 1, lat == 0
    not_bottom = jnp.logical_not(is_bottom)
    lon_e, lon_w = lax.rem(lon + 1, n_lon), lax.rem(lon + n_lon - 1, n_lon)
    lat_n, lat_s = jnp.where(is_top, lat, lat + 1), jnp.where(is_bottom, lat, lat - 1)
    east, west = (lat, lon_e), (lat, lon_w)
    north, south = (lat_n, jnp.where(is_top, n_lon - 1 - lon, lon)), (lat_s, lon)
    fold_e, fold_w = lax.rem(2 * n_lon - 2 - lon, n_lon), lax.rem(n_lon - lon, n_lon)
    own_e = is_top & (fold_e == lon)
    own_w = is_top & (fold_w == lon)
    not_own_e, not_own_w = jnp.logical_not(own_e), jnp.logical_not(own_w)
    north_e = (lat_n, jnp.where(is_top, fold_e, lon_e))
    north_w = (lat_n, jnp.where(is_top, fold_w, lon_w))
    south_e, south_w = (lat_s, lon_e), (lat_s, lon_w)

    def at(place):
        return {"lat": place[0], "lon": place[1]}

    loads = [
        pltpu.make_async_copy(src, dst, in_sem.at[i])
        for i, (src, dst) in enumerate(
            (
                (ind_hbm, ind), (str_hbm, strata),
                *(
                    (ref.at[:, pl.ds(side * (N - 8), 8), :], slabs.at[2 * f + side])
                    for f, ref in enumerate((t_rows, u_rows, v_rows, k_rows))
                    for side in (0, 1)
                ),
                (fr_hbm, fr),
                (t_hbm, t.at[pl.ds(0, FLAT)]), (u_hbm, u.at[pl.ds(0, FLAT)]),
                (k_hbm, kd.at[pl.ds(0, FLAT)]), (v_hbm, v.at[pl.ds(0, FLAT)]),
            )
        )
    ]
    for load in loads[:10]:
        load.start()
    barrier = pltpu.get_barrier_semaphore()

    def is_early(place):
        return lax.rem(place[1], n_lon // 2) < n_lon // 4

    early = is_early((lat, lon))
    always = lat >= 0
    peers = (
        (east, always, 1),
        (west, always, 0),
        (north, always, jnp.where(is_top, 2, 3)),
        (south, not_bottom, 2),
        (north_e, not_own_e, jnp.where(is_top, 4, 7)),
        (north_w, not_own_w, jnp.where(is_top, 5, 6)),
        (south_e, not_bottom, 5),
        (south_w, not_bottom, 4),
    )
    to_late = [ok & early & jnp.logical_not(is_early(place)) for place, ok, _ in peers]
    to_early = [ok & jnp.logical_not(early) & is_early(place) for place, ok, _ in peers]
    expected = jnp.int32(0)
    for (place, ok, _), ahead, behind in zip(peers, to_early, to_late):

        @pl.when(ok & jnp.logical_not(ahead))
        def _(place=place):
            pl.semaphore_signal(barrier, inc=1, device_id=at(place), device_id_type=MESH)

        expected = expected + (ok & jnp.logical_not(behind)).astype(jnp.int32)

    for load in loads[10:]:
        load.start()

    lane8 = lax.broadcasted_iota(jnp.int32, (8, N), 1)
    zero8 = jnp.zeros((8, N), jnp.float32)
    lane = lax.broadcasted_iota(jnp.int32, (NK, N), 1)
    level = lax.broadcasted_iota(jnp.int32, (NK, N), 0).astype(jnp.float32)
    first, last = lane == 0, lane == N - 1

    for load in loads[:2]:
        load.wait()
    dep[pl.ds(N, 8), :] = zero8
    dep[pl.ds(0, N), :] = (ind[...] * strata[...]).astype(jnp.float32)

    def set_columns(place, x):
        y = x.T
        cols[pl.ds(place * 16, 8), :] = y[N - 8 :]
        cols[pl.ds(place * 16 + 8, 8), :] = y[:8]

    def pack(ref, f, double):
        def step(k, _):
            block = pl.ds(pl.multiple_of(k * N, N), N)
            x = ref[block, :]
            if double:
                x = x + x
                ref[block, :] = x
            set_columns(f * NK + k, x)
            return 0

        lax.fori_loop(0, NK, step, 0, unroll=8)


    def wide(x):
        return jnp.broadcast_to(x, (NK, N))

    def column(f, entry):
        return cols[pl.ds(f * NK * 16 + 6 + entry, NK, stride=16), :]

    def plane_column(i, entry):
        return wide(cols[pl.ds((4 * NK + i) * 16 + 6 + entry, 1), :])

    def columns(entry):
        t_c, u_c, k_c, v_c = (column(f, entry) for f in range(4))
        return t_c, u_c, v_c, k_c, plane_column(0, entry)

    slab_rows = slabs.reshape(8 * NK * 8, N)

    def edge_rows(j):
        side = 0 if j < 8 else 1
        t_r, u_r, v_r, k_r = (
            slab_rows[pl.ds((2 * f + side) * NK * 8 + j % 8, NK, stride=8), :] for f in range(4)
        )
        return t_r, u_r, v_r, k_r + k_r, wide(dep[pl.ds(j, 1), :])

    def x_face(a, b):
        return face(level, jnp.minimum(a[4], b[4]), a[1], b[1], a[0], b[0], a[3], b[3])

    def y_face(a, b):
        return face(level, jnp.minimum(a[4], b[4]), a[2], b[2], a[0], b[0], a[3], b[3])

    def closed_step(mid, through, along):
        flow = jnp.where(last, 0.0, along(mid, tuple(east_of(x) for x in mid)))
        tc, _, _, kc, d = mid
        above = jnp.where(
            level + 1.0 < d,
            (kc + pltpu.roll(kc, NK - 1, 0)) * (pltpu.roll(tc, NK - 1, 0) - tc),
            0.0,
        )
        total = through + (west_of(flow) - flow) + (above - pltpu.roll(above, 1, 0))
        return jnp.where(level < d, tc + SCALE * total, 0.0)

    def marked(values):
        return (*values[:3], jnp.where(level < values[4], values[3], 0.0))

    def stage(side, values, tracer):
        for f, x in enumerate((*marked(values), tracer)):
            send[side, pl.ds(f * NK, NK), :] = x

    def stage_corners(slab, values):
        x = zero8
        for f, y in enumerate(marked(values)):
            for half in (0, 1):
                z, to = y[8 * half : 8 * half + 8], f + 16 * half
                x = jnp.where(lane8 == to, pltpu.roll(z, to, 1) if to else z, x)
                x = jnp.where(lane8 == 8 + to, pltpu.roll(z, 9 + to, 1), x)
        csend[slab] = x

    for load in loads[2:10]:
        load.wait()
    r_n, r_s = edge_rows(N - 1), edge_rows(0)
    stage(NORTH, r_n, closed_step(r_n, y_face(edge_rows(N - 2), r_n), x_face))
    stage(SOUTH, r_s, closed_step(r_s, -y_face(r_s, edge_rows(1)), x_face))
    stage_corners(0, r_n)
    stage_corners(1, r_s)

    def tracer(b, _):
        r = pl.multiple_of(b * 8, 8)
        rows = pl.ds(r, 8)
        d, de, dn = dep[rows, :], dep_e[rows, :], dep_n[rows, :]
        below = zero8
        press = zero8
        for k in range(NK):
            c = float(k)
            here, up_rows = pl.ds(r + k * N, 8), pl.ds(r + k * N + 1, 8)
            tc, kc, uc, vc = t[here, :], kd[here, :], u[here, :], v[here, :]
            next_u = east_of(uc)
            ue[here, :] = next_u
            f_e = face(c, de, uc, next_u, tc, east_of(tc), kc, east_of(kc))
            f_n = face(c, dn, vc, v[up_rows, :], tc, t[up_rows, :], kc, kd[up_rows, :])
            fa[pl.ds(r + k * PAD + 8, 8), :] = f_n
            f_s = fa[pl.ds(r + k * PAD + 7, 8), :]
            if k < NK - 1:
                t_up, k_up = t[pl.ds(r + (k + 1) * N, 8), :], kd[pl.ds(r + (k + 1) * N, 8), :]
                above = jnp.where(c + 1.0 < d, (kc + k_up) * (t_up - tc), 0.0)
            else:
                above = zero8
            total = (west_of(f_e) - f_e) + (f_s - f_n) + (above - below)
            below = above
            tc = jnp.where(c < d, tc + SCALE * total, 0.0)
            tn[here, :] = tc
            press = press + PG * tc
            p[pl.ds(r + k * PAD + 8, 8), :] = press
        return 0

    def pack_fields():
        for f, ref in enumerate((t, u, kd, v)):
            loads[11 + f].wait()
            pack(ref, f, ref is kd)

    pl.semaphore_wait(barrier, expected)
    def rim(side, slot, place):
        return pltpu.make_async_remote_copy(
            src_ref=send.at[side], dst_ref=recv.at[slot], send_sem=send_sem.at[side],
            recv_sem=recv_sem.at[slot], device_id=at(place), device_id_type=MESH,
        )

    def corner(slab, message, slot, place):
        return pltpu.make_async_remote_copy(
            src_ref=csend.at[slab], dst_ref=crecv.at[slot], send_sem=csend_sem.at[message],
            recv_sem=crecv_sem.at[slot], device_id=at(place), device_id_type=MESH,
        )

    to_north = rim(NORTH, jnp.where(is_top, NORTH, SOUTH), north)
    to_south = rim(SOUTH, NORTH, south)
    to_east, to_west = rim(EAST, WEST, east), rim(WEST, EAST, west)
    to_ne = corner(0, 0, jnp.where(is_top, NE, SW), north_e)
    to_nw = corner(0, 1, jnp.where(is_top, NW, SE), north_w)
    to_se, to_sw = corner(1, 2, NW, south_e), corner(1, 3, NE, south_w)

    messages = (to_east, to_west, to_north, to_south, to_ne, to_nw, to_se, to_sw)

    def start(numbers):
        for i in numbers:
            pl.when(peers[i][1] & jnp.logical_not(to_late[i]))(messages[i].start)

    start((2, 3, 4, 5, 6, 7))
    for (place, _, number), ahead in zip(peers, to_early):

        @pl.when(ahead)
        def _(place=place, number=number):
            pl.semaphore_signal(
                ready.at[number], inc=1, device_id=at(place), device_id_type=MESH
            )

    for k in range(NK + 1):
        p[pl.ds(k * PAD, 8), :] = zero8
        fa[pl.ds(k * PAD, 8), :] = zero8
        fb[pl.ds(k * PAD, 8), :] = zero8

    @pl.when(is_bottom)
    def _():
        recv[SOUTH] = jnp.zeros((MSG, N), jnp.float32)
        crecv[SW] = zero8
        crecv[SE] = zero8

    def set_cor(b, _):
        rows = pl.ds(pl.multiple_of(b * 8, 8), 8)
        j = lax.broadcasted_iota(jnp.int32, (8, N), 0) + (b * 8 + lat * N)
        cor[rows, :] = 0.25 * jnp.sin(
            jnp.pi * ((j.astype(jnp.float32) + 0.5) / (N * n_lat) - 0.5)
        )
        return 0

    lax.fori_loop(0, N // 8, set_cor, 0)

    loads[10].wait()
    fr[...] = fr[...] * 0.25

    def set_depth(b, _):
        r = pl.multiple_of(b * 8, 8)
        rows = pl.ds(r, 8)
        d = dep[rows, :]
        dep_e[rows, :] = jnp.where(lane8 == N - 1, 0.0, jnp.minimum(d, east_of(d)))
        dep_n[rows, :] = jnp.minimum(d, dep[pl.ds(r + 1, 8), :])
        fr_e[rows, :] = east_of(fr[rows, :])
        return 0

    lax.fori_loop(0, N // 8, set_depth, 0, unroll=True)

    set_columns(4 * NK, dep[pl.ds(0, N), :])
    set_columns(4 * NK + 1, fr[...])

    pack_fields()
    c_e, c_w = columns(1), columns(2)
    stage(EAST, c_e, closed_step(c_e, x_face(columns(0), c_e), y_face))
    stage(WEST, c_w, closed_step(c_w, -x_face(c_w, columns(3)), y_face))
    start((0, 1))
    lax.fori_loop(0, N // 8, tracer, 0, unroll=2)

    for i, message in enumerate(messages):

        @pl.when(to_late[i])
        def _(i=i, message=message):
            pl.semaphore_wait(ready.at[i], 1)
            message.start()

    def momentum(b, _):
        r = pl.multiple_of(b * 8, 8)
        rows = pl.ds(r, 8)
        d, de, dn = dep[rows, :], dep_e[rows, :], dep_n[rows, :]
        f, f_next, co = fr[rows, :], fr_e[rows, :], cor[rows, :]
        for k in range(NK):
            c = float(k)
            here, up_rows = pl.ds(r + k * N, 8), pl.ds(r + k * N + 1, 8)
            mine, south_rows = pl.ds(r + k * PAD + 8, 8), pl.ds(r + k * PAD + 7, 8)
            uc, vc, pc = u[here, :], v[here, :], p[mine, :]
            wet_e, wet_n, wet = c < de, c < dn, c < d
            u_e = jnp.where(wet_e, ue[here, :] - uc, 0.0)
            v_e = jnp.where(wet_e, east_of(vc) - vc, 0.0)
            u_n = jnp.where(wet_n, u[up_rows, :] - uc, 0.0)
            v_n = jnp.where(wet_n, v[up_rows, :] - vc, 0.0)
            fa[mine, :] = u_n
            fb[mine, :] = v_n
            gain = east_of(pc) - pc
            across_x = (f * u_e - gain) - west_of(gain + f_next * u_e)
            lap_u = u_n - fa[south_rows, :]
            lap_v = (v_e - west_of(v_e)) + (v_n - fb[south_rows, :])
            dp_y = p[pl.ds(r + k * PAD + 9, 8), :] - p[south_rows, :]
            un[here, :] = jnp.where(wet, (uc + co * vc) + across_x + f * lap_u, 0.0)
            vn[here, :] = jnp.where(wet, (vc - co * uc) - dp_y + f * lap_v, 0.0)
        return 0

    lax.fori_loop(0, N // 8, momentum, 0)

    rim(NORTH, NORTH, north).wait_recv()
    rim(EAST, EAST, east).wait_recv()
    rim(WEST, WEST, west).wait_recv()

    @pl.when(not_own_e)
    def _():
        corner(0, 0, NE, north_e).wait_recv()

    @pl.when(not_own_w)
    def _():
        corner(0, 1, NW, north_w).wait_recv()

    @pl.when(own_e)
    def _():
        crecv[NE] = csend[0]

    @pl.when(own_w)
    def _():
        crecv[NW] = csend[0]

    @pl.when(not_bottom)
    def _():
        rim(SOUTH, SOUTH, south).wait_recv()
        corner(1, 2, SE, south_e).wait_recv()
        corner(1, 3, SW, south_w).wait_recv()

    @pl.when(is_top)
    def _():
        x = mirrored(recv[NORTH])
        r = lax.broadcasted_iota(jnp.int32, (MSG, N), 0)
        recv[NORTH] = jnp.where((r >= NK) & (r < 3 * NK), -x, x)
        turned = ((lane8 & 7) == 1) | ((lane8 & 7) == 2)
        x = crecv[NW]
        x = pltpu.roll(jnp.where(turned, -x, x), 8, 1)
        crecv[NW] = x
        x = crecv[NE]
        crecv[NE] = pltpu.roll(jnp.where(turned, -x, x), N - 8, 1)

    def with_depth(t_g, u_g, v_g, k_g):
        return t_g, u_g, v_g, k_g, jnp.where(k_g > 0.0, float(NK), 0.0)

    def ghost(slot):
        return with_depth(*(recv[slot, pl.ds(f * NK, NK), :] for f in range(4)))

    def beyond(slot, entry, to):
        x = crecv[slot]

        def value(f):
            shift = to - entry - f + N
            return jnp.concatenate(
                [pltpu.roll(x, shift % N, 1), pltpu.roll(x, (shift - 16) % N, 1)], 0
            )

        return with_depth(*(value(f) for f in range(4)))

    g_w, g_e, g_s, g_n = ghost(WEST), ghost(EAST), ghost(SOUTH), ghost(NORTH)
    f_w, f_e = x_face(g_w, c_w), x_face(c_e, g_e)
    f_s, f_n = y_face(g_s, r_s), y_face(r_n, g_n)

    def whole(slot, flow, low, high):
        ends = jnp.where(first, low, jnp.where(last, high, 0.0))
        return running_sum(PG * (recv[slot, pl.ds(4 * NK, NK), :] + SCALE * (flow + ends)))

    p_w = whole(WEST, -f_w, y_face(beyond(SW, 8, 0), g_w), -y_face(g_w, beyond(NW, 8, N - 1)))
    p_e = whole(EAST, f_e, y_face(beyond(SE, 0, 0), g_e), -y_face(g_e, beyond(NE, 0, N - 1)))
    p_s = whole(SOUTH, -f_s, x_face(beyond(SW, 8, 0), g_s), -x_face(g_s, beyond(SE, 0, N - 1)))
    p_n = whole(NORTH, f_n, x_face(beyond(NW, 8, 0), g_n), -x_face(g_n, beyond(NE, 0, N - 1)))
    t_w, t_e, t_s, t_n = SCALE * f_w, -SCALE * f_e, SCALE * f_s, -SCALE * f_n
    d_w, d_e, d_s, d_n = (running_sum(PG * x) for x in (t_w, t_e, t_s, t_n))
    q_w = running_sum(PG * send[WEST, pl.ds(4 * NK, NK), :])
    q_e = running_sum(PG * send[EAST, pl.ds(4 * NK, NK), :])

    def across(x):
        return jnp.where(first, 0.0, west_of(x)) - jnp.where(last, 0.0, east_of(x))

    def friction(mid, other, f, i):
        m = level < jnp.minimum(mid[4], other[4])
        return jnp.where(m, f * (other[i] - mid[i]), 0.0)

    def masked(depth, x):
        return jnp.where(level < depth, x, 0.0)

    col_e, col_w = plane_column(1, 1), plane_column(1, 2)
    row_s, row_n = wide(fr[pl.ds(0, 1), :]), wide(fr[pl.ds(N - 1, 1), :])
    def add(ref, j, x):
        rows = pl.ds(j, NK, stride=N)
        ref[rows, :] = ref[rows, :] + x

    add(tn, N - 1, t_n)
    add(tn, 0, t_s)
    add(un, N - 1, friction(r_n, g_n, row_n, 1) + masked(r_n[4], across(d_n)))
    add(un, 0, friction(r_s, g_s, row_s, 1) + masked(r_s[4], across(d_s)))
    add(vn, N - 1, friction(r_n, g_n, row_n, 2) - masked(r_n[4], p_n))
    add(vn, 0, friction(r_s, g_s, row_s, 2) + masked(r_s[4], p_s))
    add(vn, N - 2, -masked(wide(dep[pl.ds(N - 2, 1), :]), d_n))
    add(vn, 1, masked(wide(dep[pl.ds(1, 1), :]), d_s))
    fix[pl.ds(0, NK, stride=4), :] = -masked(plane_column(0, 0), d_e)
    fix[pl.ds(1, NK, stride=4), :] = friction(c_e, g_e, col_e, 1) - masked(c_e[4], p_e - q_w)
    fix[pl.ds(2, NK, stride=4), :] = friction(c_w, g_w, col_w, 1) + masked(c_w[4], p_w - q_e)
    fix[pl.ds(3, NK, stride=4), :] = masked(plane_column(0, 3), d_w)
    fix[pl.ds(64, NK, stride=2), :] = friction(c_e, g_e, col_e, 2) + masked(c_e[4], across(d_e))
    fix[pl.ds(65, NK, stride=2), :] = friction(c_w, g_w, col_w, 2) + masked(c_w[4], across(d_w))
    fix[pl.ds(96, NK, stride=2), :] = t_e
    fix[pl.ds(97, NK, stride=2), :] = t_w
    fix_out[...] = fix[...].T

    for (_, ok, _), message in zip(peers, messages):
        pl.when(ok)(message.wait_send)


def finish(tn, un, vn, fix, t_out, u_out, v_out, t, u, v, out_sem):
    lane8 = lax.broadcasted_iota(jnp.int32, (8, N), 1)
    rim2 = (lane8 == 0) | (lane8 == N - 1)
    rim4 = (lane8 <= 1) | (lane8 >= N - 2)

    outs = ((t, t_out), (u, u_out), (v, v_out))

    def step(g, _):
        for k in range(CHUNK):
            start = pl.multiple_of((g * CHUNK + k) * N, N)
            for r in range(0, N, 8):
                here = pl.ds(start + r, 8)
                x = fix[pl.ds(r, 8), :]
                for new, old, rim, shift in (
                    (u, un, rim4, N - 2 - 4 * k), (v, vn, rim2, 63 - 2 * k), (t, tn, rim2, 31 - 2 * k),
                ):
                    shift = lax.rem(shift + N - g * CHUNK * (4 if rim is rim4 else 2), N)
                    new[here, :] = old[here, :] + jnp.where(rim, pltpu.roll(x, shift, 1), 0.0)
        block = pl.ds(pl.multiple_of(g * CHUNK * N, N), CHUNK * N)
        for i, (src, dst) in enumerate(outs):
            pltpu.make_async_copy(src.at[block], dst.at[block], out_sem.at[i]).start()
        return 0

    lax.fori_loop(0, NK // CHUNK, step, 0)
    for i, (src, dst) in enumerate(outs):
        pltpu.make_async_copy(src, dst, out_sem.at[i]).wait()


def solution(mesh):
    n_lon, n_lat = mesh.shape["lon"], mesh.shape["lat"]
    f32, i32 = jnp.float32, jnp.int32

    def on_device(t, u, v, kd, fr, ind, strata):
        flat = [x.reshape(FLAT, N) for x in (t, u, v, kd)]
        outs = pl.pallas_call(
            functools.partial(kernel, n_lon, n_lat),
            out_shape=[*[pltpu.VMEM((FLAT, N), f32)] * 3, pltpu.VMEM((N, N), f32)],
            in_specs=[pl.BlockSpec(memory_space=pltpu.HBM)] * 11,
            out_specs=[pl.BlockSpec(memory_space=pltpu.VMEM)] * 4,
            scratch_shapes=[
                *[pltpu.VMEM((FLAT + 8, N), f32)] * 4,
                *[pltpu.VMEM((NK * PAD + 8, N), f32)] * 3,
                pltpu.VMEM((N, N), f32),
                pltpu.VMEM((N, N), i32),
                pltpu.VMEM((N, N), i32),
                pltpu.VMEM((N + 8, N), f32),
                *[pltpu.VMEM((N, N), f32)] * 4,
                pltpu.VMEM((FLAT, N), f32),
                pltpu.VMEM((8, NK, 8, N), f32),
                pltpu.VMEM(((4 * NK + 2) * 16, N), f32),
                pltpu.VMEM((N, N), f32),
                pltpu.VMEM((4, MSG, N), f32),
                pltpu.VMEM((4, MSG, N), f32),
                pltpu.VMEM((2, 8, N), f32),
                pltpu.VMEM((4, 8, N), f32),
                pltpu.SemaphoreType.DMA((15,)),
                *[pltpu.SemaphoreType.DMA((4,))] * 4,
                pltpu.SemaphoreType.REGULAR((8,)),
            ],
            compiler_params=pltpu.CompilerParams(
                collective_id=0, has_side_effects=True, vmem_limit_bytes=60 * 1024 * 1024
            ),
            cost_estimate=pl.CostEstimate(
                flops=80 * FLAT * N, bytes_accessed=30 * FLAT * N, transcendentals=0
            ),
        )(*flat, t, u, v, kd, fr, ind, strata)
        outs = pl.pallas_call(
            finish,
            out_shape=[jax.ShapeDtypeStruct((FLAT, N), f32)] * 3,
            in_specs=[pl.BlockSpec(memory_space=pltpu.VMEM)] * 4,
            out_specs=[pl.BlockSpec(memory_space=pltpu.HBM)] * 3,
            scratch_shapes=[
                *[pltpu.VMEM((FLAT, N), f32)] * 3,
                pltpu.SemaphoreType.DMA((3,)),
            ],
            compiler_params=pltpu.CompilerParams(vmem_limit_bytes=32 * 1024 * 1024),
        )(*outs)
        return tuple(x.reshape(NK, N, N) for x in outs)

    plane, field = P("lat", "lon"), P(None, "lat", "lon")
    return jax.shard_map(
        on_device,
        mesh=mesh,
        in_specs=(field, field, field, field, plane, plane, plane),
        out_specs=(field, field, field),
        check_vma=False,
    )
```
